32 devices in a mesh: dp: 8 (over z, x), ns: 4 (over y, core).
Axes of the slice: x: 2, y: 2, z: 4, core: 2. Of those that a mesh axis runs over, the one named last changes fastest.
Arguments:
- fields: bfloat16 [8, 48, 360, 73], P('ns', 'dp'), may hold values from -6 to 6
- targets: bfloat16 [2, 8, 48, 360, 73], P(None, 'ns', 'dp'), may hold values from -6 to 6
- valid: int32 [8, 48, 360], P('ns', 'dp'), may hold values from 0 to 1, as said below
- var_class: int32 [73], replicated, may hold values from 0 to 3
- enc_t: float32 [256, 73], P('dp'), may hold values from -0.75 to 0.75
- enc_mom: float32 [256, 73], P('dp'), may hold values from -7.6293945e-05 to 7.6293945e-05
- dec: float32 [256, 73], P('dp'), may hold values from -0.375 to 0.375
- dec_mom: float32 [256, 73], P('dp'), may hold values from -7.6293945e-05 to 7.6293945e-05
- spec: float32 [1, 256, 96, 2, 256], P(None, 'dp', 'ns'), may hold values from -0.25 to 0.25
- spec_m: float32 [1, 256, 96, 2, 256], P(None, 'dp', 'ns'), may hold values from -9.536743e-06 to 9.536743e-06
- spec_v: float32 [1, 256, 96, 2, 256], P(None, 'dp', 'ns'), may hold values from 1.5524401e-14 to 2.4839042e-13
- up_t: float32 [1, 512, 256], P(None, ('dp', 'ns')), may hold values from -0.375 to 0.375
- up_mom: float32 [1, 512, 256], P(None, ('dp', 'ns')), may hold values from -7.6293945e-05 to 7.6293945e-05
- down: float32 [1, 512, 256], P(None, ('dp', 'ns')), may hold values from -0.25 to 0.25
- down_mom: float32 [1, 512, 256], P(None, ('dp', 'ns')), may hold values from -7.6293945e-05 to 7.6293945e-05
- gains: float32 [1, 256, 2], P(None, 'dp'), may hold values from 0.2 to 2
- gain_m: float32 [1, 256, 2], P(None, 'dp'), may hold values from -9.1552734e-05 to 9.1552734e-05
- gain_v: float32 [1, 256, 2], P(None, 'dp'), may hold values from 1.5524401e-12 to 2.4839042e-11
Outputs:
- loss_sum: float32 [], replicated
- loss_weight: float32 [], replicated
- grad_norm: float32 [], replicated
- enc_mom_new: float32 [256, 73], P('dp')
- enc_new: float32 [256, 73], P('dp')
- dec_mom_new: float32 [256, 73], P('dp')
- dec_new: float32 [256, 73], P('dp')
- up_mom_new: float32 [1, 512, 256], P(None, ('dp', 'ns'))
- up_new: float32 [1, 512, 256], P(None, ('dp', 'ns'))
- down_mom_new: float32 [1, 512, 256], P(None, ('dp', 'ns'))
- down_new: float32 [1, 512, 256], P(None, ('dp', 'ns'))
- spec_m_new: float32 [1, 256, 96, 2, 256], P(None, 'dp', 'ns')
- spec_v_new: float32 [1, 256, 96, 2, 256], P(None, 'dp', 'ns')
- spec_new: float32 [1, 256, 96, 2, 256], P(None, 'dp', 'ns')
- spec_copy: bfloat16 [1, 256, 96, 2, 256], P(None, 'dp', 'ns')
- gain_m_new: float32 [1, 256, 2], P(None, 'dp')
- gain_v_new: float32 [1, 256, 2], P(None, 'dp')
- gain_new: float32 [1, 256, 2], P(None, 'dp')
The draws below stay inside these ranges and needn't reach their ends.
Inputs may be any that keep to these rules, and one draw needn't show every extreme that they name: `valid`: 1 marks a pixel that counts in the loss.
All inputs are finite; a program needn't handle non-finite values.
Results may differ from the reference program's by a relative error of at most 0.0064.
The reference program's roundings to bfloat16 on the way count: a program that leaves them out, or rounds other values in their place, can miss the bound.
Values may be sent and summed in bfloat16 or wider, within the bound.
A program may use at most 320 MiB of HBM per device.

```python
import math
import jax
import jax.numpy as jnp
from jax import lax

E = 256
FF = 512
C = 73
LDEG = 96
MM = 96
NLON = 360
NL = 1
NS_ITERS = 5
STEP = 10
NLAT = 48
ITEMS = 8
PARAMS = 12882944


def draw_valid(key, part):
    key = jax.random.fold_in(key, 11)
    item_idx = jnp.arange(ITEMS, dtype=jnp.int32)[:, None, None]
    row_idx = jnp.arange(NLAT, dtype=jnp.int32)[None, :, None]
    threshold = 200 + 300 * row_idx // NLAT + 300 * item_idx // ITEMS
    ticket = jax.random.randint(key, (ITEMS, NLAT, NLON), 0, 1000)
    return (ticket < threshold).astype(jnp.int32)


def draw_gains(key, part):
    key = jax.random.fold_in(key, 23)
    channel = jnp.arange(E, dtype=jnp.float32)[None, :, None] / E
    low_end = 0.5
    jitter = jnp.clip(0.1 * jax.random.normal(key, (NL, E, 2), jnp.float32), -0.25, 0.25)
    return (low_end + channel) * (1.0 + jitter)


def with_ends(drawn, stream_key, smallest, high):
    longest = drawn.shape.index(max(drawn.shape))
    spots = []
    for shift in (0, 1):
        where = [jax.random.randint(jax.random.fold_in(stream_key, axis), (), 0, length) for axis, length in enumerate(drawn.shape)]
        where[longest] = (where[longest] + shift) % drawn.shape[longest]
        spots.append(tuple(where))
    return drawn.at[spots[0]].set(smallest).at[spots[1]].set(high)


def block_levels(rng, dims, shards, least, largest):
    factor_of = 1.0
    for dim, parts in shards:
        heights = jax.random.uniform(jax.random.fold_in(jax.random.fold_in(rng, 6), dim), (parts,), jnp.float32, least / len(shards), largest / len(shards))
        factor_of = factor_of * jnp.repeat(jnp.exp(heights), dims[dim] // parts).reshape((-1,) + (1,) * (len(dims) - 1 - dim))
    return factor_of


def noise(key, shape, spread, bound, cuts=(), kind=jnp.bfloat16):
    entries = jax.random.normal(key, shape, jnp.float32) * spread
    if len(cuts) > 0:
        entries = block_levels(key, shape, cuts, -0.22, 0.18) * entries
    return jnp.clip(entries, min=-bound, max=bound).astype(kind)


def setup_inputs(seed: int = 0) -> dict:
    key_of = jax.random.split(jax.random.key(seed), 19)
    return {
        "fields": noise(key_of[0], (ITEMS, NLAT, NLON, C), 1.0, 6.0, ((0, 4), (1, 8))),
        "targets": noise(key_of[1], (2, ITEMS, NLAT, NLON, C), 1.0, 6.0, ((1, 4), (2, 8))),
        "valid": draw_valid(jax.random.fold_in(key_of[18], 71), 0),
        "var_class": with_ends(jax.random.randint(key_of[3], (C,), 0, 4), jax.random.fold_in(key_of[3], 1), 0, 3).astype(jnp.int32),
        "enc_t": noise(key_of[4], (E, C), C ** -0.5, 0.75, ((0, 8),), jnp.float32),
        "enc_mom": noise(key_of[5], (E, C), (0.02 * PARAMS ** -0.5), 7.62939453125e-05, ((0, 8),), jnp.float32),
        "dec": noise(key_of[6], (E, C), E ** -0.5, 0.375, ((0, 8),), jnp.float32),
        "dec_mom": noise(key_of[7], (E, C), (0.02 * PARAMS ** -0.5), 7.62939453125e-05, ((0, 8),), jnp.float32),
        "spec": noise(key_of[8], (NL, E, LDEG, 2, E), (2 * E) ** -0.5, 0.25, ((1, 8), (2, 4)), jnp.float32),
        "spec_m": noise(key_of[9], (NL, E, LDEG, 2, E), (0.0022 * PARAMS ** -0.5), 9.5367431640625e-06, ((1, 8), (2, 4)), jnp.float32),
        "spec_v": jnp.clip(jnp.exp(math.log(2.4839041956083163e-13) - 2.7725887 * jax.random.uniform(key_of[10], (NL, E, LDEG, 2, E), jnp.float32) ** block_levels(key_of[10], (NL, E, LDEG, 2, E), ((1, 8), (2, 4)), -0.2, 0.2)), 1.5524401222551977e-14, 2.4839041956083163e-13),
        "up_t": noise(key_of[11], (NL, FF, E), E ** -0.5, 0.375, ((1, 32),), jnp.float32),
        "up_mom": noise(key_of[12], (NL, FF, E), (0.02 * PARAMS ** -0.5), 7.62939453125e-05, ((1, 32),), jnp.float32),
        "down": noise(key_of[13], (NL, FF, E), FF ** -0.5, 0.25, ((1, 32),), jnp.float32),
        "down_mom": noise(key_of[14], (NL, FF, E), (0.02 * PARAMS ** -0.5), 7.62939453125e-05, ((1, 32),), jnp.float32),
        "gains": draw_gains(jax.random.fold_in(key_of[18], 71), 0),
        "gain_m": noise(key_of[16], (NL, E, 2), (0.022 * PARAMS ** -0.5), 9.1552734375e-05, ((1, 8),), jnp.float32),
        "gain_v": jnp.clip(jnp.exp(math.log(2.4839042281343815e-11) - 2.7725887 * jax.random.uniform(key_of[17], (NL, E, 2), jnp.float32) ** block_levels(key_of[17], (NL, E, 2), ((1, 8),), -0.2, 0.2)), 1.5524401425839884e-12, 2.4839042281343815e-11),
    }


EXACT = lax.Precision.HIGHEST
EPSILON = 1e-06
CLIP_NORM = 0.02
RATE_SPECTRAL = 0.05
RATE_GAIN = 0.1
RATE_MUON = 0.5
BETA_FIRST = 0.9
BETA_SECOND = 0.999
MOMENTUM = 0.95
DECAY = 0.01
NS_FIRST = 3.4445
NS_SECOND = -4.775
NS_THIRD = 2.0315

@jax.custom_vjp
def low(v):
    return lax.optimization_barrier(v.astype(jnp.bfloat16)).astype(jnp.float32)

@jax.custom_vjp
def low_back(v):
    return v

def low_keep(v):
    return (low(v), None)

def low_pass(kept, grad):
    return (grad,)

def back_keep(v):
    return (v, None)

def back_low(kept, grad):
    return (low(grad),)
low.defvjp(low_keep, low_pass)
low_back.defvjp(back_keep, back_low)

def legendre(orders, colatitude):
    cosine = jnp.cos(colatitude)[None, :]
    log_sine = jnp.log(jnp.sin(colatitude))[None, :]
    ladder = jnp.arange(1, MM, dtype=jnp.float32)
    log_ratio = jnp.log((2.0 * ladder - 1.0) / (2.0 * ladder))
    included = (ladder[None, :] <= orders[:, None]).astype(jnp.float32)
    log_diag = 0.5 * jnp.log((2.0 * orders + 1.0) / (4.0 * math.pi)) + 0.5 * lax.optimization_barrier(jnp.sum(included * log_ratio[None, :], axis=1))
    diagonal = jnp.exp(log_diag[:, None] + orders[:, None] * log_sine)
    order_col = orders[:, None]

    def advance(previous, degree):
        second_back, first_back = previous
        denominator = jnp.maximum(degree * degree - order_col * order_col, 1.0)
        factor_a = jnp.sqrt(jnp.maximum(4.0 * degree * degree - 1.0, 1.0) / denominator)
        factor_b = jnp.sqrt(jnp.maximum((degree - 1.0) ** 2 - order_col * order_col, 0.0) / jnp.maximum(4.0 * (degree - 1.0) ** 2 - 1.0, 1.0))
        general = factor_a * (cosine * first_back - factor_b * second_back)
        result = jnp.where(degree < order_col, 0.0, jnp.where(degree == order_col, diagonal, general))
        return ((first_back, result), result)
    zeros_init = jnp.zeros_like(diagonal)
    return lax.scan(advance, (zeros_init, zeros_init), jnp.arange(LDEG, dtype=jnp.float32))[1]

def dft_tables(lon_count):
    longitude = jnp.arange(lon_count, dtype=jnp.int32)
    mode_ids = jnp.arange(MM, dtype=jnp.int32)
    turn_ids = longitude[:, None] * mode_ids[None, :] % lon_count
    phases = 2.0 * math.pi / lon_count * turn_ids.astype(jnp.float32)
    paired = jnp.stack([jnp.cos(phases), -jnp.sin(phases)], axis=2)
    forward = paired.reshape(lon_count, 2 * MM) * (2.0 * math.pi / lon_count)
    weight = jnp.where(mode_ids == 0, 1.0, 2.0).astype(jnp.float32)
    inverse = (paired * weight[None, :, None]).reshape(lon_count, 2 * MM).T / (2.0 * math.pi)
    return (forward, inverse)

def normalize(values, gain_vec):
    return values * lax.rsqrt(lax.optimization_barrier(jnp.mean(values * values, axis=-1, keepdims=True)) + EPSILON) * gain_vec

def mixing(spectrum, weights):
    dims_in = spectrum.shape
    paired = spectrum.reshape(dims_in[:-2] + (dims_in[-2] // 2, 2, dims_in[-1]))
    real_in, imag_in = (paired[..., 0, :], paired[..., 1, :])
    real_w, imag_w = (weights[:, :, 0, :], weights[:, :, 1, :])

    def contract(left_op, right_op):
        return jnp.einsum('blmi,ilo->blmo', left_op, right_op, precision=EXACT)
    real_out = contract(real_in, real_w) - contract(imag_in, imag_w)
    imag_out = contract(real_in, imag_w) + contract(imag_in, real_w)
    return jnp.stack([real_out, imag_out], axis=-2).reshape(dims_in)

def sfno_block(residual, spec_w, up_w, down_w, gain_vec, transform_tables):
    dft_fwd, dft_inv, quad_tab, plain_tab = transform_tables
    normed_a = low(normalize(residual, gain_vec[:, 0]))
    fourier = low_back(low(jnp.einsum('bjke,kq->bjqe', normed_a, dft_fwd, precision=EXACT)))
    spectrum = low_back(low(jnp.einsum('lqj,bjqe->blqe', quad_tab, fourier, precision=EXACT)))
    mixed_modes = low_back(low(mixing(spectrum, spec_w)))
    spatial = low_back(low(jnp.einsum('lqj,blqe->bjqe', plain_tab, mixed_modes, precision=EXACT)))
    middle = residual + low_back(jnp.einsum('bjqe,qk->bjke', spatial, dft_inv, precision=EXACT))
    normed_b = low(normalize(middle, gain_vec[:, 1]))
    pre_act = low_back(jnp.einsum('bjke,fe->bjkf', normed_b, up_w, precision=EXACT))
    hidden = low(jax.nn.gelu(pre_act))
    return middle + low_back(jnp.einsum('bjkf,fe->bjke', hidden, down_w, precision=EXACT))

def network(incoming_state, weights, transform_tables):
    enc_w, dec_w, spec_w, up_w, down_w, gain_w = weights
    hidden = low_back(jnp.einsum('bjkc,ec->bjke', low(incoming_state), enc_w, precision=EXACT))
    for layer_at in range(NL):
        hidden = sfno_block(hidden, spec_w[layer_at], up_w[layer_at], down_w[layer_at], gain_w[layer_at], transform_tables)
    return low_back(jnp.einsum('bjke,ec->bjkc', low(hidden), dec_w, precision=EXACT))

def orthogonal(moment):
    row_count, col_count = moment.shape[-2:]
    square = lax.optimization_barrier(jnp.sum(moment * moment, axis=(-2, -1), keepdims=True))
    matrix = moment / (jnp.sqrt(square) + 1e-07)
    for sweep_no in range(NS_ITERS):
        gram_mat = jnp.einsum('...rk,...rj->...kj', matrix, matrix, precision=EXACT)
        poly = NS_SECOND * gram_mat + NS_THIRD * jnp.einsum('...kj,...ji->...ki', gram_mat, gram_mat, precision=EXACT)
        matrix = NS_FIRST * matrix + jnp.einsum('...rk,...kj->...rj', matrix, poly, precision=EXACT)
    return matrix * math.sqrt(max(1.0, row_count / col_count))

def muon_step(weight, moment, gradient):
    moment_new = MOMENTUM * moment + gradient
    return (moment_new, weight * (1.0 - RATE_MUON * DECAY) - RATE_MUON * orthogonal(moment_new))

def adam_step(weight, moment_a, moment_b, gradient, step_rate):
    moment_a = BETA_FIRST * moment_a + (1.0 - BETA_FIRST) * gradient
    moment_b = BETA_SECOND * moment_b + (1.0 - BETA_SECOND) * gradient * gradient
    corrected_a = moment_a / (1.0 - BETA_FIRST ** STEP)
    corrected_b = moment_b / (1.0 - BETA_SECOND ** STEP)
    return (moment_a, moment_b, weight - step_rate * (corrected_a / (jnp.sqrt(corrected_b) + 1e-08) + DECAY * weight))

def reference(fields, targets, valid, var_class, enc_t, enc_mom, dec, dec_mom, spec, spec_m, spec_v, up_t, up_mom, down, down_mom, gains, gain_m, gain_v):
    colatitude = math.pi * (jnp.arange(NLAT, dtype=jnp.float32) + 0.5) / NLAT
    legendre_tab = jnp.repeat(legendre(jnp.arange(MM, dtype=jnp.float32), colatitude), 2, axis=1)
    quadrature = 2.0 * math.pi * math.pi / NLAT * jnp.sin(colatitude)
    dft_fwd, dft_inv = dft_tables(NLON)
    transform_tables = (low(dft_fwd), low(dft_inv), low(legendre_tab * quadrature[None, None, :]), low(legendre_tab))
    var_weight = 1.0 + 0.5 * var_class.astype(jnp.float32)
    pixel_map = valid.astype(jnp.float32) * jnp.sin(colatitude)[None, :, None]
    loss_weight = jnp.sum(pixel_map) * jnp.sum(var_weight)
    masters = (enc_t, dec, spec, up_t, down, gains)

    def item_step(totals, inputs):
        input_field, target, item_map = inputs
        weight_map = item_map[None, :, :, None] * var_weight

        def loss_of(params_in):
            rounded = tuple((low(master) for master in params_in))
            state_now = input_field[None].astype(jnp.float32)
            loss_total = jnp.zeros((), jnp.float32)
            for unrolled_predict in range(2):
                state_now = network(state_now, rounded, transform_tables)
                error_amount = state_now - target[unrolled_predict][None].astype(jnp.float32)
                loss_total = loss_total + jnp.sum(weight_map * error_amount * error_amount)
            return loss_total
        loss_item, pullback = jax.vjp(loss_of, masters)
        gradients = pullback(1.0 / loss_weight)[0]
        return ((totals[0] + loss_item, jax.tree.map(jnp.add, totals[1], gradients)), None)
    initial = (jnp.zeros((), jnp.float32), jax.tree.map(jnp.zeros_like, masters))
    (loss_sum, gradients), _ = lax.scan(item_step, initial, (fields, jnp.moveaxis(targets, 0, 1), pixel_map))
    squares = sum((jnp.sum(grad_part * grad_part) for grad_part in gradients))
    grad_norm = jnp.sqrt(squares)
    clip_scale = CLIP_NORM / jnp.maximum(grad_norm, CLIP_NORM)
    g_enc, g_dec, g_spec, g_up, g_down, g_gain = [clip_scale * grad_part for grad_part in gradients]
    enc_mom_new, enc_new = muon_step(enc_t, enc_mom, g_enc)
    dec_mom_new, dec_new = muon_step(dec, dec_mom, g_dec)
    up_mom_new, up_new = muon_step(up_t, up_mom, g_up)
    down_mom_new, down_new = muon_step(down, down_mom, g_down)
    spec_m_new, spec_v_new, spec_new = adam_step(spec, spec_m, spec_v, g_spec, RATE_SPECTRAL)
    gain_m_new, gain_v_new, gain_new = adam_step(gains, gain_m, gain_v, g_gain, RATE_GAIN)
    return (loss_sum, loss_weight, grad_norm, enc_mom_new, enc_new, dec_mom_new, dec_new, up_mom_new, up_new, down_mom_new, down_new, spec_m_new, spec_v_new, spec_new, spec_new.astype(jnp.bfloat16), gain_m_new, gain_v_new, gain_new)
```

```python
import math

import jax
import jax.numpy as jnp
import ml_dtypes
import numpy as np
from jax import lax
from jax.experimental import pallas as pl
from jax.experimental.pallas import tpu as pltpu
from jax.sharding import PartitionSpec as P

E = 256
FF = 512
C = 73
LDEG = 96
MM = 96
NL = 1
NS_ITERS = 5
STEP = 10

EXACT = lax.Precision.HIGHEST
EPSILON = 1e-06
CLIP_NORM = 0.02
RATE_SPECTRAL = 0.05
RATE_GAIN = 0.1
RATE_MUON = 0.5
BETA_FIRST = 0.9
BETA_SECOND = 0.999
MOMENTUM = 0.95
DECAY = 0.01
NS_FIRST = 3.4445
NS_SECOND = -4.775
NS_THIRD = 2.0315
LOW = jnp.bfloat16
FULL = jnp.float32
MESH = pl.DeviceIdType.MESH
BOTH = ("dp", "ns")


class Layout:
    def __init__(self, dp, ns, items, rows):
        self.dp, self.ns, self.items, self.rows = dp, ns, items, rows
        self.x = dp // ns
        self.mper, self.lper, self.lns = MM // dp, LDEG // dp, LDEG // ns
        self.kb = 8 // items
        self.nkb = -(-self.mper // self.kb)
        self.blocks = [[i for i in range(self.lper) if i >= k * self.kb] for k in range(self.nkb)]
        self.starts = np.cumsum([0] + [len(b) for b in self.blocks]).tolist()
        self.nblk = self.starts[-1]
        self.cols = items * rows * 8 // items * (self.kb * 2) // 8
        self.cols = items * rows * self.kb * 2
        self.slots = -(-self.lns // dp)
        self.even = self.lns % dp == 0
        self.e_dev = E // dp

    def fore(self, n):
        half = self.ns // 2
        return (n % 2) * half + n // 2

    def back(self, z):
        half = self.ns // 2
        return (z % half) * 2 + z // half

    def here(self):
        d, n = lax.axis_index("dp"), lax.axis_index("ns")
        return d // self.x, d % self.x, n


def group_of(lay, kind):
    z, x, n = lay.here()
    if kind == "plane":
        return lay.dp, lay.fore(n) * lay.x + x, lambda p: (z * lay.x + p % lay.x, lay.back(p // lay.x))
    if kind == "line":
        return lay.ns, z, lambda q: (q * lay.x + x, n)
    return (
        lay.dp * lay.ns,
        (z * lay.x + x) * lay.ns + n,
        lambda q: (q // lay.ns, q % lay.ns),
    )


def exchange(lay, arrays, kinds, group, tag):
    count = {"plane": lay.dp, "line": lay.ns, "all": lay.dp * lay.ns}[group]

    def kernel(*refs):
        total = len(arrays)
        ins, outs = refs[:total], refs[total : 2 * total]
        send, recv, own = refs[2 * total :]
        size, me, device = group_of(lay, group)
        barrier = pltpu.get_barrier_semaphore()

        @pl.loop(1, size)
        def _(step):
            pl.semaphore_signal(
                barrier, inc=1, device_id=device(lax.rem(me + step, size)), device_id_type=MESH
            )

        pl.semaphore_wait(barrier, size - 1)

        @pl.loop(1, size)
        def _(step):
            peer = lax.rem(me + step, size)
            for at in range(total):
                pltpu.make_async_remote_copy(
                    src_ref=ins[at].at[peer] if kinds[at] == "each" else ins[at],
                    dst_ref=outs[at].at[me],
                    send_sem=send.at[at],
                    recv_sem=recv.at[at],
                    device_id=device(peer),
                    device_id_type=MESH,
                ).start()

        for at in range(total):
            mine = ins[at].at[me] if kinds[at] == "each" else ins[at]
            copy = pltpu.make_async_copy(mine, outs[at].at[me], own)
            copy.start()
            copy.wait()
        for at in range(total):
            some = outs[at].at[pl.ds(0, size - 1)]
            pltpu.make_async_remote_copy(
                src_ref=some,
                dst_ref=some,
                send_sem=send.at[at],
                recv_sem=recv.at[at],
                device_id=device(lax.rem(me + 1, size)),
                device_id_type=MESH,
            ).wait()

    shapes = [
        jax.ShapeDtypeStruct(a.shape if k == "each" else (count,) + a.shape, a.dtype)
        for a, k in zip(arrays, kinds)
    ]
    spot = pl.BlockSpec(memory_space=pl.ANY)
    return pl.pallas_call(
        kernel,
        out_shape=shapes,
        in_specs=[spot] * len(arrays),
        out_specs=[spot] * len(arrays),
        scratch_shapes=[
            pltpu.SemaphoreType.DMA((len(arrays),)),
            pltpu.SemaphoreType.DMA((len(arrays),)),
            pltpu.SemaphoreType.DMA,
        ],
        compiler_params=pltpu.CompilerParams(collective_id=tag, has_side_effects=True),
        name=f"exchange_{group}_{tag}",
    )(*arrays)


def legendre(lat_count):
    colatitude = math.pi * (np.arange(lat_count) + 0.5) / lat_count
    cosine, log_sine = np.cos(colatitude)[None, :], np.log(np.sin(colatitude))[None, :]
    orders = np.arange(MM, dtype=np.float64)
    ladder = np.arange(1, MM, dtype=np.float64)
    sums = np.concatenate([[0.0], np.cumsum(np.log((2 * ladder - 1) / (2 * ladder)))])
    diagonal = np.exp(
        (0.5 * np.log((2 * orders + 1) / (4 * math.pi)) + 0.5 * sums)[:, None]
        + orders[:, None] * log_sine
    )
    table = np.zeros((LDEG, MM, lat_count))
    for degree in range(LDEG):
        for order in range(min(degree, MM - 1) + 1):
            if degree == order:
                table[degree, order] = diagonal[order]
                continue
            a = math.sqrt((4.0 * degree**2 - 1) / (degree**2 - order**2))
            value = cosine[0] * table[degree - 1, order]
            if degree >= 2:
                b = math.sqrt(
                    max((degree - 1.0) ** 2 - order**2, 0) / (4 * (degree - 1.0) ** 2 - 1)
                )
                value = value - b * table[degree - 2, order]
            table[degree, order] = a * value
    return table.astype(np.float32)


def low_table(values):
    return values.astype(np.float32).astype(ml_dtypes.bfloat16)


def dft_tables(lay, lon_count):
    turns = np.arange(lon_count)[:, None] * np.arange(MM)[None, :] % lon_count
    phases = 2 * math.pi / lon_count * turns
    paired = np.stack([np.cos(phases), -np.sin(phases)], axis=2)
    weight = np.where(np.arange(MM) == 0, 1.0, 2.0)
    forward = paired * (2 * math.pi / lon_count)
    inverse = paired * weight[None, :, None] / (2 * math.pi)

    def order(table):
        table = table.reshape(lon_count, lay.mper, lay.dp, 2).transpose(0, 2, 1, 3)
        pad = lay.nkb * lay.kb - lay.mper
        table = np.pad(table, ((0, 0), (0, 0), (0, pad), (0, 0)))
        return low_table(table.reshape(lon_count, -1))

    return order(forward), order(inverse)


def legendre_tables(lay, member, lat_count):
    plain = legendre(lat_count)
    colatitude = math.pi * (np.arange(lat_count) + 0.5) / lat_count
    quadrature = 2 * math.pi * math.pi / lat_count * np.sin(colatitude)
    pad = lay.nkb * lay.kb - lay.mper

    def own(table):
        table = table.reshape(lay.lper, lay.dp, lay.mper, lay.dp, lat_count)
        table = np.pad(table.transpose(3, 1, 0, 2, 4), ((0, 0), (0, 0), (0, 0), (0, pad), (0, 0)))
        return lax.dynamic_index_in_dim(jnp.asarray(low_table(table)), member, keepdims=False)

    rows_of = np.arange(lat_count).reshape(lay.dp, 1, lay.rows, 1, 1)
    rows_of = np.broadcast_to(rows_of, (lay.dp, lay.items, lay.rows, lay.kb, 2)).reshape(-1)
    spread = (np.arange(lat_count)[:, None] == rows_of[None, :]).astype(ml_dtypes.bfloat16)
    col = np.arange(lay.dp * lay.cols)
    col_part, col_k = col % 2, col // 2 % lay.kb
    col_item = col // (2 * lay.kb * lay.rows) % lay.items
    row = np.arange(2 * lay.kb * lay.items)
    row_item, row_k = row % lay.items, row // lay.items % lay.kb
    row_part = row // (lay.items * lay.kb)
    same = (
        (row_part[:, None] == col_part)
        & (row_k[:, None] == col_k)
        & (row_item[:, None] == col_item)
    )

    def build(table):
        mine = own(table)
        out = []
        for k in range(lay.nkb):
            part = mine[:, k * lay.kb :, k * lay.kb : (k + 1) * lay.kb]
            wide = jnp.einsum("pikj,jc->pikc", part, spread, preferred_element_type=FULL).astype(LOW)
            shape = wide.shape[:2] + (2, lay.kb, lay.items, wide.shape[-1])
            wide = jnp.broadcast_to(wide[:, :, None, :, None, :], shape)
            wide = wide.reshape(wide.shape[:2] + (len(row), len(col)))
            wide = jnp.where(same, wide, jnp.zeros((), LOW))
            out.append(wide.reshape(-1, len(col)))
        return out

    return build(plain * quadrature.astype(np.float32)[None, None, :]), build(plain)


def normalize(values, gain_vec):
    return (
        values * lax.rsqrt(jnp.mean(values * values, axis=-1, keepdims=True) + EPSILON) * gain_vec
    )


def to_modes(lay, values, tables, tag):
    items, rows = values.shape[:2]
    laid = values.reshape(items, rows, lay.dp, lay.nkb, 2 * lay.kb, E)
    laid = laid.transpose(2, 3, 0, 1, 4, 5).reshape(lay.dp, lay.nkb * lay.cols, E)
    (got,) = exchange(lay, [laid], ["each"], "plane", tag)
    got = got.reshape(lay.dp, lay.nkb, lay.cols, E)
    parts = []
    for k in range(lay.nkb):
        block = got[:, k].reshape(lay.dp * lay.cols, E)
        out = jnp.dot(tables[k], block, preferred_element_type=FULL).astype(LOW)
        parts.append(out.reshape(lay.dp, -1, E))
    (back,) = exchange(lay, [jnp.concatenate(parts, axis=1)], ["each"], "plane", tag + 1)
    return back


def to_rows(lay, modes, tables, tag):
    (got,) = exchange(lay, [modes], ["each"], "plane", tag + 1)
    size = 2 * lay.kb * lay.items
    parts = []
    for k in range(lay.nkb):
        block = got[:, lay.starts[k] * size : lay.starts[k + 1] * size].reshape(-1, E)
        out = lax.dot_general(
            tables[k], block, (((0,), (0,)), ((), ())), preferred_element_type=FULL
        ).astype(LOW)
        parts.append(out.reshape(lay.dp, lay.cols, E))
    (back,) = exchange(lay, [jnp.concatenate(parts, axis=1)], ["each"], "plane", tag)
    back = back.reshape(lay.dp, lay.nkb, lay.items, lay.rows, 2 * lay.kb, E)
    return back.transpose(2, 3, 0, 1, 4, 5).reshape(lay.items, lay.rows, -1, E)


def by_degree(lay, modes):
    size = 2 * lay.kb * lay.items
    blocks = modes.reshape(lay.dp, lay.nblk, size, E)
    out = []
    for g in range(lay.nkb):
        first, last = g * lay.kb, min((g + 1) * lay.kb, lay.lper)
        if g == lay.nkb - 1:
            last = lay.lper
        pieces = []
        for k in range(g + 1):
            at = lay.starts[k] + first - k * lay.kb
            pieces.append(blocks[:, at : at + last - first])
        stacked = jnp.stack(pieces, axis=1)
        out.append(stacked.transpose(2, 1, 0, 3, 4).reshape(last - first, -1, E))
    return out


def from_degree(lay, groups):
    size = 2 * lay.kb * lay.items
    pieces = [[] for _ in range(lay.nkb)]
    for g, values in enumerate(groups):
        count = values.shape[0]
        values = values.reshape(count, g + 1, lay.dp, size, E)
        for k in range(g + 1):
            pieces[k].append(values[:, k].transpose(1, 0, 2, 3))
    flat = [jnp.concatenate(p, axis=1) for p in pieces]
    return jnp.concatenate(flat, axis=1).reshape(lay.dp, -1, E)


def halves(values):
    split = values.reshape(values.shape[0], -1, 2, 8, E)
    return split[:, :, 0], split[:, :, 1]


def joined(real, imag):
    return jnp.stack([real, imag], axis=2).reshape(real.shape[0], -1, E)


def degrees_of(lay, groups):
    edges = np.cumsum([0] + [g.shape[0] for g in groups]).tolist()
    return list(zip(edges[:-1], edges[1:]))


def mixing(lay, modes, spec_w):
    groups = by_degree(lay, modes)
    out = []
    for (a, b), values in zip(degrees_of(lay, groups), groups):
        by_real = jnp.einsum("lre,leo->lro", values, spec_w[a:b, 0], preferred_element_type=FULL)
        by_imag = jnp.einsum("lre,leo->lro", values, spec_w[a:b, 1], preferred_element_type=FULL)
        (rr, ir), (ri, ii) = halves(by_real), halves(by_imag)
        out.append(joined(rr - ii, ri + ir).astype(LOW))
    return from_degree(lay, out)


def mixing_back(lay, modes, d_modes, spec_w):
    groups, d_groups = by_degree(lay, modes), by_degree(lay, d_modes)
    out, d_real, d_imag = [], [], []
    for (a, b), values, grads in zip(degrees_of(lay, groups), groups, d_groups):
        by_real = jnp.einsum("lro,leo->lre", grads, spec_w[a:b, 0], preferred_element_type=FULL)
        by_imag = jnp.einsum("lro,leo->lre", grads, spec_w[a:b, 1], preferred_element_type=FULL)
        (rr, ir), (ri, ii) = halves(by_real), halves(by_imag)
        out.append(joined(rr + ii, ir - ri).astype(LOW))
        g_real, g_imag = halves(grads)
        turned = joined(g_imag, -g_real)
        d_real.append(jnp.einsum("lre,lro->leo", values, grads, preferred_element_type=FULL))
        d_imag.append(jnp.einsum("lre,lro->leo", values, turned, preferred_element_type=FULL))
    d_spec = jnp.stack([jnp.concatenate(d_real), jnp.concatenate(d_imag)], axis=1)
    return from_degree(lay, out), d_spec


def fetch_spec(lay, spec):
    z, x, n = lay.here()
    member = lay.fore(n) * lay.x + x
    low = spec.astype(LOW).transpose(1, 2, 0, 3)
    tail = (2, lay.e_dev, E)
    if lay.even:
        laid = low.reshape((lay.slots, lay.dp) + tail).swapaxes(0, 1)
    else:
        at = (jnp.arange(lay.dp) - lay.lns * n) % lay.dp
        at = at[:, None] + lay.dp * jnp.arange(lay.slots)
        laid = jnp.take(low, jnp.minimum(at, lay.lns - 1), axis=0)
    (got,) = exchange(
        lay, [laid.reshape(lay.dp, -1, E)], ["each"], "plane", 2
    )
    got = got.reshape((lay.ns, lay.x, lay.slots) + tail)
    got = got[np.array([lay.fore(k) for k in range(lay.ns)])]
    got = got.transpose(0, 2, 3, 1, 4, 5).reshape(lay.ns, lay.slots, 2, lay.x * lay.e_dev, E)
    if lay.even:
        mine = got.reshape((lay.lper,) + got.shape[2:])
    else:
        degree = lay.dp * jnp.arange(lay.lper) + member
        mine = got[degree // lay.lns, degree % lay.lns // lay.dp]
    (every,) = exchange(lay, [mine.reshape(-1, E)], ["same"], "line", 3)
    every = every.reshape((lay.ns, lay.lper, 2, lay.x * lay.e_dev, E))
    return every.transpose(1, 2, 0, 3, 4).reshape(lay.lper, 2, E, E)


def return_spec(lay, d_spec):
    z, x, n = lay.here()
    member = lay.fore(n) * lay.x + x
    tail = (2, lay.x * lay.e_dev, E)
    laid = d_spec.reshape(lay.lper, 2, lay.ns, lay.x * lay.e_dev, E).transpose(2, 0, 1, 3, 4)
    (got,) = exchange(lay, [laid.astype(LOW).reshape(lay.ns, -1, E)], ["each"], "line", 4)
    total = jnp.sum(got.astype(FULL), axis=0).reshape((lay.lper,) + tail)
    if lay.even:
        slots = total.reshape((lay.ns, lay.slots) + tail)
    else:
        first = (member - lay.lns * jnp.arange(lay.ns)) % lay.dp + lay.lns * jnp.arange(lay.ns)
        at = (first[:, None] + lay.dp * jnp.arange(lay.slots) - member) // lay.dp
        slots = total[jnp.clip(at, 0, lay.lper - 1)]
    slots = slots[np.array([lay.back(k) for k in range(lay.ns)])]
    slots = slots.reshape(lay.ns, lay.slots, 2, lay.x, lay.e_dev, E).transpose(0, 3, 1, 2, 4, 5)
    (back,) = exchange(lay, [slots.reshape(lay.dp, -1, E)], ["each"], "plane", 5)
    back = back.reshape(lay.dp, lay.slots, 2, lay.e_dev, E)
    if lay.even:
        mine = back.swapaxes(0, 1).reshape(lay.lns, 2, lay.e_dev, E)
    else:
        degree = lay.lns * n + jnp.arange(lay.lns)
        source = degree % lay.dp
        slot = (jnp.arange(lay.lns) - (source - lay.lns * n) % lay.dp) // lay.dp
        mine = back[source, slot]
    return mine.transpose(2, 0, 1, 3)


def pad_rows(values, rows):
    return jnp.pad(values, ((0, 0),) * (values.ndim - 2) + ((0, rows - values.shape[-2]), (0, 0)))


def wide(values):
    return jnp.pad(values, ((0, 0),) * (values.ndim - 1) + ((0, 128 - values.shape[-1]),))


def forward_block(lay, residual, weights, tables, tag):
    spec_w, up_w, down_w, gain_low = weights
    gain_vec = gain_low.astype(FULL)
    dft_fwd, dft_inv, quad_tab, plain_tab = tables
    normed_a = normalize(residual, gain_vec[:, 0]).astype(LOW)
    fourier = jnp.einsum("brke,kq->brqe", normed_a, dft_fwd, preferred_element_type=FULL)
    spectrum = to_modes(lay, fourier.astype(LOW), quad_tab, tag)
    mixed = mixing(lay, spectrum, spec_w)
    restored = to_rows(lay, mixed, plain_tab, tag)
    middle = residual + jnp.einsum(
        "brqe,kq->brke", restored, dft_inv, preferred_element_type=FULL
    )
    normed_b = normalize(middle, gain_vec[:, 1]).astype(LOW)
    pre_act = jnp.einsum("brke,fe->brkf", normed_b, up_w, preferred_element_type=FULL)
    hidden = jax.nn.gelu(pre_act).astype(LOW)
    output = middle + jnp.einsum("brkf,fe->brke", hidden, down_w, preferred_element_type=FULL)
    return (output, (residual, spectrum, middle, normed_b, pre_act, hidden))


def backward_block(lay, output_gradient, saved, weights, tables, tag):
    residual, spectrum, middle, normed_b, pre_act, hidden = saved
    spec_w, up_w, down_w, gain_low = weights
    gain_vec = gain_low.astype(FULL)
    dft_fwd, dft_inv, quad_tab, plain_tab = tables
    g_out = output_gradient.astype(LOW)
    d_down = jnp.einsum("brkf,brke->fe", hidden, g_out, preferred_element_type=FULL)
    d_hidden = jnp.einsum("brke,fe->brkf", g_out, down_w, preferred_element_type=FULL)
    d_pre = jax.vjp(jax.nn.gelu, pre_act)[1](d_hidden)[0].astype(LOW)
    d_up = jnp.einsum("brkf,brke->fe", d_pre, normed_b, preferred_element_type=FULL)
    d_normed_b = jnp.einsum("brkf,fe->brke", d_pre, up_w, preferred_element_type=FULL)
    d_mid_part, d_gain_b = jax.vjp(normalize, middle, gain_vec[:, 1])[1](d_normed_b)
    d_middle = output_gradient + d_mid_part
    d_restored = jnp.einsum(
        "brke,kq->brqe", d_middle.astype(LOW), dft_inv, preferred_element_type=FULL
    ).astype(LOW)
    d_mixed = to_modes(lay, d_restored, plain_tab, tag)
    d_spectrum, d_spec = mixing_back(lay, spectrum, d_mixed, spec_w)
    d_fourier = to_rows(lay, d_spectrum, quad_tab, tag)
    d_normed_a = jnp.einsum("brqe,kq->brke", d_fourier, dft_fwd, preferred_element_type=FULL)
    d_res_part, d_gain_a = jax.vjp(normalize, residual, gain_vec[:, 0])[1](d_normed_a)
    d_gain = jnp.stack([d_gain_a, d_gain_b], axis=1)
    return (d_middle + d_res_part, (d_spec, d_up, d_down, d_gain))


def newton(moment):
    square = jnp.sum(moment * moment, axis=(-2, -1), keepdims=True)
    matrix = moment / (jnp.sqrt(square) + 1e-07)
    for sweep_no in range(NS_ITERS):
        gram_mat = jnp.einsum("...rk,...rj->...kj", matrix, matrix, precision=EXACT)
        poly = NS_SECOND * gram_mat + NS_THIRD * jnp.einsum(
            "...kj,...ji->...ki", gram_mat, gram_mat, precision=EXACT
        )
        matrix = NS_FIRST * matrix + jnp.einsum(
            "...rk,...kj->...rj", matrix, poly, precision=EXACT
        )
    return matrix


def adam_step(weight, moment_a, moment_b, gradient, step_rate):
    moment_a = BETA_FIRST * moment_a + (1.0 - BETA_FIRST) * gradient
    moment_b = BETA_SECOND * moment_b + (1.0 - BETA_SECOND) * gradient * gradient
    corrected_a = moment_a / (1.0 - BETA_FIRST**STEP)
    corrected_b = moment_b / (1.0 - BETA_SECOND**STEP)
    return (
        moment_a,
        moment_b,
        weight - step_rate * (corrected_a / (jnp.sqrt(corrected_b) + 1e-08) + DECAY * weight),
    )


def local(
    fields,
    targets,
    valid,
    var_class,
    enc_t,
    enc_mom,
    dec,
    dec_mom,
    spec,
    spec_m,
    spec_v,
    up_t,
    up_mom,
    down,
    down_mom,
    gains,
    gain_m,
    gain_v,
):
    dp_count, ns_count = lax.axis_size("dp"), lax.axis_size("ns")
    devices = dp_count * ns_count
    lay = Layout(dp_count, ns_count, fields.shape[0], fields.shape[1])
    z, x, n = lay.here()
    member = lay.fore(n) * lay.x + x
    lat_count = lay.rows * dp_count

    moves = []
    for d in range(dp_count):
        for k in range(ns_count):
            to = (lay.fore(k) * lay.x + d % lay.x) * ns_count + lay.back(d // lay.x)
            moves.append((d * ns_count + k, to))
    fields, targets, valid = [lax.ppermute(v, BOTH, moves) for v in (fields, targets, valid)]

    colatitude = math.pi * (np.arange(lat_count) + 0.5) / lat_count
    sines = jnp.asarray(np.sin(colatitude).astype(np.float32).reshape(dp_count, lay.rows))
    local_sine = lax.dynamic_index_in_dim(sines, member, keepdims=False)
    var_weight = 1.0 + 0.5 * var_class.astype(FULL)
    pixel_map = valid.astype(FULL) * local_sine[None, :, None]
    weight_part = jnp.sum(pixel_map)
    weight_map = pixel_map[..., None] * var_weight

    ff_dev, e_own = up_t.shape[1], E // devices
    pack = -(-(2 * ff_dev + 2 * e_own) // 16) * 16

    def mine(values):
        return lax.dynamic_slice_in_dim(values, n * e_own, e_own, 0)

    def packed(up, down_, enc, dec_, extra):
        both = jnp.concatenate([wide(mine(enc)), wide(mine(dec_))], axis=1)
        return pad_rows(jnp.concatenate([up[0], down_[0], both, extra], axis=0), pack)

    def unpacked(every):
        up = every[:, :ff_dev].reshape(FF, E)
        down_ = every[:, ff_dev : 2 * ff_dev].reshape(FF, E)
        both = every[:, 2 * ff_dev : 2 * ff_dev + e_own].reshape(E, E)
        extra = every[:, 2 * ff_dev + e_own : 2 * ff_dev + 2 * e_own]
        return up, down_, both[:, :C], both[:, 128 : 128 + C], extra

    gain_rows = jnp.pad(mine(gains[0]), ((0, 0), (0, E - 2)))
    weight_rows = jnp.broadcast_to(weight_part, (e_own, E))
    every_low, every_mom = exchange(
        lay,
        [
            packed(up_t, down, enc_t, dec, gain_rows).astype(LOW),
            packed(up_mom, down_mom, enc_mom, dec_mom, weight_rows),
        ],
        ["same", "same"],
        "all",
        0,
    )
    up_w, down_w, enc_w, dec_w, extra = unpacked(every_low)
    gain_w = extra.reshape(E, E)[:, :2]
    up_mom_all, down_mom_all, enc_mom_all, dec_mom_all, extra = unpacked(every_mom)
    loss_weight = jnp.sum(extra[:, 0, 0]) * jnp.sum(var_weight)

    spec_w = fetch_spec(lay, spec[0])
    tables = dft_tables(lay, fields.shape[2]) + legendre_tables(lay, member, lat_count)
    weights = (spec_w, up_w, down_w, gain_w)

    incoming = fields
    saved = []
    forecasts = []
    for step in range(2):
        hidden = jnp.einsum("brkc,ec->brke", incoming, enc_w, preferred_element_type=FULL)
        hidden, kept = forward_block(lay, hidden, weights, tables, 6)
        closing = hidden.astype(LOW)
        forecast = jnp.einsum("brke,ec->brkc", closing, dec_w, preferred_element_type=FULL)
        saved.append((incoming, kept, closing))
        forecasts.append(forecast)
        incoming = forecast.astype(LOW)
    loss_local = jnp.zeros((), FULL)
    loss_grads = []
    for step in range(2):
        error = forecasts[step] - targets[step].astype(FULL)
        loss_local = loss_local + jnp.sum(weight_map * error * error)
        loss_grads.append(2.0 * weight_map * error / loss_weight)
    gradient = loss_grads[1]
    sums = None
    for step in (1, 0):
        incoming, kept, closing = saved[step]
        low_grad = gradient.astype(LOW)
        d_dec = jnp.einsum("brke,brkc->ec", closing, low_grad, preferred_element_type=FULL)
        gradient = jnp.einsum("brkc,ec->brke", low_grad, dec_w, preferred_element_type=FULL)
        gradient, pieces = backward_block(lay, gradient, kept, weights, tables, 6)
        low_grad = gradient.astype(LOW)
        d_enc = jnp.einsum("brkc,brke->ec", incoming, low_grad, preferred_element_type=FULL)
        terms = pieces + (d_enc, d_dec)
        sums = terms if sums is None else tuple(a + b for a, b in zip(sums, terms))
        if step == 1:
            gradient = loss_grads[0] + jnp.einsum(
                "brke,ec->brkc", low_grad, enc_w, preferred_element_type=FULL
            )
    d_spec, d_up, d_down, d_gain, d_enc, d_dec = sums

    g_spec = return_spec(lay, d_spec)[None]
    both = jnp.concatenate([wide(d_enc), wide(d_dec)], axis=1).reshape(devices, e_own, E)
    extra = jnp.concatenate([d_gain, jnp.broadcast_to(loss_local, (E, 1))], axis=1)
    extra = jnp.pad(extra, ((0, 0), (0, E - 3))).reshape(devices, e_own, E)
    blocks = [d_up.reshape(devices, ff_dev, E), d_down.reshape(devices, ff_dev, E), both, extra]
    (got,) = exchange(
        lay, [pad_rows(jnp.concatenate(blocks, axis=1), pack)], ["each"], "all", 1
    )
    chunk = jnp.sum(got, axis=0)
    at_extra = 2 * ff_dev + e_own
    lanes = jnp.arange(E) == 3
    spec_sq = jnp.sum(g_spec * g_spec)
    chunk = chunk.at[at_extra].set(jnp.where(lanes, spec_sq, chunk[at_extra]))
    (every,) = exchange(lay, [chunk], ["same"], "all", 8)
    g_up, g_down, g_enc, g_dec, extra = unpacked(every)
    loss_sum = extra[0, 0, 2]
    g_gain = extra.reshape(E, E)[:, :2]
    total_sq = jnp.sum(extra[:, 0, 3])
    for value in (g_up, g_down, g_enc, g_dec, g_gain):
        total_sq = total_sq + jnp.sum(value * value)
    grad_norm = jnp.sqrt(total_sq)
    clip_scale = CLIP_NORM / jnp.maximum(grad_norm, CLIP_NORM)

    d = lax.axis_index("dp")
    index = d * ns_count + n
    enc_new_mom = MOMENTUM * enc_mom_all + clip_scale * g_enc
    dec_new_mom = MOMENTUM * dec_mom_all + clip_scale * g_dec
    up_new_mom = MOMENTUM * up_mom_all + clip_scale * g_up
    down_new_mom = MOMENTUM * down_mom_all + clip_scale * g_down
    small = newton(jnp.stack([enc_new_mom, dec_new_mom])) * math.sqrt(max(1.0, E / C))
    large = newton(jnp.stack([up_new_mom, down_new_mom])) * math.sqrt(max(1.0, FF / E))

    def muon(master, matrix, at, rows):
        own = lax.dynamic_slice_in_dim(matrix, at * rows, rows, 0)
        return master * (1.0 - RATE_MUON * DECAY) - RATE_MUON * own.reshape(master.shape)

    def own_rows(values, at, rows):
        return lax.dynamic_slice_in_dim(values, at * rows, rows, 0)

    e_dev = lay.e_dev
    g_gain_own = own_rows(g_gain, d, e_dev)[None]
    spec_m_new, spec_v_new, spec_new = adam_step(
        spec, spec_m, spec_v, clip_scale * g_spec, RATE_SPECTRAL
    )
    gain_m_new, gain_v_new, gain_new = adam_step(
        gains, gain_m, gain_v, clip_scale * g_gain_own, RATE_GAIN
    )
    return (
        loss_sum,
        loss_weight,
        grad_norm,
        own_rows(enc_new_mom, d, e_dev),
        muon(enc_t, small[0], d, e_dev),
        own_rows(dec_new_mom, d, e_dev),
        muon(dec, small[1], d, e_dev),
        own_rows(up_new_mom, index, ff_dev)[None],
        muon(up_t, large[0], index, ff_dev),
        own_rows(down_new_mom, index, ff_dev)[None],
        muon(down, large[1], index, ff_dev),
        spec_m_new,
        spec_v_new,
        spec_new,
        spec_new.astype(LOW),
        gain_m_new,
        gain_v_new,
        gain_new,
    )


def solution(mesh):
    rows = P(None, BOTH, None)
    shard = P("dp", None)
    whole = P(None, "dp", "ns", None, None)
    gain = P(None, "dp", None)
    placed = (
        P("ns", "dp", None, None),
        P(None, "ns", "dp", None, None),
        P("ns", "dp", None),
        P(),
        *[shard] * 4,
        *[whole] * 3,
        *[rows] * 4,
        *[gain] * 3,
    )
    return jax.shard_map(
        local,
        mesh=mesh,
        in_specs=placed,
        out_specs=(P(), P(), P(), *[shard] * 4, *[rows] * 4, *[whole] * 4, *[gain] * 3),
        check_vma=False,
    )
```

```python
import math

import jax
import jax.numpy as jnp
import ml_dtypes
import numpy as np
from jax import lax
from jax.experimental import pallas as pl
from jax.experimental.layout import Layout as DeviceLayout
from jax.experimental.layout import with_layout_constraint
from jax.experimental.pallas import tpu as pltpu
from jax.sharding import PartitionSpec as P

E = 256
FF = 512
C = 73
LDEG = 96
MM = 96
NL = 1
NS_ITERS = 5
STEP = 10

EXACT = lax.Precision.HIGHEST
EPSILON = 1e-06
CLIP_NORM = 0.02
RATE_SPECTRAL = 0.05
RATE_GAIN = 0.1
RATE_MUON = 0.5
BETA_FIRST = 0.9
BETA_SECOND = 0.999
MOMENTUM = 0.95
DECAY = 0.01
NS_FIRST = 3.4445
NS_SECOND = -4.775
NS_THIRD = 2.0315
LOW = jnp.bfloat16
FULL = jnp.float32
MESH = pl.DeviceIdType.MESH
CHUNK = 16
BOTH = ("dp", "ns")


class Layout:
    def __init__(self, dp, ns, items, rows):
        self.dp, self.ns, self.items, self.rows = dp, ns, items, rows
        self.x = dp // ns
        self.mper, self.lper, self.lns = MM // dp, LDEG // dp, LDEG // ns
        self.kb = 8 // items
        self.nkb = -(-self.mper // self.kb)
        self.blocks = [[i for i in range(self.lper) if i >= k * self.kb] for k in range(self.nkb)]
        self.starts = np.cumsum([0] + [len(b) for b in self.blocks]).tolist()
        self.nblk = self.starts[-1]
        self.cols = items * rows * self.kb * 2
        self.slots = -(-self.lns // dp)
        self.even = self.lns % dp == 0
        self.e_dev = E // dp
        self.e_plane = self.x * self.e_dev
        self.size = 2 * self.kb * items
        self.counts = [len(b) for b in self.blocks]
        self.ends = [min((g + 1) * self.kb, self.lper) for g in range(self.nkb)]
        self.ends[-1] = self.lper

    def fore(self, n):
        half = self.ns // 2
        return (n % 2) * half + n // 2

    def back(self, z):
        half = self.ns // 2
        return (z % half) * 2 + z // half

    def here(self):
        d, n = lax.axis_index("dp"), lax.axis_index("ns")
        return d // self.x, d % self.x, n


def group_of(lay, kind):
    z, x, n = lay.here()
    if kind == "plane":
        return lay.dp, lay.fore(n) * lay.x + x, lambda p: (z * lay.x + p % lay.x, lay.back(p // lay.x))
    if kind == "line":
        return lay.ns, z, lambda q: (q * lay.x + x, n)
    return (
        lay.dp * lay.ns,
        (z * lay.x + x) * lay.ns + n,
        lambda q: (q // lay.ns, q % lay.ns),
    )


def exchange(lay, arrays, kinds, group, tag):
    count = {"plane": lay.dp, "line": lay.ns, "all": lay.dp * lay.ns}[group]

    def kernel(*refs):
        total = len(arrays)
        ins, outs = refs[:total], refs[total : 2 * total]
        send, recv, own = refs[2 * total :]
        size, me, device = group_of(lay, group)
        barrier = pltpu.get_barrier_semaphore()

        @pl.loop(1, size)
        def _(step):
            pl.semaphore_signal(
                barrier, inc=1, device_id=device(lax.rem(me + step, size)), device_id_type=MESH
            )

        pl.semaphore_wait(barrier, size - 1)

        @pl.loop(1, size)
        def _(step):
            peer = lax.rem(me + step, size)
            for at in range(total):
                pltpu.make_async_remote_copy(
                    src_ref=ins[at].at[peer] if kinds[at] == "each" else ins[at],
                    dst_ref=outs[at].at[me],
                    send_sem=send.at[at],
                    recv_sem=recv.at[at],
                    device_id=device(peer),
                    device_id_type=MESH,
                ).start()

        for at in range(total):
            mine = ins[at].at[me] if kinds[at] == "each" else ins[at]
            copy = pltpu.make_async_copy(mine, outs[at].at[me], own)
            copy.start()
            copy.wait()
        for at in range(total):
            some = outs[at].at[pl.ds(0, size - 1)]
            pltpu.make_async_remote_copy(
                src_ref=some,
                dst_ref=some,
                send_sem=send.at[at],
                recv_sem=recv.at[at],
                device_id=device(lax.rem(me + 1, size)),
                device_id_type=MESH,
            ).wait()

    shapes = [
        jax.ShapeDtypeStruct(a.shape if k == "each" else (count,) + a.shape, a.dtype)
        for a, k in zip(arrays, kinds)
    ]
    spot = pl.BlockSpec(memory_space=pl.ANY)
    return pl.pallas_call(
        kernel,
        out_shape=shapes,
        in_specs=[spot] * len(arrays),
        out_specs=[spot] * len(arrays),
        scratch_shapes=[
            pltpu.SemaphoreType.DMA((len(arrays),)),
            pltpu.SemaphoreType.DMA((len(arrays),)),
            pltpu.SemaphoreType.DMA,
        ],
        compiler_params=pltpu.CompilerParams(collective_id=tag, has_side_effects=True),
        name=f"exchange_{group}_{tag}",
    )(*arrays)


def legendre(lat_count):
    colatitude = math.pi * (np.arange(lat_count) + 0.5) / lat_count
    cosine, log_sine = np.cos(colatitude)[None, :], np.log(np.sin(colatitude))[None, :]
    orders = np.arange(MM, dtype=np.float64)
    ladder = np.arange(1, MM, dtype=np.float64)
    sums = np.concatenate([[0.0], np.cumsum(np.log((2 * ladder - 1) / (2 * ladder)))])
    diagonal = np.exp(
        (0.5 * np.log((2 * orders + 1) / (4 * math.pi)) + 0.5 * sums)[:, None]
        + orders[:, None] * log_sine
    )
    table = np.zeros((LDEG, MM, lat_count))
    for degree in range(LDEG):
        for order in range(min(degree, MM - 1) + 1):
            if degree == order:
                table[degree, order] = diagonal[order]
                continue
            a = math.sqrt((4.0 * degree**2 - 1) / (degree**2 - order**2))
            value = cosine[0] * table[degree - 1, order]
            if degree >= 2:
                b = math.sqrt(
                    max((degree - 1.0) ** 2 - order**2, 0) / (4 * (degree - 1.0) ** 2 - 1)
                )
                value = value - b * table[degree - 2, order]
            table[degree, order] = a * value
    return table.astype(np.float32)


def low_table(values):
    return values.astype(np.float32).astype(ml_dtypes.bfloat16)


def dft_tables(lay, lon_count):
    turns = np.arange(lon_count)[:, None] * np.arange(MM)[None, :] % lon_count
    phases = 2 * math.pi / lon_count * turns
    paired = np.stack([np.cos(phases), -np.sin(phases)], axis=2)
    weight = np.where(np.arange(MM) == 0, 1.0, 2.0)
    forward = paired * (2 * math.pi / lon_count)
    inverse = paired * weight[None, :, None] / (2 * math.pi)

    def order(table):
        table = table.reshape(lon_count, lay.mper, lay.dp, 2).transpose(0, 2, 1, 3)
        pad = lay.nkb * lay.kb - lay.mper
        table = np.pad(table, ((0, 0), (0, 0), (0, pad), (0, 0)))
        return low_table(table.reshape(lon_count, -1))

    return order(forward), order(inverse)


def legendre_tables(lay, lat_count):
    plain = legendre(lat_count)
    colatitude = math.pi * (np.arange(lat_count) + 0.5) / lat_count
    quadrature = 2 * math.pi * math.pi / lat_count * np.sin(colatitude)
    pad = lay.nkb * lay.kb - lay.mper

    def own(table):
        table = table.reshape(lay.lper, lay.dp, lay.mper, lay.dp, lat_count)
        table = np.pad(table.transpose(3, 1, 0, 2, 4), ((0, 0), (0, 0), (0, 0), (0, pad), (0, 0)))
        table = low_table(table)
        blocks = []
        for k in range(lay.nkb):
            part = table[:, :, k * lay.kb :, k * lay.kb : (k + 1) * lay.kb]
            blocks.append(part.reshape(lay.dp, -1, lay.kb * lat_count))
        across = [jnp.asarray(np.ascontiguousarray(b.swapaxes(1, 2))) for b in blocks]
        return jnp.asarray(np.concatenate(blocks, axis=1)), across

    col = np.arange(lay.dp * lay.cols)
    col_part, col_k = col % 2, col // 2 % lay.kb
    col_item = col // (2 * lay.kb * lay.rows) % lay.items
    col_lat = col // lay.cols * lay.rows + col // (2 * lay.kb) % lay.rows
    col_kind = (col_part * lay.kb + col_k) * lay.items + col_item
    pick = col_k * lat_count + col_lat
    spread = np.arange(lay.kb * lat_count)[:, None] == pick[None, :]
    same = np.arange(lay.size)[:, None] == col_kind[None, :]
    wide_same = np.tile(same.T, (1, CHUNK))
    count = lay.dp * lay.lper
    repeat = np.arange(CHUNK * lay.size)[:, None] // lay.size == np.arange(CHUNK)[None, :]
    across = np.arange(count)[:, None] == np.arange(count * lay.size)[None, :] // lay.size
    ones = [
        jnp.asarray(v.astype(ml_dtypes.bfloat16))
        for v in (spread, spread.T, same, wide_same, repeat, across)
    ]
    return own(plain * quadrature.astype(np.float32)[None, None, :]), own(plain), ones


def normalize(values, gain_vec):
    return (
        values * lax.rsqrt(jnp.mean(values * values, axis=-1, keepdims=True) + EPSILON) * gain_vec
    )


def turned(real, imag):
    both = jnp.concatenate([real[:, None], imag[:, None]], axis=1)
    return both.reshape(-1, E).astype(LOW)


def parts_of(values):
    split = values.reshape(-1, 2, 8, E)
    return split[:, 0], split[:, 1]


def spectral(lay, values, first, second, ones, tag, spec_w, fetch=(), carry=(), saved=(), earlier=()):
    back, last = bool(saved), bool(earlier)
    nkb, dp, ns, size = lay.nkb, lay.dp, lay.ns, lay.size
    counts, ends, lper = lay.counts, lay.ends, lay.lper
    items, rows = values.shape[:2]
    laid = values.reshape(items, rows, dp, nkb, 2 * lay.kb, E)
    laid = laid.transpose(2, 3, 0, 1, 4, 5).reshape(dp, nkb, lay.cols, E)
    w_shape = (ns, lper, 2, lay.e_plane, E)
    dma = pltpu.SemaphoreType.DMA
    tiles = [(dp, c, size, E) for c in counts]
    spans = [(g * lay.kb, ends[g] - g * lay.kb) for g in range(nkb)]

    ins = {"f": [laid], "p1": [first], "p2": list(second), "ones": list(ones), "w": [spec_w]}
    ins |= {"old": list(saved), "earlier": list(earlier), "carry": list(carry)}
    outs = {"y": [((dp, nkb, lay.cols, E), LOW)]}
    outs["keep"] = [] if back else [(t, LOW) for t in tiles]
    outs["whole"] = [(w_shape, LOW)] if fetch else []
    outs["d"] = [(w_shape, LOW)] if back and not last else []
    owned = (dp, lay.slots, 2, lay.e_dev, E) if lay.even else (lper, lay.x, 2, lay.e_dev, E)
    outs["g"] = [(owned, FULL)] if last else []
    outs["carried"] = [(c.shape, c.dtype) for c in carry]
    tall, broad = lay.size * dp * np.array(counts), dp * lay.cols
    buffers = {
        "f_got": [((nkb, dp, lay.cols, E), LOW)],
        "t1": [((int(h), broad), LOW) for h in tall],
        "t2": [((broad, int(h)), LOW) for h in tall],
        "p1_v": [(first.shape[1:], LOW)],
        "p2_v": [(p.shape[1:], LOW) for p in second],
        "ones_v": [(o.shape, LOW) for o in ones],
        "w_v": [(w_shape, LOW)],
        "s_put": [(t, LOW) for t in tiles],
        "s_got": [(t, LOW) for t in tiles],
        "m_put": [(t, LOW) for t in tiles],
        "m_got": [(t, LOW) for t in tiles],
        "y_put": [((dp, nkb, lay.cols, E), LOW)],
        "old_v": [(t, LOW) for t in tiles] if back else [],
        "early_v": [(w_shape, LOW)] if last else [],
        "d_put": [(w_shape, LOW)] if back else [],
        "d_got": [(w_shape, LOW)] if last else [],
        "g_put": [((lper, lay.x, 2, lay.e_dev, E), FULL)] if last else [],
    }
    sems = {"f_sem": nkb, "s_sem": nkb, "m_sem": nkb, "y_sem": 1, "send": 4, "own": nkb + 4}
    sems |= {"load": 2 + len(second) + len(ones) + len(saved) + 1}
    sems |= {"line_send": 1, "line_got": 2 * (ns - 1) * nkb, "carry_sem": 2, "g_sem": 2}

    def kernel(*refs):
        refs = list(refs)
        r = {}
        for group in (ins, outs, buffers):
            for name, entries in group.items():
                r[name] = refs[: len(entries)]
                del refs[: len(entries)]
        for name in sems:
            r[name] = refs.pop(0)
        (f_ref,), (y_ref,), (f_got,), (y_put,), (w,) = (
            r[k] for k in ("f", "y", "f_got", "y_put", "w_v")
        )
        t1, t2, s_put, s_got, m_put, m_got = (
            r[k] for k in ("t1", "t2", "s_put", "s_got", "m_put", "m_got")
        )
        spread, spread_t, same, wide_same, repeat, across = r["ones_v"]
        send, own = r["send"], r["own"]
        z, x, n = lay.here()
        _, me, device = group_of(lay, "plane")
        _, _, line_device = group_of(lay, "line")
        line = bool(fetch) or last
        partner = (lay.fore(n) * lay.x + x, lay.back(z))
        apart = lay.fore(n) != z
        barrier = pltpu.get_barrier_semaphore()

        def greet(target):
            pl.semaphore_signal(barrier, inc=1, device_id=target, device_id_type=MESH)

        @pl.loop(1, dp)
        def _(step):
            greet(device(lax.rem(me + step, dp)))

        if line:

            @pl.loop(1, ns)
            def _(step):
                greet(line_device(lax.rem(z + step, ns)))

        if carry:

            @pl.when(apart)
            def _():
                greet(partner)

        pairs = [(r["p1"][0].at[me], r["p1_v"][0])]
        pairs += [(a, b) for a, b in zip(r["ones"], r["ones_v"])]
        pairs += [(a.at[me], b) for a, b in zip(r["p2"], r["p2_v"])]
        tables_at = len(pairs)
        if not fetch:
            pairs += [(r["w"][0], w)]
        else:
            pairs += [(r["w"][0], w.at[z])]
        pairs += list(zip(r["old"], r["old_v"])) + list(zip(r["earlier"], r["early_v"]))
        loads = []
        for at, (source, target) in enumerate(pairs):
            copy = pltpu.make_async_copy(source, target, r["load"].at[at])
            copy.start()
            loads.append(copy)
        mine = []
        for k in range(nkb):
            copy = pltpu.make_async_copy(f_ref.at[me, k], f_got.at[k, me], own.at[k])
            copy.start()
            mine.append(copy)
        waits = dp - 1 + (ns - 1 if line else 0)
        if carry:
            pl.semaphore_wait(barrier, waits + jnp.where(apart, 1, 0))
        else:
            pl.semaphore_wait(barrier, waits)

        def remote(source, target, sent, got, to):
            return pltpu.make_async_remote_copy(
                src_ref=source,
                dst_ref=target,
                send_sem=sent,
                recv_sem=got,
                device_id=to,
                device_id_type=MESH,
            )

        def push(source, target, sent, got, peer):
            remote(source, target, sent, got, device(peer)).start()

        def settle(ref, sent, got, sending):
            copy = remote(ref, ref, sent, got, device(lax.rem(me + 1, dp)))
            if sending:
                copy.wait_send()
            else:
                copy.wait_recv()

        for k in range(nkb):

            @pl.loop(1, dp)
            def _(step):
                peer = lax.rem(me + step, dp)
                push(f_ref.at[peer, k], f_got.at[k, me], send.at[0], r["f_sem"].at[k], peer)

        lines = [(sign, at * (ns - 1) * nkb) for at, sign in enumerate((1, -1))]

        def inside(at):
            return jnp.logical_and(at >= 0, at < ns)

        def line_wait(distance, g):
            for sign, at in lines:

                @pl.when(inside(z - sign * distance))
                def _():
                    some = w.at[0, pl.ds(*spans[g])]
                    sem = r["line_got"].at[at + (distance - 1) * nkb + g]
                    remote(some, some, r["line_send"].at[0], sem, device(me)).wait_recv()

        def line_push(distance):
            for g, (begin, length) in enumerate(spans):
                span = pl.ds(begin, length)
                if distance > 1:
                    line_wait(distance - 1, g)
                for sign, at in lines:
                    source = z - sign * (distance - 1)

                    @pl.when(jnp.logical_and(inside(z + sign), inside(source)))
                    def _():
                        remote(
                            r["w"][0].at[span] if distance == 1 else w.at[source, span],
                            w.at[source, span],
                            r["line_send"].at[0],
                            r["line_got"].at[at + (distance - 1) * nkb + g],
                            line_device(z + sign),
                        ).start()

        if fetch:
            line_push(1)

        if carry:
            (gone,), (come,) = r["carry"], r["carried"]
            swap = remote(gone, come, r["carry_sem"].at[0], r["carry_sem"].at[1], partner)
            stay = pltpu.make_async_copy(gone, come, r["carry_sem"].at[0])

            @pl.when(apart)
            def _():
                swap.start()

            @pl.when(jnp.logical_not(apart))
            def _():
                stay.start()

        for at in range(tables_at):
            loads[at].wait()
        for k in range(nkb):

            @pl.loop(0, dp * counts[k] // CHUNK)
            def _(chunk):
                at = pl.multiple_of(dp * lay.starts[k] + chunk * CHUNK, CHUNK)
                part = r["p1_v"][0][pl.ds(at, CHUNK), :]
                part = jnp.dot(repeat[...], part, preferred_element_type=FULL).astype(LOW)
                full = jnp.dot(part, spread[...], preferred_element_type=FULL)
                full = full.reshape(CHUNK, size, broad) * same[...].astype(FULL)[None]
                to = pl.multiple_of(chunk * CHUNK * size, CHUNK * size)
                t1[k][pl.ds(to, CHUNK * size), :] = full.reshape(CHUNK * size, broad).astype(LOW)

        for k in range(nkb):
            mine[k].wait()
            settle(f_got.at[k, pl.ds(0, dp - 1)], send.at[0], r["f_sem"].at[k], False)
            high = counts[k] * size

            def modes_for(peer):
                part = t1[k][pl.ds(pl.multiple_of(peer * high, 16), high), :]
                got = f_got[k].reshape(dp * lay.cols, E)
                out = jnp.dot(part, got, preferred_element_type=FULL).astype(LOW)
                return out.reshape(counts[k], size, E)

            @pl.loop(1, dp)
            def _(step):
                peer = lax.rem(me + step, dp)
                s_put[k][peer] = modes_for(peer)
                push(s_put[k].at[peer], s_got[k].at[me], send.at[1], r["s_sem"].at[k], peer)

            s_got[k][me] = modes_for(me)

        if fetch:
            line_push(2)
        for k in range(nkb):
            width = CHUNK * size
            count = dp * counts[k]

            @pl.loop(0, count // CHUNK)
            def _(chunk):
                to = pl.ds(pl.multiple_of(chunk * width, width), width)
                part = jnp.dot(
                    r["p2_v"][k][...], across[pl.ds(0, count), to], preferred_element_type=FULL
                )
                full = jnp.dot(spread_t[...], part.astype(LOW), preferred_element_type=FULL)
                t2[k][:, to] = (full * wide_same[...].astype(FULL)).astype(LOW)

        if fetch:
            for distance in range(3, ns):
                line_push(distance)

        for copy in loads[tables_at:]:
            copy.wait()
        for g, (begin, length) in enumerate(spans):
            settle(s_got[g].at[pl.ds(0, dp - 1)], send.at[1], r["s_sem"].at[g], False)
            span = pl.ds(begin, length)
            if fetch:
                line_wait(ns - 1, g)

            def rows_at(group, degree):
                tiles = [group[k][:, degree - k * lay.kb] for k in range(g + 1)]
                return jnp.concatenate([t.reshape(dp * size, E) for t in tiles], axis=0)

            @pl.loop(begin, ends[g])
            def _(degree):
                rows_in = rows_at(s_got, degree)
                dims = (((1,), (1 if back else 0,)), ((), ()))
                by_real, by_imag = (
                    lax.dot_general(
                        rows_in, w[:, degree, p].reshape(E, E), dims, preferred_element_type=FULL
                    )
                    for p in (0, 1)
                )
                (rr, ir), (ri, ii) = parts_of(by_real), parts_of(by_imag)
                mixed = turned(rr + ii, ir - ri) if back else turned(rr - ii, ri + ir)
                for k in range(g + 1):
                    part = mixed[k * dp * size : (k + 1) * dp * size]
                    m_put[k][:, degree - k * lay.kb] = part.reshape(dp, size, E)

            for k in range(g + 1):
                there = pl.ds(begin - k * lay.kb, length)

                @pl.loop(1, dp)
                def _(step):
                    peer = lax.rem(me + step, dp)
                    target = m_got[k].at[me, there]
                    push(m_put[k].at[peer, there], target, send.at[2], r["m_sem"].at[k], peer)

            if back:
                (d_put,) = r["d_put"]

                @pl.loop(begin, ends[g])
                def _(degree):
                    dims = (((0,), (0,)), ((), ()))
                    olds, grads = rows_at(r["old_v"], degree), rows_at(s_got, degree)
                    real, imag = parts_of(grads.astype(FULL))
                    for p, right in ((0, grads), (1, turned(imag, -real))):
                        total = lax.dot_general(olds, right, dims, preferred_element_type=FULL)
                        total = total.reshape(ns, lay.e_plane, E)
                        if last:
                            total = total + r["early_v"][0][:, degree, p].astype(FULL)
                        d_put[:, degree, p] = total.astype(LOW)

                if last:
                    (d_got,) = r["d_got"]

                    @pl.loop(1, ns)
                    def _(step):
                        to = lax.rem(z + step, ns)
                        remote(
                            d_put.at[to, span],
                            d_got.at[z, span],
                            r["line_send"].at[0],
                            r["line_got"].at[g],
                            line_device(to),
                        ).start()

        for k in range(nkb):
            m_got[k][me] = m_put[k][me]
        keeps = []
        for at, (source, target) in enumerate(
            list(zip(s_got, r["keep"])) + [(w, t) for t in r["whole"]] + list(zip(r["d_put"], r["d"]))
        ):
            copy = pltpu.make_async_copy(source, target, own.at[at])
            copy.start()
            keeps.append(copy)

        for k in range(nkb):
            settle(m_got[k].at[pl.ds(0, dp - 1)], send.at[2], r["m_sem"].at[k], False)

            def rows_for(peer):
                part = t2[k][pl.ds(pl.multiple_of(peer * lay.cols, 16), lay.cols), :]
                got = m_got[k][...].reshape(-1, E)
                return jnp.dot(part, got, preferred_element_type=FULL).astype(LOW)

            @pl.loop(1, dp)
            def _(step):
                peer = lax.rem(me + step, dp)
                y_put[peer, k] = rows_for(peer)
                push(y_put.at[peer, k], y_ref.at[me, k], send.at[3], r["y_sem"].at[0], peer)

            y_put[me, k] = rows_for(me)
        ends_with = pltpu.make_async_copy(y_put.at[me], y_ref.at[me], own.at[nkb + 2])
        ends_with.start()

        if last:
            (g_put,), (g_ref,) = r["g_put"], r["g"]
            for g, (begin, length) in enumerate(spans):
                got = d_got.at[pl.ds(0, ns - 1), pl.ds(begin, length)]
                settle(got, r["line_send"].at[0], r["line_got"].at[g], False)

                @pl.loop(begin, ends[g])
                def _(degree):
                    for p in (0, 1):
                        total = d_put[z, degree, p].astype(FULL)
                        for step in range(1, ns):
                            source = lax.rem(z + step, ns)
                            total = total + d_got[source, degree, p].astype(FULL)
                        g_put[degree, :, p] = total.reshape(lay.x, lay.e_dev, E)
                    if lay.even:
                        slot = lax.rem(degree, lay.slots)
                        for at_x in range(lay.x):
                            peer = lay.fore(degree // lay.slots) * lay.x + at_x

                            @pl.when(peer != me)
                            def _():
                                push(
                                    g_put.at[degree, at_x],
                                    g_ref.at[me, slot],
                                    r["g_sem"].at[0],
                                    r["g_sem"].at[1],
                                    peer,
                                )

            if lay.even:
                copy = pltpu.make_async_copy(
                    g_put.at[pl.ds(n * lay.slots, lay.slots), x], g_ref.at[me], own.at[nkb + 3]
                )
            else:
                copy = pltpu.make_async_copy(g_put, g_ref, own.at[nkb + 3])
            copy.start()
            copy.wait()
            if lay.even:
                some = g_ref.at[pl.ds(0, dp - 1)]
                settle(some, r["g_sem"].at[0], r["g_sem"].at[1], True)
                settle(some, r["g_sem"].at[0], r["g_sem"].at[1], False)

        ends_with.wait()
        for copy in keeps:
            copy.wait()
        settle(f_ref.at[pl.ds(0, dp - 1)], send.at[0], r["f_sem"].at[0], True)
        for k in range(nkb):
            settle(s_got[k].at[pl.ds(0, dp - 1)], send.at[1], r["s_sem"].at[0], True)
            settle(m_got[k].at[pl.ds(0, dp - 1)], send.at[2], r["m_sem"].at[0], True)
        if last:
            settle(w.at[pl.ds(0, ns - 1)], r["line_send"].at[0], r["line_got"].at[0], True)
        if fetch:
            for distance in range(1, ns):
                for sign, _ in lines:

                    @pl.when(jnp.logical_and(inside(z + sign), inside(z - sign * (distance - 1))))
                    def _():
                        settle(w.at[0], r["line_send"].at[0], r["line_got"].at[0], True)

        if carry:

            @pl.when(apart)
            def _():
                swap.wait()

            @pl.when(jnp.logical_not(apart))
            def _():
                stay.wait()

        settle(y_put.at[pl.ds(0, dp - 1)], send.at[3], r["y_sem"].at[0], True)
        settle(y_put.at[pl.ds(0, dp - 1)], send.at[3], r["y_sem"].at[0], False)

    spot = pl.BlockSpec(memory_space=pl.ANY)
    operands = [v for group in ins.values() for v in group]
    results = [jax.ShapeDtypeStruct(*v) for group in outs.values() for v in group]
    scratch = [pltpu.VMEM(*v) for group in buffers.values() for v in group]
    scratch += [dma((count,)) for count in sems.values()]
    got = list(
        pl.pallas_call(
            kernel,
            out_shape=results,
            in_specs=[spot] * len(operands),
            out_specs=[spot] * len(results),
            scratch_shapes=scratch,
            compiler_params=pltpu.CompilerParams(
                collective_id=tag, has_side_effects=True, vmem_limit_bytes=58 << 20
            ),
            cost_estimate=pl.CostEstimate(
                flops=40_000_000_000, bytes_accessed=100_000_000, transcendentals=0
            ),
            name="spectral_back" if back else "spectral",
        )(*operands)
    )
    given = {}
    for name, entries in outs.items():
        given[name] = got[: len(entries)]
        del got[: len(entries)]
    rows_out = given["y"][0].reshape(dp, nkb, items, rows, 2 * lay.kb, E)
    rows_out = rows_out.transpose(2, 3, 0, 1, 4, 5).reshape(items, rows, -1, E)
    return rows_out, given


def prologue(lay, spec_laid, small, swaps, tag):
    chips = lay.dp * lay.ns // 2

    def kernel(*refs):
        spec_ref, small_ref = refs[:2]
        swap_refs = refs[2 : 2 + len(swaps)]
        spec_got, small_got = refs[2 + len(swaps) : 4 + len(swaps)]
        swap_got = refs[4 + len(swaps) : 4 + 2 * len(swaps)]
        sent, got, own = refs[4 + 2 * len(swaps) :]
        z, x, n = lay.here()
        _, me, device = group_of(lay, "plane")
        core = n % 2
        chip = (z * lay.x + x) * (lay.ns // 2) + n // 2
        sibling = (z * lay.x + x, n + 1 - 2 * core)
        partner = (lay.fore(n) * lay.x + x, lay.back(z))
        apart = lay.fore(n) != z

        def chip_device(at):
            return at // (lay.ns // 2), at % (lay.ns // 2) * 2 + core

        barrier = pltpu.get_barrier_semaphore()

        def greet(target):
            pl.semaphore_signal(barrier, inc=1, device_id=target, device_id_type=MESH)

        @pl.loop(1, lay.dp)
        def _(step):
            greet(device(lax.rem(me + step, lay.dp)))

        @pl.loop(1, chips)
        def _(step):
            greet(chip_device(lax.rem(chip + step, chips)))

        greet(sibling)

        @pl.when(apart)
        def _():
            greet(partner)

        pl.semaphore_wait(barrier, lay.dp + chips - 1 + jnp.where(apart, 1, 0))

        def remote(source, target, at, to):
            return pltpu.make_async_remote_copy(
                src_ref=source,
                dst_ref=target,
                send_sem=sent.at[at],
                recv_sem=got.at[at],
                device_id=to,
                device_id_type=MESH,
            )

        @pl.loop(1, chips)
        def _(step):
            to = chip_device(lax.rem(chip + step, chips))
            remote(small_ref, small_got.at[core, chip], 1, to).start()

        @pl.loop(1, lay.dp)
        def _(step):
            peer = lax.rem(me + step, lay.dp)
            remote(spec_ref.at[peer], spec_got.at[me], 0, device(peer)).start()

        moves = []
        for at, (a, b) in enumerate(zip(swap_refs, swap_got)):
            moves.append((remote(a, b, 3 + at, partner), pltpu.make_async_copy(a, b, sent.at[3 + at])))

        @pl.when(apart)
        def _():
            for far, near in moves:
                far.start()

        @pl.when(jnp.logical_not(apart))
        def _():
            for far, near in moves:
                near.start()

        copies = [
            pltpu.make_async_copy(small_ref, small_got.at[core, chip], own.at[0]),
            pltpu.make_async_copy(spec_ref.at[me], spec_got.at[me], own.at[1]),
        ]
        for copy in copies:
            copy.start()
        for copy in copies:
            copy.wait()
        some = small_got.at[core, pl.ds(0, chips - 1)]
        remote(some, some, 1, sibling).wait()
        remote(small_got.at[core], small_got.at[core], 2, sibling).start()
        some = spec_got.at[pl.ds(0, lay.dp - 1)]
        remote(some, some, 0, sibling).wait()
        remote(small_got.at[core], small_got.at[core], 2, sibling).wait()

        @pl.when(apart)
        def _():
            for far, near in moves:
                far.wait()

        @pl.when(jnp.logical_not(apart))
        def _():
            for far, near in moves:
                near.wait()

    spot = pl.BlockSpec(memory_space=pl.ANY)
    outs = [spec_laid, jax.ShapeDtypeStruct((2, chips) + small.shape, small.dtype), *swaps]
    count = 3 + len(swaps)
    got = pl.pallas_call(
        kernel,
        out_shape=[jax.ShapeDtypeStruct(o.shape, o.dtype) for o in outs],
        in_specs=[spot] * (2 + len(swaps)),
        out_specs=[spot] * len(outs),
        scratch_shapes=[
            pltpu.SemaphoreType.DMA((count,)),
            pltpu.SemaphoreType.DMA((count,)),
            pltpu.SemaphoreType.DMA((2,)),
        ],
        compiler_params=pltpu.CompilerParams(collective_id=tag, has_side_effects=True),
        name="prologue",
    )(spec_laid, small, *swaps)
    every = got[1].swapaxes(0, 1).reshape((2 * chips,) + small.shape)
    return got[0], every, list(got[2:])


def spec_out(lay, spec):
    z, x, n = lay.here()
    low = spec.astype(LOW).transpose(1, 2, 0, 3)
    tail = (2, lay.e_dev, E)
    if lay.even:
        laid = low.reshape((lay.slots, lay.dp) + tail).swapaxes(0, 1)
    else:
        at = (jnp.arange(lay.dp) - lay.lns * n) % lay.dp
        at = at[:, None] + lay.dp * jnp.arange(lay.slots)
        laid = jnp.take(low, jnp.minimum(at, lay.lns - 1), axis=0)
    return laid.reshape(lay.dp, -1, E)


def spec_in(lay, got):
    z, x, n = lay.here()
    member = lay.fore(n) * lay.x + x
    got = got.reshape((lay.ns, lay.x, lay.slots, 2, lay.e_dev, E))
    got = got.transpose(0, 2, 3, 1, 4, 5).reshape(lay.ns, lay.slots, 2, lay.e_plane, E)
    got = jnp.stack([got[lay.fore(k)] for k in range(lay.ns)])
    if lay.even:
        return got.reshape((lay.lper,) + got.shape[2:])
    degree = lay.dp * jnp.arange(lay.lper) + member
    return got[degree // lay.lns, degree % lay.lns // lay.dp]


def spec_home(lay, given, tag):
    z, x, n = lay.here()
    member = lay.fore(n) * lay.x + x
    if lay.even:
        mine = given.swapaxes(0, 1).reshape(lay.lns, 2, lay.e_dev, E)
        return mine.transpose(2, 0, 1, 3)
    first = (member - lay.lns * jnp.arange(lay.ns)) % lay.dp + lay.lns * jnp.arange(lay.ns)
    at = (first[:, None] + lay.dp * jnp.arange(lay.slots) - member) // lay.dp
    slots = given[jnp.clip(at, 0, lay.lper - 1)]
    slots = slots[np.array([lay.back(k) for k in range(lay.ns)])]
    slots = slots.transpose(0, 2, 1, 3, 4, 5)
    (back,) = exchange(lay, [slots.reshape(lay.dp, -1, E)], ["each"], "plane", tag)
    back = back.reshape(lay.dp, lay.slots, 2, lay.e_dev, E)
    degree = lay.lns * n + jnp.arange(lay.lns)
    source = degree % lay.dp
    slot = (jnp.arange(lay.lns) - (source - lay.lns * n) % lay.dp) // lay.dp
    return back[source, slot].transpose(2, 0, 1, 3)


def pad_rows(values, rows):
    return jnp.pad(values, ((0, 0),) * (values.ndim - 2) + ((0, rows - values.shape[-2]), (0, 0)))


def wide(values):
    return jnp.pad(values, ((0, 0),) * (values.ndim - 1) + ((0, 128 - values.shape[-1]),))


def forward_block(lay, residual, weights, tables, tag, fetch, carry):
    spec_w, up_w, down_w, gain_low = weights
    gain_vec = gain_low.astype(FULL)
    dft_fwd, dft_inv, quad_tab, plain_tab, ones = tables
    normed_a = normalize(residual, gain_vec[:, 0]).astype(LOW)
    fourier = jnp.einsum("brke,kq->brqe", normed_a, dft_fwd, preferred_element_type=FULL)
    restored, given = spectral(
        lay, fourier.astype(LOW), quad_tab[0], plain_tab[1], ones, tag, spec_w, fetch, carry
    )
    middle = residual + jnp.einsum(
        "brqe,kq->brke", restored, dft_inv, preferred_element_type=FULL
    )
    normed_b = normalize(middle, gain_vec[:, 1]).astype(LOW)
    pre_act = jnp.einsum("brke,fe->brkf", normed_b, up_w, preferred_element_type=FULL)
    hidden = jax.nn.gelu(pre_act).astype(LOW)
    output = middle + jnp.einsum("brkf,fe->brke", hidden, down_w, preferred_element_type=FULL)
    return (output, (residual, given["keep"], middle, normed_b, pre_act, hidden), given)


def backward_block(
    lay, output_gradient, saved, weights, tables, tag, earlier, carry, sums, d_dec
):
    residual, spectrum, middle, normed_b, pre_act, hidden = saved
    spec_w, up_w, down_w, gain_low = weights
    gain_vec = gain_low.astype(FULL)
    dft_fwd, dft_inv, quad_tab, plain_tab, ones = tables
    g_out = output_gradient.astype(LOW)
    d_down = jnp.einsum("brkf,brke->fe", hidden, g_out, preferred_element_type=FULL)
    d_hidden = jnp.einsum("brke,fe->brkf", g_out, down_w, preferred_element_type=FULL)
    d_pre = jax.vjp(jax.nn.gelu, pre_act)[1](d_hidden)[0].astype(LOW)
    d_up = jnp.einsum("brkf,brke->fe", d_pre, normed_b, preferred_element_type=FULL)
    d_normed_b = jnp.einsum("brkf,fe->brke", d_pre, up_w, preferred_element_type=FULL)
    d_mid_part, d_gain_b = jax.vjp(normalize, middle, gain_vec[:, 1])[1](d_normed_b)
    d_middle = output_gradient + d_mid_part
    d_restored = jnp.einsum(
        "brke,kq->brqe", d_middle.astype(LOW), dft_inv, preferred_element_type=FULL
    ).astype(LOW)
    sums = tuple(a + b for a, b in zip(sums, (d_up, d_down, d_dec))) if sums else (
        d_up,
        d_down,
        d_dec,
    )
    d_restored, sums = lax.optimization_barrier((d_restored, sums))
    d_fourier, given = spectral(
        lay,
        d_restored,
        plain_tab[0],
        quad_tab[1],
        ones,
        tag,
        spec_w,
        carry=carry,
        saved=spectrum,
        earlier=earlier,
    )
    d_normed_a = jnp.einsum("brqe,kq->brke", d_fourier, dft_fwd, preferred_element_type=FULL)
    d_res_part, d_gain_a = jax.vjp(normalize, residual, gain_vec[:, 0])[1](d_normed_a)
    d_gain = jnp.stack([d_gain_a, d_gain_b], axis=1)
    return d_middle + d_res_part, given, sums, d_gain


def product(left, right, dims):
    parts = []
    for value in (left, right):
        high = value.astype(LOW)
        parts.append((high, (value - high.astype(FULL)).astype(LOW)))
    (a, a_rest), (b, b_rest) = parts

    def dot(p, q):
        return lax.dot_general(p, q, (dims, ((), ())), preferred_element_type=FULL)

    return dot(a, b) + (dot(a, b_rest) + dot(a_rest, b))


def finish(lay, blocks, moments, extra, ff_dev, e_own, tag):
    places, planes, pack = blocks.shape[1:4]
    count = 2 * places * planes
    at_enc = 2 * ff_dev

    def kernel(blocks_ref, moment_ref, extra_ref, every_ref, x_ref, scalars_ref, *scratch):
        pair_got, pair, plane_got, plane, line_got, up, down, enc, dec, sent, came = scratch
        z, x, n = lay.here()
        core, y, half = n % 2, n // 2, lay.ns // 2
        place = x * half + y

        def at_core(c):
            return (z * lay.x + x, 2 * y + c)

        def at_place(p):
            return (z * lay.x + p // half, p % half * 2 + core)

        def at_plane(q):
            return (q * lay.x + x, n)

        barrier = pltpu.get_barrier_semaphore()

        def greet(target):
            pl.semaphore_signal(barrier, inc=1, device_id=target, device_id_type=MESH)

        greet(at_core(1 - core))

        @pl.loop(1, places)
        def _(step):
            greet(at_place(lax.rem(place + step, places)))

        @pl.loop(1, planes)
        def _(step):
            greet(at_plane(lax.rem(z + step, planes)))

        pl.semaphore_wait(barrier, places + planes - 1)

        def remote(source, target, at, to):
            return pltpu.make_async_remote_copy(
                src_ref=source,
                dst_ref=target,
                send_sem=sent.at[at],
                recv_sem=came.at[at],
                device_id=to,
                device_id_type=MESH,
            )

        def settle(ref, at):
            remote(ref, ref, at, at_core(1 - core)).wait()

        remote(blocks_ref.at[1 - core], pair_got, 0, at_core(1 - core)).start()
        settle(pair_got, 0)
        for p in range(places):
            pair[p] = blocks_ref[core, p] + pair_got[p]

        @pl.loop(1, places)
        def _(step):
            to = lax.rem(place + step, places)
            remote(pair.at[to], plane_got.at[place], 1, at_place(to)).start()

        plane_got[place] = pair[place]
        settle(plane_got.at[pl.ds(0, places - 1)], 1)
        for q in range(planes):
            total = plane_got[0, q]
            for p in range(1, places):
                total = total + plane_got[p, q]
            plane[q] = total

        @pl.loop(1, planes)
        def _(step):
            to = lax.rem(z + step, planes)
            remote(plane.at[to], line_got.at[z], 2, at_plane(to)).start()

        line_got[z] = plane[z]
        settle(line_got.at[pl.ds(0, planes - 1)], 2)
        total = line_got[0]
        for q in range(1, planes):
            total = total + line_got[q]
        every_ref[core, place, z] = total + extra_ref[...]

        @pl.loop(1, planes)
        def _(step):
            mine = every_ref.at[core, place, z]
            remote(mine, mine, 3, at_plane(lax.rem(z + step, planes))).start()

        settle(every_ref.at[core, place, pl.ds(0, planes - 1)], 3)

        @pl.loop(1, places)
        def _(step):
            mine = every_ref.at[core, place]
            remote(mine, mine, 4, at_place(lax.rem(place + step, places))).start()

        settle(every_ref.at[core, pl.ds(0, places - 1)], 4)
        remote(every_ref.at[core], every_ref.at[core], 5, at_core(1 - core)).start()
        settle(every_ref.at[core], 5)

        every = every_ref[...].reshape(count, pack, E)
        row = lax.broadcasted_iota(jnp.int32, (pack, E), 0)
        lane = lax.broadcasted_iota(jnp.int32, (pack, E), 1)
        enc_rows = jnp.logical_and(row >= at_enc, row < at_enc + e_own)
        added = jnp.logical_and(enc_rows, jnp.logical_or(lane == C + 2, lane == C + 3))
        squares = jnp.sum(jnp.where(added[None], 0.0, every * every), axis=0)
        owned = jnp.logical_and(row == at_enc, lane == C + 3)
        squares = squares + jnp.where(owned, jnp.sum(every, axis=0), 0.0)
        norm = jnp.sqrt(jnp.sum(squares, keepdims=True))
        clip = CLIP_NORM / jnp.maximum(norm, CLIP_NORM)
        at_lane = lax.broadcasted_iota(jnp.int32, (8, 128), 1)
        scalars_ref[...] = jnp.where(at_lane == 0, norm, clip)

        moment = MOMENTUM * moment_ref[...].reshape(count, pack, E) + clip[None] * every
        whole = ff_dev % 8 == 0 and e_own % 8 == 0

        def rows_of(begin, size):
            if whole:
                return moment[:, begin : begin + size].reshape(-1, E)
            inside = jnp.logical_and(row >= begin, row < begin + size)
            return jnp.where(inside[None], moment, 0.0).reshape(-1, E)

        both = rows_of(at_enc, e_own)
        near = lax.broadcasted_iota(jnp.int32, (both.shape[0], 128), 1) < C
        starts = [rows_of(0, ff_dev), rows_of(ff_dev, ff_dev)]
        starts += [jnp.where(near, both[:, :128], 0.0), both[:, 128:]]
        for start, out in zip(starts, (up, down, enc, dec)):
            square = jnp.sum(start * start, keepdims=True)
            out[...] = start / (jnp.sqrt(square) + 1e-07)

        @pl.loop(0, NS_ITERS)
        def _(sweep):
            for out in (up, down, enc, dec):
                matrix = out[...]
                gram_mat = product(matrix, matrix, ((0,), (0,)))
                square = product(gram_mat, gram_mat, ((1,), (0,)))
                poly = NS_SECOND * gram_mat + NS_THIRD * square
                out[...] = NS_FIRST * matrix + product(matrix, poly, ((1,), (0,)))

        both = jnp.concatenate([enc[...], dec[...]], axis=1)
        shape = (2, places, planes)
        if whole:
            x_ref[:, :, :, :ff_dev] = up[...].reshape(shape + (ff_dev, E))
            x_ref[:, :, :, ff_dev:at_enc] = down[...].reshape(shape + (ff_dev, E))
            x_ref[:, :, :, at_enc : at_enc + e_own] = both.reshape(shape + (e_own, E))
        else:
            x_ref[...] = (up[...] + down[...] + both).reshape(shape + (pack, E))

    whole = ff_dev % 8 == 0 and e_own % 8 == 0
    tall = FF if whole else count * pack
    small = E if whole else count * pack
    fast = pl.BlockSpec(memory_space=pltpu.VMEM)
    return pl.pallas_call(
        kernel,
        out_shape=[
            jax.ShapeDtypeStruct(blocks.shape, FULL),
            jax.ShapeDtypeStruct(blocks.shape, FULL),
            jax.ShapeDtypeStruct((8, 128), FULL),
        ],
        in_specs=[fast] * 3,
        out_specs=[fast] * 3,
        scratch_shapes=[
            pltpu.VMEM(blocks.shape[1:], FULL),
            pltpu.VMEM(blocks.shape[1:], FULL),
            pltpu.VMEM(blocks.shape[1:], FULL),
            pltpu.VMEM(blocks.shape[2:], FULL),
            pltpu.VMEM(blocks.shape[2:], FULL),
            pltpu.VMEM((tall, E), FULL),
            pltpu.VMEM((tall, E), FULL),
            pltpu.VMEM((small, 128), FULL),
            pltpu.VMEM((small, 128), FULL),
            pltpu.SemaphoreType.DMA((6,)),
            pltpu.SemaphoreType.DMA((6,)),
        ],
        compiler_params=pltpu.CompilerParams(
            collective_id=tag, has_side_effects=True, vmem_limit_bytes=56 << 20
        ),
        name="finish",
    )(blocks, moments, extra)


def natural(values):
    order = tuple(range(values.ndim))
    return with_layout_constraint(values, DeviceLayout(major_to_minor=order))


def adam_step(weight, moment_a, moment_b, gradient, step_rate):
    moment_a = BETA_FIRST * moment_a + (1.0 - BETA_FIRST) * gradient
    moment_b = BETA_SECOND * moment_b + (1.0 - BETA_SECOND) * gradient * gradient
    corrected_a = moment_a / (1.0 - BETA_FIRST**STEP)
    corrected_b = moment_b / (1.0 - BETA_SECOND**STEP)
    return (
        moment_a,
        moment_b,
        weight - step_rate * (corrected_a / (jnp.sqrt(corrected_b) + 1e-08) + DECAY * weight),
    )


def local(
    fields,
    targets,
    valid,
    var_class,
    enc_t,
    enc_mom,
    dec,
    dec_mom,
    spec,
    spec_m,
    spec_v,
    up_t,
    up_mom,
    down,
    down_mom,
    gains,
    gain_m,
    gain_v,
):
    dp_count, ns_count = lax.axis_size("dp"), lax.axis_size("ns")
    devices = dp_count * ns_count
    lay = Layout(dp_count, ns_count, fields.shape[0], fields.shape[1])
    z, x, n = lay.here()
    member = lay.fore(n) * lay.x + x
    lat_count = lay.rows * dp_count

    ff_dev, e_own = up_t.shape[1], E // devices
    pack = -(-(2 * ff_dev + 2 * e_own) // 16) * 16

    def mine(values):
        return lax.dynamic_slice_in_dim(values, n * e_own, e_own, 0)

    def packed(up, down_, enc, dec_, extra):
        both = jnp.concatenate([wide(mine(enc)), wide(mine(dec_))], axis=1)
        return pad_rows(jnp.concatenate([up[0], down_[0], both, extra], axis=0), pack)

    def unpacked(every):
        up = every[:, :ff_dev].reshape(FF, E)
        down_ = every[:, ff_dev : 2 * ff_dev].reshape(FF, E)
        both = every[:, 2 * ff_dev : 2 * ff_dev + e_own].reshape(E, E)
        extra = every[:, 2 * ff_dev + e_own : 2 * ff_dev + 2 * e_own]
        return up, down_, both[:, :128], both[:, 128:], extra

    gain_rows = jnp.pad(mine(gains[0]), ((0, 0), (0, E - 2)))
    small = packed(up_t, down, enc_t, dec, gain_rows).astype(LOW)
    lon_count = fields.shape[2]
    lon_pad = ((0, 0),) * 3 + ((0, -lon_count % 128),)

    def dense(values):
        return jnp.pad(values.transpose(1, 3, 0, 2), lon_pad)

    def usual(values):
        return values[..., :lon_count].transpose(2, 0, 3, 1)

    swaps = [dense(fields), dense(valid[..., None])]
    spec_got, every_low, swaps = prologue(lay, spec_out(lay, spec[0]), small, swaps, 0)
    fields, valid = usual(swaps[0]), usual(swaps[1])[..., 0]
    targets = [dense(targets[step]) for step in range(2)]
    up_w, down_w, enc_w, dec_w, extra = unpacked(every_low)
    enc_w, dec_w = enc_w[:, :C], dec_w[:, :C]
    gain_w = extra.reshape(E, E)[:, :2]
    spec_w = spec_in(lay, spec_got)

    colatitude = math.pi * (np.arange(lat_count) + 0.5) / lat_count
    sines = jnp.asarray(np.sin(colatitude).astype(np.float32).reshape(dp_count, lay.rows))
    local_sine = lax.dynamic_index_in_dim(sines, member, keepdims=False)
    var_weight = 1.0 + 0.5 * var_class.astype(FULL)
    pixel_map = valid.astype(FULL) * local_sine[None, :, None]
    weight_part = jnp.sum(pixel_map)
    weight_map = pixel_map[..., None] * var_weight
    weight_rows = jnp.broadcast_to(weight_part, (e_own, E))
    every_mom = lax.all_gather(packed(up_mom, down_mom, enc_mom, dec_mom, weight_rows), BOTH)
    loss_weight = jnp.sum(every_mom[:, 2 * ff_dev + e_own, 0]) * jnp.sum(var_weight)
    core_pack = -(-(2 * ff_dev + e_own) // 8) * 8

    def by_core(values):
        values = values.reshape((ns_count, lay.x, ns_count // 2, 2) + values.shape[1:])
        values = jnp.moveaxis(values, (3, 1, 2, 0), (0, 1, 2, 3))
        return values.reshape((2, dp_count // 2, ns_count) + values.shape[4:])

    def by_device(values):
        values = values.reshape((2, lay.x, ns_count // 2, ns_count) + values.shape[3:])
        values = jnp.moveaxis(values, (3, 1, 2, 0), (0, 1, 2, 3))
        return values.reshape((devices,) + values.shape[4:])

    moments = by_core(pad_rows(every_mom[:, : 2 * ff_dev + e_own], core_pack))

    tables = dft_tables(lay, fields.shape[2]) + legendre_tables(lay, lat_count)
    incoming = fields
    saved = []
    forecasts = []
    for step in range(2):
        weights = (spec_w, up_w, down_w, gain_w)
        hidden = jnp.einsum("brkc,ec->brke", incoming, enc_w, preferred_element_type=FULL)
        fetch, carry = ((True,), ()) if step == 0 else ((), (targets[1],))
        hidden, kept, given = forward_block(lay, hidden, weights, tables, 1 + step, fetch, carry)
        if step == 0:
            (spec_w,) = given["whole"]
        else:
            targets[1] = usual(given["carried"][0])
        closing = hidden.astype(LOW)
        forecast = jnp.einsum("brke,ec->brkc", closing, dec_w, preferred_element_type=FULL)
        saved.append((incoming, kept, closing))
        forecasts.append(forecast)
        incoming = forecast.astype(LOW)

    def loss_of(step):
        error = forecasts[step] - targets[step].astype(FULL)
        return jnp.sum(weight_map * error * error), 2.0 * weight_map * error / loss_weight

    last_loss, gradient = loss_of(1)
    early, d_spec = (), ()
    carry = (targets[0],)
    for step in (1, 0):
        incoming, kept, closing = saved[step]
        low_grad = gradient.astype(LOW)
        d_dec = jnp.einsum("brke,brkc->ec", closing, low_grad, preferred_element_type=FULL)
        gradient = jnp.einsum("brkc,ec->brke", low_grad, dec_w, preferred_element_type=FULL)
        gradient, given, early, d_gain = backward_block(
            lay, gradient, kept, weights, tables, 4 - step, d_spec, carry, early, d_dec
        )
        d_spec, carry = given["d"] + given["g"], ()
        low_grad = gradient.astype(LOW)
        d_enc = jnp.einsum("brkc,brke->ec", incoming, low_grad, preferred_element_type=FULL)
        if step == 1:
            late = (d_gain, d_enc)
            targets[0] = usual(given["carried"][0])
            first_loss, gradient = loss_of(0)
            gradient = gradient + jnp.einsum(
                "brke,ec->brkc", low_grad, enc_w, preferred_element_type=FULL
            )
            loss_local = first_loss + last_loss
    d_gain, d_enc = late[0] + d_gain, late[1] + d_enc
    d_up, d_down, d_dec = early
    g_spec = natural(spec_home(lay, d_spec[0], 5)[None])
    near = jnp.concatenate([d_enc, d_gain, jnp.broadcast_to(loss_local, (E, 1))], axis=1)
    both = jnp.concatenate([wide(near), wide(d_dec)], axis=1).reshape(devices, e_own, E)
    blocks = [d_up.reshape(devices, ff_dev, E), d_down.reshape(devices, ff_dev, E), both]
    blocks = by_core(pad_rows(jnp.concatenate(blocks, axis=1), core_pack))
    at_row = jnp.arange(core_pack)[:, None] == 2 * ff_dev
    at_lane = at_row & (jnp.arange(E)[None, :] == C + 3)
    extra = jnp.where(at_lane, jnp.sum(g_spec * g_spec), 0.0)
    every, matrices, scalars = finish(lay, blocks, moments, extra, ff_dev, e_own, 6)
    grad_norm, clip_scale = scalars[0, 0], scalars[0, 1]
    d = lax.axis_index("dp")
    place = x * (ns_count // 2) + n // 2
    at_enc = 2 * ff_dev

    def own_block(values):
        return values[n % 2, place, z]

    def enc_block(values):
        both = by_device(values[:, :, :, at_enc : at_enc + e_own]).reshape(dp_count, lay.e_dev, E)
        return lax.dynamic_index_in_dim(both, d, keepdims=False)

    loss_sum = every[0, 0, 0, at_enc, C + 2]
    own_grad, own_step = own_block(every), own_block(matrices)
    enc_grad, enc_step = enc_block(every), enc_block(matrices)
    factors = [math.sqrt(max(1.0, FF / E))] * 2 + [math.sqrt(max(1.0, E / C))] * 2

    def muon(master, moment, gradient, matrix, factor):
        moment = MOMENTUM * moment + clip_scale * gradient.reshape(master.shape)
        step = RATE_MUON * (matrix.reshape(master.shape) * factor)
        return moment, master * (1.0 - RATE_MUON * DECAY) - step

    up, down_at = slice(0, ff_dev), slice(ff_dev, 2 * ff_dev)
    up_mom_new, up_new = muon(up_t, up_mom, own_grad[up], own_step[up], factors[0])
    down_mom_new, down_new = muon(
        down, down_mom, own_grad[down_at], own_step[down_at], factors[1]
    )
    enc_mom_new, enc_new = muon(enc_t, enc_mom, enc_grad[:, :C], enc_step[:, :C], factors[2])
    dec_at = slice(128, 128 + C)
    dec_mom_new, dec_new = muon(
        dec, dec_mom, enc_grad[:, dec_at], enc_step[:, dec_at], factors[3]
    )
    g_gain_own = enc_grad[:, C : C + 2][None]
    spec_m_new, spec_v_new, spec_new = adam_step(
        spec, spec_m, spec_v, clip_scale * g_spec, RATE_SPECTRAL
    )
    gain_m_new, gain_v_new, gain_new = adam_step(
        gains, gain_m, gain_v, clip_scale * g_gain_own, RATE_GAIN
    )
    return (
        loss_sum,
        loss_weight,
        grad_norm,
        enc_mom_new,
        enc_new,
        dec_mom_new,
        dec_new,
        up_mom_new,
        up_new,
        down_mom_new,
        down_new,
        spec_m_new,
        spec_v_new,
        spec_new,
        spec_new.astype(LOW),
        gain_m_new,
        gain_v_new,
        gain_new,
    )


def solution(mesh):
    rows = P(None, BOTH, None)
    shard = P("dp", None)
    whole = P(None, "dp", "ns", None, None)
    gain = P(None, "dp", None)
    placed = (
        P("ns", "dp", None, None),
        P(None, "ns", "dp", None, None),
        P("ns", "dp", None),
        P(),
        *[shard] * 4,
        *[whole] * 3,
        *[rows] * 4,
        *[gain] * 3,
    )
    return jax.shard_map(
        local,
        mesh=mesh,
        in_specs=placed,
        out_specs=(P(), P(), P(), *[shard] * 4, *[rows] * 4, *[whole] * 4, *[gain] * 3),
        check_vma=False,
    )
```

```python
import math

import jax
import jax.numpy as jnp
import ml_dtypes
import numpy as np
from jax import lax
from jax.experimental import pallas as pl
from jax.experimental.layout import Layout as DeviceLayout
from jax.experimental.layout import with_layout_constraint
from jax.experimental.pallas import tpu as pltpu
from jax.sharding import PartitionSpec as P

E = 256
FF = 512
C = 73
LDEG = 96
MM = 96
NL = 1
NS_ITERS = 5
STEP = 10

EXACT = lax.Precision.HIGHEST
EPSILON = 1e-06
CLIP_NORM = 0.02
RATE_SPECTRAL = 0.05
RATE_GAIN = 0.1
RATE_MUON = 0.5
BETA_FIRST = 0.9
BETA_SECOND = 0.999
MOMENTUM = 0.95
DECAY = 0.01
NS_FIRST = 3.4445
NS_SECOND = -4.775
NS_THIRD = 2.0315
LOW = jnp.bfloat16
FULL = jnp.float32
MESH = pl.DeviceIdType.MESH
CHUNK = 16
BOTH = ("dp", "ns")


class Layout:
    def __init__(self, dp, ns, items, rows):
        self.dp, self.ns = dp, ns
        self.x, self.half, self.g = dp // ns, ns // 2, dp // 2
        self.block_rows, self.rows = rows, 2 * rows
        self.kper, self.lper, self.lns = MM // self.g, LDEG // dp, LDEG // ns
        self.kb = 8
        self.kd = self.kb * self.g // dp
        self.nkb = -(-self.kper // self.kb)
        self.blocks = [[i for i in range(self.lper) if i >= k * self.kd] for k in range(self.nkb)]
        self.counts = [len(b) for b in self.blocks]
        self.starts = np.cumsum([0] + self.counts).tolist()
        self.size = 2 * self.kb
        self.cols = self.rows * self.size
        self.ends = [min((k + 1) * self.kd, self.lper) for k in range(self.nkb)]
        self.ends[-1] = self.lper
        self.slots = -(-self.lns // dp)
        self.even = self.lns % dp == 0
        self.e_dev = E // dp
        self.e_plane = self.x * self.e_dev

    def here(self):
        d, n = lax.axis_index("dp"), lax.axis_index("ns")
        return d // self.x, d % self.x, n

    def row_blocks(self, n, x):
        return [(2 * (n % self.half) + s) * self.x + x for s in (0, 1)]

    def item_goes(self, at):
        z, x, n = self.here()
        plane = 2 * (n % self.half) + at
        to = n // self.half * self.half + z // 2
        return (plane * self.x + x, to), jnp.logical_and(plane == z, to == n)

    def item_comes(self, slot):
        z, x, n = self.here()
        return ((2 * (n % self.half) + slot) * self.x + x, n // self.half * self.half + z // 2)

    def stays(self):
        z, x, n = self.here()
        return z // 2 == n % self.half


def group_of(lay, kind):
    z, x, n = lay.here()
    if kind == "plane":
        return lay.dp, n * lay.x + x, lambda p: (z * lay.x + p % lay.x, p // lay.x)
    if kind == "half":
        first = n // lay.half * lay.half
        return (
            lay.g,
            n % lay.half * lay.x + x,
            lambda q: (z * lay.x + q % lay.x, first + q // lay.x),
        )
    return lay.ns, z, lambda q: (q * lay.x + x, n)


def exchange(lay, arrays, kinds, group, tag):
    count = {"plane": lay.dp, "line": lay.ns}[group]

    def kernel(*refs):
        total = len(arrays)
        ins, outs = refs[:total], refs[total : 2 * total]
        send, recv, own = refs[2 * total :]
        size, me, device = group_of(lay, group)
        barrier = pltpu.get_barrier_semaphore()

        @pl.loop(1, size)
        def _(step):
            pl.semaphore_signal(
                barrier, inc=1, device_id=device(lax.rem(me + step, size)), device_id_type=MESH
            )

        pl.semaphore_wait(barrier, size - 1)

        @pl.loop(1, size)
        def _(step):
            peer = lax.rem(me + step, size)
            for at in range(total):
                pltpu.make_async_remote_copy(
                    src_ref=ins[at].at[peer] if kinds[at] == "each" else ins[at],
                    dst_ref=outs[at].at[me],
                    send_sem=send.at[at],
                    recv_sem=recv.at[at],
                    device_id=device(peer),
                    device_id_type=MESH,
                ).start()

        for at in range(total):
            mine = ins[at].at[me] if kinds[at] == "each" else ins[at]
            copy = pltpu.make_async_copy(mine, outs[at].at[me], own)
            copy.start()
            copy.wait()
        for at in range(total):
            some = outs[at].at[pl.ds(0, size - 1)]
            pltpu.make_async_remote_copy(
                src_ref=some,
                dst_ref=some,
                send_sem=send.at[at],
                recv_sem=recv.at[at],
                device_id=device(lax.rem(me + 1, size)),
                device_id_type=MESH,
            ).wait()

    shapes = [
        jax.ShapeDtypeStruct(a.shape if k == "each" else (count,) + a.shape, a.dtype)
        for a, k in zip(arrays, kinds)
    ]
    spot = pl.BlockSpec(memory_space=pl.ANY)
    return pl.pallas_call(
        kernel,
        out_shape=shapes,
        in_specs=[spot] * len(arrays),
        out_specs=[spot] * len(arrays),
        scratch_shapes=[
            pltpu.SemaphoreType.DMA((len(arrays),)),
            pltpu.SemaphoreType.DMA((len(arrays),)),
            pltpu.SemaphoreType.DMA,
        ],
        compiler_params=pltpu.CompilerParams(collective_id=tag, has_side_effects=True),
        name=f"exchange_{group}_{tag}",
    )(*arrays)


def legendre(lat_count):
    colatitude = math.pi * (np.arange(lat_count) + 0.5) / lat_count
    cosine, log_sine = np.cos(colatitude)[None, :], np.log(np.sin(colatitude))[None, :]
    orders = np.arange(MM, dtype=np.float64)
    ladder = np.arange(1, MM, dtype=np.float64)
    sums = np.concatenate([[0.0], np.cumsum(np.log((2 * ladder - 1) / (2 * ladder)))])
    diagonal = np.exp(
        (0.5 * np.log((2 * orders + 1) / (4 * math.pi)) + 0.5 * sums)[:, None]
        + orders[:, None] * log_sine
    )
    table = np.zeros((LDEG, MM, lat_count))
    for degree in range(LDEG):
        for order in range(min(degree, MM - 1) + 1):
            if degree == order:
                table[degree, order] = diagonal[order]
                continue
            a = math.sqrt((4.0 * degree**2 - 1) / (degree**2 - order**2))
            value = cosine[0] * table[degree - 1, order]
            if degree >= 2:
                b = math.sqrt(
                    max((degree - 1.0) ** 2 - order**2, 0) / (4 * (degree - 1.0) ** 2 - 1)
                )
                value = value - b * table[degree - 2, order]
            table[degree, order] = a * value
    return table.astype(np.float32)


def low_table(values):
    return values.astype(np.float32).astype(ml_dtypes.bfloat16)


def dft_tables(lay, lon_count):
    turns = np.arange(lon_count)[:, None] * np.arange(MM)[None, :] % lon_count
    phases = 2 * math.pi / lon_count * turns
    paired = np.stack([np.cos(phases), -np.sin(phases)], axis=2)
    weight = np.where(np.arange(MM) == 0, 1.0, 2.0)
    forward = paired * (2 * math.pi / lon_count)
    inverse = paired * weight[None, :, None] / (2 * math.pi)

    def order(table):
        table = table.reshape(lon_count, lay.kper, lay.g, 2).transpose(0, 2, 1, 3)
        pad = lay.nkb * lay.kb - lay.kper
        table = np.pad(table, ((0, 0), (0, 0), (0, pad), (0, 0)))
        return low_table(table.reshape(lon_count, -1))

    return order(forward), order(inverse)


def legendre_tables(lay, lat_count):
    plain = legendre(lat_count)
    colatitude = math.pi * (np.arange(lat_count) + 0.5) / lat_count
    quadrature = 2 * math.pi * math.pi / lat_count * np.sin(colatitude)
    pad = lay.nkb * lay.kb - lay.kper

    def own(table):
        table = table.reshape(lay.lper, lay.dp, lay.kper, lay.g, lat_count)
        table = np.pad(table.transpose(3, 1, 0, 2, 4), ((0, 0), (0, 0), (0, 0), (0, pad), (0, 0)))
        table = low_table(table)
        blocks = []
        for k in range(lay.nkb):
            part = table[:, :, k * lay.kd :, k * lay.kb : (k + 1) * lay.kb]
            blocks.append(part.reshape(lay.g, -1, lay.kb * lat_count))
        across = [jnp.asarray(np.ascontiguousarray(b.swapaxes(1, 2))) for b in blocks]
        return jnp.asarray(np.concatenate(blocks, axis=1)), across

    col = np.arange(lay.g * lay.cols)
    col_part, col_k = col % 2, col // 2 % lay.kb
    member, row = col // lay.cols, col // lay.size % lay.rows
    block = (2 * (member // lay.x) + row // lay.block_rows) * lay.x + member % lay.x
    col_lat = block * lay.block_rows + row % lay.block_rows
    col_kind = col_part * lay.kb + col_k
    pick = col_k * lat_count + col_lat
    spread = np.arange(lay.kb * lat_count)[:, None] == pick[None, :]
    same = np.arange(lay.size)[:, None] == col_kind[None, :]
    wide_same = np.tile(same.T, (1, CHUNK))
    count = lay.dp * lay.lper
    repeat = np.arange(CHUNK * lay.size)[:, None] // lay.size == np.arange(CHUNK)[None, :]
    across = np.arange(count)[:, None] == np.arange(count * lay.size)[None, :] // lay.size
    ones = [
        jnp.asarray(v.astype(ml_dtypes.bfloat16))
        for v in (spread, spread.T, same, wide_same, repeat, across)
    ]
    return own(plain * quadrature.astype(np.float32)[None, None, :]), own(plain), ones


def normalize(values, gain_vec):
    return (
        values * lax.rsqrt(jnp.mean(values * values, axis=-1, keepdims=True) + EPSILON) * gain_vec
    )


def greet_senders(lay, greet):
    z, _, _ = lay.here()
    for slot in (0, 1):

        @pl.when(jnp.logical_not(jnp.logical_and(lay.stays(), z % 2 == slot)))
        def _():
            greet(lay.item_comes(slot))


class Swap:
    def __init__(self, lay, gone, come, sems):
        z, _, _ = lay.here()
        slot = z % 2
        self.here = [lay.item_goes(at)[1] for at in (0, 1)]
        self.far = [
            pltpu.make_async_remote_copy(
                src_ref=gone.at[at],
                dst_ref=come.at[slot],
                send_sem=sems[0],
                recv_sem=sems[1],
                device_id=lay.item_goes(at)[0],
                device_id_type=MESH,
            )
            for at in (0, 1)
        ]
        self.near = [
            pltpu.make_async_copy(gone.at[at], come.at[slot], sems[2]) for at in (0, 1)
        ]
        whole, one = come, come.at[0]
        self.stays = lay.stays()
        self.all_far, self.one_far = [
            pltpu.make_async_remote_copy(
                src_ref=ref,
                dst_ref=ref,
                send_sem=sems[0],
                recv_sem=sems[1],
                device_id=lay.item_goes(0)[0],
                device_id_type=MESH,
            )
            for ref in (whole, one)
        ]

    def start(self):
        for here, far, near in zip(self.here, self.far, self.near):

            @pl.when(here)
            def _():
                near.start()

            @pl.when(jnp.logical_not(here))
            def _():
                far.start()

    def wait(self):
        @pl.when(self.stays)
        def _():
            self.one_far.wait()
            self.near[0].wait()

        @pl.when(jnp.logical_not(self.stays))
        def _():
            self.all_far.wait()


def turned(real, imag):
    both = jnp.concatenate([real[:, None], imag[:, None]], axis=1)
    return both.reshape(-1, E).astype(LOW)


def parts_of(values):
    split = values.reshape(-1, 2, 8, E)
    return split[:, 0], split[:, 1]


def spectral(lay, values, first, second, ones, tag, spec_w, fetch=(), carry=(), saved=(), earlier=()):
    back, last = bool(saved), bool(earlier)
    nkb, dp, ns, size, half = lay.nkb, lay.dp, lay.ns, lay.size, lay.g
    counts, ends, lper = lay.counts, lay.ends, lay.lper
    items, rows = values.shape[:2]
    laid = values.reshape(items, rows, half, nkb, size, E)
    laid = laid.transpose(2, 3, 0, 1, 4, 5).reshape(half, nkb, lay.cols, E)
    w_shape = (ns, lper, 2, lay.e_plane, E)
    dma = pltpu.SemaphoreType.DMA
    tiles = [(dp, c, size, E) for c in counts]
    spans = [(g * lay.kd, ends[g] - g * lay.kd) for g in range(nkb)]

    ins = {"f": [laid], "p1": [first], "p2": list(second), "ones": list(ones), "w": [spec_w]}
    ins |= {"old": list(saved), "earlier": list(earlier), "carry": list(carry)}
    outs = {"y": [((half, nkb, lay.cols, E), LOW)]}
    outs["keep"] = [] if back else [(t, LOW) for t in tiles]
    outs["whole"] = [(w_shape, LOW)] if fetch else []
    outs["d"] = [(w_shape, LOW)] if back and not last else []
    owned = (dp, lay.slots, 2, lay.e_dev, E) if lay.even else (lper, lay.x, 2, lay.e_dev, E)
    outs["g"] = [(owned, FULL)] if last else []
    outs["carried"] = [(c.shape, c.dtype) for c in carry]
    tall, broad = lay.size * dp * np.array(counts), half * lay.cols
    buffers = {
        "f_got": [((nkb, half, lay.cols, E), LOW)],
        "t1": [((int(h), broad), LOW) for h in tall],
        "t2": [((broad, int(h)), LOW) for h in tall],
        "p1_v": [(first.shape[1:], LOW)],
        "p2_v": [(p.shape[1:], LOW) for p in second],
        "ones_v": [(o.shape, LOW) for o in ones],
        "w_v": [(w_shape, LOW)],
        "s_put": [(t, LOW) for t in tiles],
        "s_got": [(t, LOW) for t in tiles],
        "m_put": [(t, LOW) for t in tiles],
        "m_got": [(t, LOW) for t in tiles],
        "y_put": [((half, nkb, lay.cols, E), LOW)],
        "old_v": [(t, LOW) for t in tiles] if back else [],
        "early_v": [(w_shape, LOW)] if last else [],
        "d_put": [(w_shape, LOW)] if back else [],
        "d_got": [(w_shape, LOW)] if last else [],
        "g_put": [((lper, lay.x, 2, lay.e_dev, E), FULL)] if last else [],
    }
    sems = {"f_sem": nkb, "s_sem": nkb, "m_sem": nkb, "y_sem": 1, "send": 4, "own": nkb + 4}
    sems |= {"load": 2 + len(second) + len(ones) + len(saved) + 1}
    sems |= {"line_send": 1, "line_got": 2 * (ns - 1) * nkb, "carry_sem": 4, "g_sem": 2}

    def kernel(*refs):
        refs = list(refs)
        r = {}
        for group in (ins, outs, buffers):
            for name, entries in group.items():
                r[name] = refs[: len(entries)]
                del refs[: len(entries)]
        for name in sems:
            r[name] = refs.pop(0)
        (f_ref,), (y_ref,), (f_got,), (y_put,), (w,) = (
            r[k] for k in ("f", "y", "f_got", "y_put", "w_v")
        )
        t1, t2, s_put, s_got, m_put, m_got = (
            r[k] for k in ("t1", "t2", "s_put", "s_got", "m_put", "m_got")
        )
        spread, spread_t, same, wide_same, repeat, across = r["ones_v"]
        send, own = r["send"], r["own"]
        z, x, n = lay.here()
        _, me, device = group_of(lay, "plane")
        _, mine_at, half_device = group_of(lay, "half")
        _, _, line_device = group_of(lay, "line")
        line = bool(fetch) or last
        barrier = pltpu.get_barrier_semaphore()

        def greet(target):
            pl.semaphore_signal(barrier, inc=1, device_id=target, device_id_type=MESH)

        @pl.loop(1, dp)
        def _(step):
            greet(device(lax.rem(me + step, dp)))

        if line:

            @pl.loop(1, ns)
            def _(step):
                greet(line_device(lax.rem(z + step, ns)))

        if carry:
            greet_senders(lay, greet)
        pairs = [(r["p1"][0].at[mine_at], r["p1_v"][0])]
        pairs += [(a, b) for a, b in zip(r["ones"], r["ones_v"])]
        pairs += [(a.at[mine_at], b) for a, b in zip(r["p2"], r["p2_v"])]
        tables_at = len(pairs)
        if not fetch:
            pairs += [(r["w"][0], w)]
        else:
            pairs += [(r["w"][0], w.at[z])]
        pairs += list(zip(r["old"], r["old_v"])) + list(zip(r["earlier"], r["early_v"]))
        loads = []
        for at, (source, target) in enumerate(pairs):
            copy = pltpu.make_async_copy(source, target, r["load"].at[at])
            copy.start()
            loads.append(copy)
        mine = []
        for k in range(nkb):
            copy = pltpu.make_async_copy(f_ref.at[mine_at, k], f_got.at[k, mine_at], own.at[k])
            copy.start()
            mine.append(copy)
        waits = dp - 1 + (ns - 1 if line else 0)
        if carry:
            pl.semaphore_wait(barrier, waits + jnp.where(lay.stays(), 1, 2))
        else:
            pl.semaphore_wait(barrier, waits)

        def remote(source, target, sent, got, to):
            return pltpu.make_async_remote_copy(
                src_ref=source,
                dst_ref=target,
                send_sem=sent,
                recv_sem=got,
                device_id=to,
                device_id_type=MESH,
            )

        def push(source, target, sent, got, peer):
            remote(source, target, sent, got, device(peer)).start()

        def settle(ref, sent, got, sending):
            copy = remote(ref, ref, sent, got, device(lax.rem(me + 1, dp)))
            if sending:
                copy.wait_send()
            else:
                copy.wait_recv()

        for k in range(nkb):

            @pl.loop(1, half)
            def _(step):
                peer = lax.rem(mine_at + step, half)
                target = f_got.at[k, mine_at]
                sem = r["f_sem"].at[k]
                remote(f_ref.at[peer, k], target, send.at[0], sem, half_device(peer)).start()

        lines = [(sign, at * (ns - 1) * nkb) for at, sign in enumerate((1, -1))]

        def inside(at):
            return jnp.logical_and(at >= 0, at < ns)

        def line_wait(distance, g):
            for sign, at in lines:

                @pl.when(inside(z - sign * distance))
                def _():
                    some = w.at[0, pl.ds(*spans[g])]
                    sem = r["line_got"].at[at + (distance - 1) * nkb + g]
                    remote(some, some, r["line_send"].at[0], sem, device(me)).wait_recv()

        def line_push(distance):
            for g, (begin, length) in enumerate(spans):
                span = pl.ds(begin, length)
                if distance > 1:
                    line_wait(distance - 1, g)
                for sign, at in lines:
                    source = z - sign * (distance - 1)

                    @pl.when(jnp.logical_and(inside(z + sign), inside(source)))
                    def _():
                        remote(
                            r["w"][0].at[span] if distance == 1 else w.at[source, span],
                            w.at[source, span],
                            r["line_send"].at[0],
                            r["line_got"].at[at + (distance - 1) * nkb + g],
                            line_device(z + sign),
                        ).start()

        if fetch:
            line_push(1)

        if carry:
            (gone,), (come,) = r["carry"], r["carried"]
            swap = Swap(lay, gone, come, [r["carry_sem"].at[at] for at in range(4)])
            swap.start()

        for at in range(tables_at):
            loads[at].wait()
        for k in range(nkb):

            @pl.loop(0, dp * counts[k] // CHUNK)
            def _(chunk):
                at = pl.multiple_of(dp * lay.starts[k] + chunk * CHUNK, CHUNK)
                part = r["p1_v"][0][pl.ds(at, CHUNK), :]
                part = jnp.dot(repeat[...], part, preferred_element_type=FULL).astype(LOW)
                full = jnp.dot(part, spread[...], preferred_element_type=FULL)
                full = full.reshape(CHUNK, size, broad) * same[...].astype(FULL)[None]
                to = pl.multiple_of(chunk * CHUNK * size, CHUNK * size)
                t1[k][pl.ds(to, CHUNK * size), :] = full.reshape(CHUNK * size, broad).astype(LOW)

        for k in range(nkb):
            mine[k].wait()
            settle(f_got.at[k, pl.ds(0, half - 1)], send.at[0], r["f_sem"].at[k], False)
            high = counts[k] * size

            def modes_for(peer):
                part = t1[k][pl.ds(pl.multiple_of(peer * high, 16), high), :]
                got = f_got[k].reshape(half * lay.cols, E)
                out = jnp.dot(part, got, preferred_element_type=FULL).astype(LOW)
                return out.reshape(counts[k], size, E)

            @pl.loop(1, dp)
            def _(step):
                peer = lax.rem(me + step, dp)
                s_put[k][peer] = modes_for(peer)
                push(s_put[k].at[peer], s_got[k].at[me], send.at[1], r["s_sem"].at[k], peer)

            s_got[k][me] = modes_for(me)

        if fetch:
            line_push(2)
        for k in range(nkb):
            width = CHUNK * size
            count = dp * counts[k]

            @pl.loop(0, count // CHUNK)
            def _(chunk):
                to = pl.ds(pl.multiple_of(chunk * width, width), width)
                part = jnp.dot(
                    r["p2_v"][k][...], across[pl.ds(0, count), to], preferred_element_type=FULL
                )
                full = jnp.dot(spread_t[...], part.astype(LOW), preferred_element_type=FULL)
                t2[k][:, to] = (full * wide_same[...].astype(FULL)).astype(LOW)

        if fetch:
            for distance in range(3, ns):
                line_push(distance)

        for copy in loads[tables_at:]:
            copy.wait()
        for g, (begin, length) in enumerate(spans):
            settle(s_got[g].at[pl.ds(0, dp - 1)], send.at[1], r["s_sem"].at[g], False)
            span = pl.ds(begin, length)
            if fetch:
                line_wait(ns - 1, g)

            def rows_at(group, degree):
                tiles = [group[k][:, degree - k * lay.kd] for k in range(g + 1)]
                return jnp.concatenate([t.reshape(dp * size, E) for t in tiles], axis=0)

            @pl.loop(begin, ends[g])
            def _(degree):
                rows_in = rows_at(s_got, degree)
                dims = (((1,), (1 if back else 0,)), ((), ()))
                by_real, by_imag = (
                    lax.dot_general(
                        rows_in, w[:, degree, p].reshape(E, E), dims, preferred_element_type=FULL
                    )
                    for p in (0, 1)
                )
                (rr, ir), (ri, ii) = parts_of(by_real), parts_of(by_imag)
                mixed = turned(rr + ii, ir - ri) if back else turned(rr - ii, ri + ir)
                for k in range(g + 1):
                    part = mixed[k * dp * size : (k + 1) * dp * size]
                    m_put[k][:, degree - k * lay.kd] = part.reshape(dp, size, E)

            for k in range(g + 1):
                there = pl.ds(begin - k * lay.kd, length)

                @pl.loop(1, dp)
                def _(step):
                    peer = lax.rem(me + step, dp)
                    target = m_got[k].at[me, there]
                    push(m_put[k].at[peer, there], target, send.at[2], r["m_sem"].at[k], peer)

            if back:
                (d_put,) = r["d_put"]

                @pl.loop(begin, ends[g])
                def _(degree):
                    dims = (((0,), (0,)), ((), ()))
                    olds, grads = rows_at(r["old_v"], degree), rows_at(s_got, degree)
                    real, imag = parts_of(grads.astype(FULL))
                    for p, right in ((0, grads), (1, turned(imag, -real))):
                        total = lax.dot_general(olds, right, dims, preferred_element_type=FULL)
                        total = total.reshape(ns, lay.e_plane, E)
                        if last:
                            total = total + r["early_v"][0][:, degree, p].astype(FULL)
                        d_put[:, degree, p] = total.astype(LOW)

                if last:
                    (d_got,) = r["d_got"]

                    @pl.loop(1, ns)
                    def _(step):
                        to = lax.rem(z + step, ns)
                        remote(
                            d_put.at[to, span],
                            d_got.at[z, span],
                            r["line_send"].at[0],
                            r["line_got"].at[g],
                            line_device(to),
                        ).start()

        for k in range(nkb):
            m_got[k][me] = m_put[k][me]
        keeps = []
        for at, (source, target) in enumerate(
            list(zip(s_got, r["keep"])) + [(w, t) for t in r["whole"]] + list(zip(r["d_put"], r["d"]))
        ):
            copy = pltpu.make_async_copy(source, target, own.at[at])
            copy.start()
            keeps.append(copy)

        for k in range(nkb):
            settle(m_got[k].at[pl.ds(0, dp - 1)], send.at[2], r["m_sem"].at[k], False)

            def rows_for(peer):
                part = t2[k][pl.ds(pl.multiple_of(peer * lay.cols, 16), lay.cols), :]
                got = m_got[k][...].reshape(-1, E)
                return jnp.dot(part, got, preferred_element_type=FULL).astype(LOW)

            @pl.loop(1, half)
            def _(step):
                peer = lax.rem(mine_at + step, half)
                y_put[peer, k] = rows_for(peer)
                target, sem = y_ref.at[mine_at, k], r["y_sem"].at[0]
                remote(y_put.at[peer, k], target, send.at[3], sem, half_device(peer)).start()

            y_put[mine_at, k] = rows_for(mine_at)
        ends_with = pltpu.make_async_copy(y_put.at[mine_at], y_ref.at[mine_at], own.at[nkb + 2])
        ends_with.start()

        if last:
            (g_put,), (g_ref,) = r["g_put"], r["g"]
            for g, (begin, length) in enumerate(spans):
                got = d_got.at[pl.ds(0, ns - 1), pl.ds(begin, length)]
                settle(got, r["line_send"].at[0], r["line_got"].at[g], False)

                @pl.loop(begin, ends[g])
                def _(degree):
                    for p in (0, 1):
                        total = d_put[z, degree, p].astype(FULL)
                        for step in range(1, ns):
                            source = lax.rem(z + step, ns)
                            total = total + d_got[source, degree, p].astype(FULL)
                        g_put[degree, :, p] = total.reshape(lay.x, lay.e_dev, E)
                    if lay.even:
                        slot = lax.rem(degree, lay.slots)
                        for at_x in range(lay.x):
                            peer = degree // lay.slots * lay.x + at_x

                            @pl.when(peer != me)
                            def _():
                                push(
                                    g_put.at[degree, at_x],
                                    g_ref.at[me, slot],
                                    r["g_sem"].at[0],
                                    r["g_sem"].at[1],
                                    peer,
                                )

            if lay.even:
                copy = pltpu.make_async_copy(
                    g_put.at[pl.ds(n * lay.slots, lay.slots), x], g_ref.at[me], own.at[nkb + 3]
                )
            else:
                copy = pltpu.make_async_copy(g_put, g_ref, own.at[nkb + 3])
            copy.start()
            copy.wait()
            if lay.even:
                some = g_ref.at[pl.ds(0, dp - 1)]
                settle(some, r["g_sem"].at[0], r["g_sem"].at[1], True)
                settle(some, r["g_sem"].at[0], r["g_sem"].at[1], False)

        ends_with.wait()
        for copy in keeps:
            copy.wait()
        settle(f_ref.at[pl.ds(0, half - 1)], send.at[0], r["f_sem"].at[0], True)
        for k in range(nkb):
            settle(s_got[k].at[pl.ds(0, dp - 1)], send.at[1], r["s_sem"].at[0], True)
            settle(m_got[k].at[pl.ds(0, dp - 1)], send.at[2], r["m_sem"].at[0], True)
        if last:
            settle(w.at[pl.ds(0, ns - 1)], r["line_send"].at[0], r["line_got"].at[0], True)
        if fetch:
            for distance in range(1, ns):
                for sign, _ in lines:

                    @pl.when(jnp.logical_and(inside(z + sign), inside(z - sign * (distance - 1))))
                    def _():
                        settle(w.at[0], r["line_send"].at[0], r["line_got"].at[0], True)

        if carry:
            swap.wait()
        settle(y_put.at[pl.ds(0, half - 1)], send.at[3], r["y_sem"].at[0], True)
        settle(y_put.at[pl.ds(0, half - 1)], send.at[3], r["y_sem"].at[0], False)

    spot = pl.BlockSpec(memory_space=pl.ANY)
    operands = [v for group in ins.values() for v in group]
    results = [jax.ShapeDtypeStruct(*v) for group in outs.values() for v in group]
    scratch = [pltpu.VMEM(*v) for group in buffers.values() for v in group]
    scratch += [dma((count,)) for count in sems.values()]
    got = list(
        pl.pallas_call(
            kernel,
            out_shape=results,
            in_specs=[spot] * len(operands),
            out_specs=[spot] * len(results),
            scratch_shapes=scratch,
            compiler_params=pltpu.CompilerParams(
                collective_id=tag, has_side_effects=True, vmem_limit_bytes=58 << 20
            ),
            cost_estimate=pl.CostEstimate(
                flops=40_000_000_000, bytes_accessed=100_000_000, transcendentals=0
            ),
            name="spectral_back" if back else "spectral",
        )(*operands)
    )
    given = {}
    for name, entries in outs.items():
        given[name] = got[: len(entries)]
        del got[: len(entries)]
    rows_out = given["y"][0].reshape(half, nkb, items, rows, size, E)
    rows_out = rows_out.transpose(2, 3, 0, 1, 4, 5).reshape(items, rows, -1, E)
    return rows_out, given


def prologue(lay, spec_laid, small, swaps, tag):
    chips = lay.dp * lay.ns // 2

    def kernel(*refs):
        spec_ref, small_ref = refs[:2]
        swap_refs = refs[2 : 2 + len(swaps)]
        spec_got, small_got = refs[2 + len(swaps) : 4 + len(swaps)]
        swap_got = refs[4 + len(swaps) : 4 + 2 * len(swaps)]
        sent, got, own, swap_sem = refs[4 + 2 * len(swaps) :]
        z, x, n = lay.here()
        _, me, device = group_of(lay, "plane")
        core = n % 2
        chip = (z * lay.x + x) * (lay.ns // 2) + n // 2
        sibling = (z * lay.x + x, n + 1 - 2 * core)

        def chip_device(at):
            return at // (lay.ns // 2), at % (lay.ns // 2) * 2 + core

        barrier = pltpu.get_barrier_semaphore()

        def greet(target):
            pl.semaphore_signal(barrier, inc=1, device_id=target, device_id_type=MESH)

        @pl.loop(1, lay.dp)
        def _(step):
            greet(device(lax.rem(me + step, lay.dp)))

        @pl.loop(1, chips)
        def _(step):
            greet(chip_device(lax.rem(chip + step, chips)))

        greet(sibling)

        greet_senders(lay, greet)
        pl.semaphore_wait(barrier, lay.dp + chips - 1 + jnp.where(lay.stays(), 1, 2))

        def remote(source, target, at, to):
            return pltpu.make_async_remote_copy(
                src_ref=source,
                dst_ref=target,
                send_sem=sent.at[at],
                recv_sem=got.at[at],
                device_id=to,
                device_id_type=MESH,
            )

        @pl.loop(1, chips)
        def _(step):
            to = chip_device(lax.rem(chip + step, chips))
            remote(small_ref, small_got.at[core, chip], 1, to).start()

        @pl.loop(1, lay.dp)
        def _(step):
            peer = lax.rem(me + step, lay.dp)
            remote(spec_ref.at[peer], spec_got.at[me], 0, device(peer)).start()

        moves = [
            Swap(lay, a, b, [swap_sem.at[at, k] for k in range(3)])
            for at, (a, b) in enumerate(zip(swap_refs, swap_got))
        ]
        for move in moves:
            move.start()
        copies = [
            pltpu.make_async_copy(small_ref, small_got.at[core, chip], own.at[0]),
            pltpu.make_async_copy(spec_ref.at[me], spec_got.at[me], own.at[1]),
        ]
        for copy in copies:
            copy.start()
        for copy in copies:
            copy.wait()
        some = small_got.at[core, pl.ds(0, chips - 1)]
        remote(some, some, 1, sibling).wait()
        remote(small_got.at[core], small_got.at[core], 2, sibling).start()
        some = spec_got.at[pl.ds(0, lay.dp - 1)]
        remote(some, some, 0, sibling).wait()
        remote(small_got.at[core], small_got.at[core], 2, sibling).wait()

        for move in moves:
            move.wait()

    spot = pl.BlockSpec(memory_space=pl.ANY)
    outs = [spec_laid, jax.ShapeDtypeStruct((2, chips) + small.shape, small.dtype), *swaps]
    count = 3
    got = pl.pallas_call(
        kernel,
        out_shape=[jax.ShapeDtypeStruct(o.shape, o.dtype) for o in outs],
        in_specs=[spot] * (2 + len(swaps)),
        out_specs=[spot] * len(outs),
        scratch_shapes=[
            pltpu.SemaphoreType.DMA((count,)),
            pltpu.SemaphoreType.DMA((count,)),
            pltpu.SemaphoreType.DMA((2,)),
            pltpu.SemaphoreType.DMA((len(swaps), 3)),
        ],
        compiler_params=pltpu.CompilerParams(collective_id=tag, has_side_effects=True),
        name="prologue",
    )(spec_laid, small, *swaps)
    every = got[1].swapaxes(0, 1).reshape((2 * chips,) + small.shape)
    return got[0], every, list(got[2:])


def spec_out(lay, spec):
    z, x, n = lay.here()
    low = spec.astype(LOW).transpose(1, 2, 0, 3)
    tail = (2, lay.e_dev, E)
    if lay.even:
        laid = low.reshape((lay.slots, lay.dp) + tail).swapaxes(0, 1)
    else:
        at = (jnp.arange(lay.dp) - lay.lns * n) % lay.dp
        at = at[:, None] + lay.dp * jnp.arange(lay.slots)
        laid = jnp.take(low, jnp.minimum(at, lay.lns - 1), axis=0)
    return laid.reshape(lay.dp, -1, E)


def spec_in(lay, got):
    z, x, n = lay.here()
    member = n * lay.x + x
    got = got.reshape((lay.ns, lay.x, lay.slots, 2, lay.e_dev, E))
    got = got.transpose(0, 2, 3, 1, 4, 5).reshape(lay.ns, lay.slots, 2, lay.e_plane, E)
    if lay.even:
        return got.reshape((lay.lper,) + got.shape[2:])
    degree = lay.dp * jnp.arange(lay.lper) + member
    return got[degree // lay.lns, degree % lay.lns // lay.dp]


def spec_home(lay, given, tag):
    z, x, n = lay.here()
    member = n * lay.x + x
    if lay.even:
        mine = given.swapaxes(0, 1).reshape(lay.lns, 2, lay.e_dev, E)
        return mine.transpose(2, 0, 1, 3)
    first = (member - lay.lns * jnp.arange(lay.ns)) % lay.dp + lay.lns * jnp.arange(lay.ns)
    at = (first[:, None] + lay.dp * jnp.arange(lay.slots) - member) // lay.dp
    slots = given[jnp.clip(at, 0, lay.lper - 1)]
    slots = slots.transpose(0, 2, 1, 3, 4, 5)
    (back,) = exchange(lay, [slots.reshape(lay.dp, -1, E)], ["each"], "plane", tag)
    back = back.reshape(lay.dp, lay.slots, 2, lay.e_dev, E)
    degree = lay.lns * n + jnp.arange(lay.lns)
    source = degree % lay.dp
    slot = (jnp.arange(lay.lns) - (source - lay.lns * n) % lay.dp) // lay.dp
    return back[source, slot].transpose(2, 0, 1, 3)


def pad_rows(values, rows):
    return jnp.pad(values, ((0, 0),) * (values.ndim - 2) + ((0, rows - values.shape[-2]), (0, 0)))


def wide(values):
    return jnp.pad(values, ((0, 0),) * (values.ndim - 1) + ((0, 128 - values.shape[-1]),))


def forward_block(lay, residual, weights, tables, tag, fetch, carry):
    spec_w, up_w, down_w, gain_low = weights
    gain_vec = gain_low.astype(FULL)
    dft_fwd, dft_inv, quad_tab, plain_tab, ones = tables
    normed_a = normalize(residual, gain_vec[:, 0]).astype(LOW)
    fourier = jnp.einsum("brke,kq->brqe", normed_a, dft_fwd, preferred_element_type=FULL)
    restored, given = spectral(
        lay, fourier.astype(LOW), quad_tab[0], plain_tab[1], ones, tag, spec_w, fetch, carry
    )
    middle = residual + jnp.einsum(
        "brqe,kq->brke", restored, dft_inv, preferred_element_type=FULL
    )
    normed_b = normalize(middle, gain_vec[:, 1]).astype(LOW)
    pre_act = jnp.einsum("brke,fe->brkf", normed_b, up_w, preferred_element_type=FULL)
    hidden = jax.nn.gelu(pre_act).astype(LOW)
    output = middle + jnp.einsum("brkf,fe->brke", hidden, down_w, preferred_element_type=FULL)
    return (output, (residual, given["keep"], middle, normed_b, pre_act, hidden), given)


def backward_block(
    lay, output_gradient, saved, weights, tables, tag, earlier, carry, sums, d_dec
):
    residual, spectrum, middle, normed_b, pre_act, hidden = saved
    spec_w, up_w, down_w, gain_low = weights
    gain_vec = gain_low.astype(FULL)
    dft_fwd, dft_inv, quad_tab, plain_tab, ones = tables
    g_out = output_gradient.astype(LOW)
    d_down = jnp.einsum("brkf,brke->fe", hidden, g_out, preferred_element_type=FULL)
    d_hidden = jnp.einsum("brke,fe->brkf", g_out, down_w, preferred_element_type=FULL)
    d_pre = jax.vjp(jax.nn.gelu, pre_act)[1](d_hidden)[0].astype(LOW)
    d_up = jnp.einsum("brkf,brke->fe", d_pre, normed_b, preferred_element_type=FULL)
    d_normed_b = jnp.einsum("brkf,fe->brke", d_pre, up_w, preferred_element_type=FULL)
    d_mid_part, d_gain_b = jax.vjp(normalize, middle, gain_vec[:, 1])[1](d_normed_b)
    d_middle = output_gradient + d_mid_part
    d_restored = jnp.einsum(
        "brke,kq->brqe", d_middle.astype(LOW), dft_inv, preferred_element_type=FULL
    ).astype(LOW)
    sums = tuple(a + b for a, b in zip(sums, (d_up, d_down, d_dec))) if sums else (
        d_up,
        d_down,
        d_dec,
    )
    d_restored, sums = lax.optimization_barrier((d_restored, sums))
    d_fourier, given = spectral(
        lay,
        d_restored,
        plain_tab[0],
        quad_tab[1],
        ones,
        tag,
        spec_w,
        carry=carry,
        saved=spectrum,
        earlier=earlier,
    )
    d_normed_a = jnp.einsum("brqe,kq->brke", d_fourier, dft_fwd, preferred_element_type=FULL)
    d_res_part, d_gain_a = jax.vjp(normalize, residual, gain_vec[:, 0])[1](d_normed_a)
    d_gain = jnp.stack([d_gain_a, d_gain_b], axis=1)
    return d_middle + d_res_part, given, sums, d_gain


def product(left, right, dims):
    parts = []
    for value in (left, right):
        high = value.astype(LOW)
        parts.append((high, (value - high.astype(FULL)).astype(LOW)))
    (a, a_rest), (b, b_rest) = parts

    def dot(p, q):
        return lax.dot_general(p, q, (dims, ((), ())), preferred_element_type=FULL)

    return dot(a, b) + (dot(a, b_rest) + dot(a_rest, b))


def finish(lay, blocks, moments, extra, ff_dev, e_own, tag):
    places, planes, pack = blocks.shape[1:4]
    count = 2 * places * planes
    at_enc = 2 * ff_dev

    def kernel(blocks_ref, moment_ref, extra_ref, every_ref, x_ref, scalars_ref, *scratch):
        pair_got, pair, plane_got, plane, line_got, up, down, enc, dec, sent, came = scratch
        z, x, n = lay.here()
        core, y, half = n % 2, n // 2, lay.ns // 2
        place = x * half + y

        def at_core(c):
            return (z * lay.x + x, 2 * y + c)

        def at_place(p):
            return (z * lay.x + p // half, p % half * 2 + core)

        def at_plane(q):
            return (q * lay.x + x, n)

        barrier = pltpu.get_barrier_semaphore()

        def greet(target):
            pl.semaphore_signal(barrier, inc=1, device_id=target, device_id_type=MESH)

        greet(at_core(1 - core))

        @pl.loop(1, places)
        def _(step):
            greet(at_place(lax.rem(place + step, places)))

        @pl.loop(1, planes)
        def _(step):
            greet(at_plane(lax.rem(z + step, planes)))

        pl.semaphore_wait(barrier, places + planes - 1)

        def remote(source, target, at, to):
            return pltpu.make_async_remote_copy(
                src_ref=source,
                dst_ref=target,
                send_sem=sent.at[at],
                recv_sem=came.at[at],
                device_id=to,
                device_id_type=MESH,
            )

        def settle(ref, at):
            remote(ref, ref, at, at_core(1 - core)).wait()

        remote(blocks_ref.at[1 - core], pair_got, 0, at_core(1 - core)).start()
        settle(pair_got, 0)
        for p in range(places):
            pair[p] = blocks_ref[core, p] + pair_got[p]

        @pl.loop(1, places)
        def _(step):
            to = lax.rem(place + step, places)
            remote(pair.at[to], plane_got.at[place], 1, at_place(to)).start()

        plane_got[place] = pair[place]
        settle(plane_got.at[pl.ds(0, places - 1)], 1)
        for q in range(planes):
            total = plane_got[0, q]
            for p in range(1, places):
                total = total + plane_got[p, q]
            plane[q] = total

        @pl.loop(1, planes)
        def _(step):
            to = lax.rem(z + step, planes)
            remote(plane.at[to], line_got.at[z], 2, at_plane(to)).start()

        line_got[z] = plane[z]
        settle(line_got.at[pl.ds(0, planes - 1)], 2)
        total = line_got[0]
        for q in range(1, planes):
            total = total + line_got[q]
        every_ref[core, place, z] = total + extra_ref[...]

        @pl.loop(1, planes)
        def _(step):
            mine = every_ref.at[core, place, z]
            remote(mine, mine, 3, at_plane(lax.rem(z + step, planes))).start()

        settle(every_ref.at[core, place, pl.ds(0, planes - 1)], 3)

        @pl.loop(1, places)
        def _(step):
            mine = every_ref.at[core, place]
            remote(mine, mine, 4, at_place(lax.rem(place + step, places))).start()

        settle(every_ref.at[core, pl.ds(0, places - 1)], 4)
        remote(every_ref.at[core], every_ref.at[core], 5, at_core(1 - core)).start()
        settle(every_ref.at[core], 5)

        every = every_ref[...].reshape(count, pack, E)
        row = lax.broadcasted_iota(jnp.int32, (pack, E), 0)
        lane = lax.broadcasted_iota(jnp.int32, (pack, E), 1)
        enc_rows = jnp.logical_and(row >= at_enc, row < at_enc + e_own)
        added = jnp.logical_and(enc_rows, jnp.logical_or(lane == C + 2, lane == C + 3))
        squares = jnp.sum(jnp.where(added[None], 0.0, every * every), axis=0)
        owned = jnp.logical_and(row == at_enc, lane == C + 3)
        squares = squares + jnp.where(owned, jnp.sum(every, axis=0), 0.0)
        norm = jnp.sqrt(jnp.sum(squares, keepdims=True))
        clip = CLIP_NORM / jnp.maximum(norm, CLIP_NORM)
        at_lane = lax.broadcasted_iota(jnp.int32, (8, 128), 1)
        scalars_ref[...] = jnp.where(at_lane == 0, norm, clip)

        moment = MOMENTUM * moment_ref[...].reshape(count, pack, E) + clip[None] * every
        whole = ff_dev % 8 == 0 and e_own % 8 == 0

        def rows_of(begin, size):
            if whole:
                return moment[:, begin : begin + size].reshape(-1, E)
            inside = jnp.logical_and(row >= begin, row < begin + size)
            return jnp.where(inside[None], moment, 0.0).reshape(-1, E)

        both = rows_of(at_enc, e_own)
        near = lax.broadcasted_iota(jnp.int32, (both.shape[0], 128), 1) < C
        starts = [rows_of(0, ff_dev), rows_of(ff_dev, ff_dev)]
        starts += [jnp.where(near, both[:, :128], 0.0), both[:, 128:]]
        for start, out in zip(starts, (up, down, enc, dec)):
            square = jnp.sum(start * start, keepdims=True)
            out[...] = start / (jnp.sqrt(square) + 1e-07)

        @pl.loop(0, NS_ITERS)
        def _(sweep):
            for out in (up, down, enc, dec):
                matrix = out[...]
                gram_mat = product(matrix, matrix, ((0,), (0,)))
                square = product(gram_mat, gram_mat, ((1,), (0,)))
                poly = NS_SECOND * gram_mat + NS_THIRD * square
                out[...] = NS_FIRST * matrix + product(matrix, poly, ((1,), (0,)))

        both = jnp.concatenate([enc[...], dec[...]], axis=1)
        shape = (2, places, planes)
        if whole:
            x_ref[:, :, :, :ff_dev] = up[...].reshape(shape + (ff_dev, E))
            x_ref[:, :, :, ff_dev:at_enc] = down[...].reshape(shape + (ff_dev, E))
            x_ref[:, :, :, at_enc : at_enc + e_own] = both.reshape(shape + (e_own, E))
        else:
            x_ref[...] = (up[...] + down[...] + both).reshape(shape + (pack, E))

    whole = ff_dev % 8 == 0 and e_own % 8 == 0
    tall = FF if whole else count * pack
    small = E if whole else count * pack
    fast = pl.BlockSpec(memory_space=pltpu.VMEM)
    return pl.pallas_call(
        kernel,
        out_shape=[
            jax.ShapeDtypeStruct(blocks.shape, FULL),
            jax.ShapeDtypeStruct(blocks.shape, FULL),
            jax.ShapeDtypeStruct((8, 128), FULL),
        ],
        in_specs=[fast] * 3,
        out_specs=[fast] * 3,
        scratch_shapes=[
            pltpu.VMEM(blocks.shape[1:], FULL),
            pltpu.VMEM(blocks.shape[1:], FULL),
            pltpu.VMEM(blocks.shape[1:], FULL),
            pltpu.VMEM(blocks.shape[2:], FULL),
            pltpu.VMEM(blocks.shape[2:], FULL),
            pltpu.VMEM((tall, E), FULL),
            pltpu.VMEM((tall, E), FULL),
            pltpu.VMEM((small, 128), FULL),
            pltpu.VMEM((small, 128), FULL),
            pltpu.SemaphoreType.DMA((6,)),
            pltpu.SemaphoreType.DMA((6,)),
        ],
        compiler_params=pltpu.CompilerParams(
            collective_id=tag, has_side_effects=True, vmem_limit_bytes=56 << 20
        ),
        name="finish",
    )(blocks, moments, extra)


def natural(values):
    order = tuple(range(values.ndim))
    return with_layout_constraint(values, DeviceLayout(major_to_minor=order))


def adam_step(weight, moment_a, moment_b, gradient, step_rate):
    moment_a = BETA_FIRST * moment_a + (1.0 - BETA_FIRST) * gradient
    moment_b = BETA_SECOND * moment_b + (1.0 - BETA_SECOND) * gradient * gradient
    corrected_a = moment_a / (1.0 - BETA_FIRST**STEP)
    corrected_b = moment_b / (1.0 - BETA_SECOND**STEP)
    return (
        moment_a,
        moment_b,
        weight - step_rate * (corrected_a / (jnp.sqrt(corrected_b) + 1e-08) + DECAY * weight),
    )


def local(
    fields,
    targets,
    valid,
    var_class,
    enc_t,
    enc_mom,
    dec,
    dec_mom,
    spec,
    spec_m,
    spec_v,
    up_t,
    up_mom,
    down,
    down_mom,
    gains,
    gain_m,
    gain_v,
):
    dp_count, ns_count = lax.axis_size("dp"), lax.axis_size("ns")
    devices = dp_count * ns_count
    lay = Layout(dp_count, ns_count, fields.shape[0], fields.shape[1])
    z, x, n = lay.here()
    lat_count = lay.block_rows * dp_count

    ff_dev, e_own = up_t.shape[1], E // devices
    pack = -(-(2 * ff_dev + 2 * e_own) // 16) * 16

    def mine(values):
        return lax.dynamic_slice_in_dim(values, n * e_own, e_own, 0)

    def packed(up, down_, enc, dec_, extra):
        both = jnp.concatenate([wide(mine(enc)), wide(mine(dec_))], axis=1)
        return pad_rows(jnp.concatenate([up[0], down_[0], both, extra], axis=0), pack)

    def unpacked(every):
        up = every[:, :ff_dev].reshape(FF, E)
        down_ = every[:, ff_dev : 2 * ff_dev].reshape(FF, E)
        both = every[:, 2 * ff_dev : 2 * ff_dev + e_own].reshape(E, E)
        extra = every[:, 2 * ff_dev + e_own : 2 * ff_dev + 2 * e_own]
        return up, down_, both[:, :128], both[:, 128:], extra

    gain_rows = jnp.pad(mine(gains[0]), ((0, 0), (0, E - 2)))
    small = packed(up_t, down, enc_t, dec, gain_rows).astype(LOW)
    lon_count = fields.shape[2]

    def dense(values):
        fill = (-values.shape[-1] % 16, -lon_count % 128)
        values = values.transpose(0, 1, 3, 2)
        return jnp.pad(values, ((0, 0), (0, 0), (0, fill[0]), (0, fill[1])))

    def usual(values, count=C):
        values = values[:, :, :count, :lon_count].reshape((1, lay.rows, count, lon_count))
        return values.transpose(0, 1, 3, 2)

    swaps = [dense(fields), jnp.pad(valid, ((0, 0), (0, 0), (0, -lon_count % 128)))]
    spec_got, every_low, swaps = prologue(lay, spec_out(lay, spec[0]), small, swaps, 0)
    fields = usual(swaps[0])
    valid = swaps[1][..., :lon_count].reshape(1, lay.rows, lon_count)
    targets = [dense(targets[step]) for step in range(2)]
    up_w, down_w, enc_w, dec_w, extra = unpacked(every_low)
    enc_w, dec_w = enc_w[:, :C], dec_w[:, :C]
    gain_w = extra.reshape(E, E)[:, :2]
    spec_w = spec_in(lay, spec_got)

    colatitude = math.pi * (np.arange(lat_count) + 0.5) / lat_count
    sines = jnp.asarray(np.sin(colatitude).astype(np.float32).reshape(dp_count, lay.block_rows))
    local_sine = jnp.concatenate([sines[at] for at in lay.row_blocks(n, x)])
    var_weight = 1.0 + 0.5 * var_class.astype(FULL)
    pixel_map = valid.astype(FULL) * local_sine[None, :, None]
    weight_part = jnp.sum(pixel_map)
    weight_map = pixel_map[..., None] * var_weight
    weight_rows = jnp.broadcast_to(weight_part, (e_own, E))
    every_mom = lax.all_gather(packed(up_mom, down_mom, enc_mom, dec_mom, weight_rows), BOTH)
    loss_weight = jnp.sum(every_mom[:, 2 * ff_dev + e_own, 0]) * jnp.sum(var_weight)
    core_pack = -(-(2 * ff_dev + e_own) // 8) * 8

    def by_core(values):
        values = values.reshape((ns_count, lay.x, ns_count // 2, 2) + values.shape[1:])
        values = jnp.moveaxis(values, (3, 1, 2, 0), (0, 1, 2, 3))
        return values.reshape((2, dp_count // 2, ns_count) + values.shape[4:])

    def by_device(values):
        values = values.reshape((2, lay.x, ns_count // 2, ns_count) + values.shape[3:])
        values = jnp.moveaxis(values, (3, 1, 2, 0), (0, 1, 2, 3))
        return values.reshape((devices,) + values.shape[4:])

    moments = by_core(pad_rows(every_mom[:, : 2 * ff_dev + e_own], core_pack))

    tables = dft_tables(lay, fields.shape[2]) + legendre_tables(lay, lat_count)
    incoming = fields
    saved = []
    forecasts = []
    for step in range(2):
        weights = (spec_w, up_w, down_w, gain_w)
        hidden = jnp.einsum("brkc,ec->brke", incoming, enc_w, preferred_element_type=FULL)
        fetch, carry = ((True,), ()) if step == 0 else ((), (targets[1],))
        hidden, kept, given = forward_block(lay, hidden, weights, tables, 1 + step, fetch, carry)
        if step == 0:
            (spec_w,) = given["whole"]
        else:
            targets[1] = usual(given["carried"][0])
        closing = hidden.astype(LOW)
        forecast = jnp.einsum("brke,ec->brkc", closing, dec_w, preferred_element_type=FULL)
        saved.append((incoming, kept, closing))
        forecasts.append(forecast)
        incoming = forecast.astype(LOW)

    def loss_of(step):
        error = forecasts[step] - targets[step].astype(FULL)
        return jnp.sum(weight_map * error * error), 2.0 * weight_map * error / loss_weight

    last_loss, gradient = loss_of(1)
    early, d_spec = (), ()
    carry = (targets[0],)
    for step in (1, 0):
        incoming, kept, closing = saved[step]
        low_grad = gradient.astype(LOW)
        d_dec = jnp.einsum("brke,brkc->ec", closing, low_grad, preferred_element_type=FULL)
        gradient = jnp.einsum("brkc,ec->brke", low_grad, dec_w, preferred_element_type=FULL)
        gradient, given, early, d_gain = backward_block(
            lay, gradient, kept, weights, tables, 4 - step, d_spec, carry, early, d_dec
        )
        d_spec, carry = given["d"] + given["g"], ()
        low_grad = gradient.astype(LOW)
        d_enc = jnp.einsum("brkc,brke->ec", incoming, low_grad, preferred_element_type=FULL)
        if step == 1:
            late = (d_gain, d_enc)
            targets[0] = usual(given["carried"][0])
            first_loss, gradient = loss_of(0)
            gradient = gradient + jnp.einsum(
                "brke,ec->brkc", low_grad, enc_w, preferred_element_type=FULL
            )
            loss_local = first_loss + last_loss
    d_gain, d_enc = late[0] + d_gain, late[1] + d_enc
    d_up, d_down, d_dec = early
    g_spec = natural(spec_home(lay, d_spec[0], 5)[None])
    near = jnp.concatenate([d_enc, d_gain, jnp.broadcast_to(loss_local, (E, 1))], axis=1)
    both = jnp.concatenate([wide(near), wide(d_dec)], axis=1).reshape(devices, e_own, E)
    blocks = [d_up.reshape(devices, ff_dev, E), d_down.reshape(devices, ff_dev, E), both]
    blocks = by_core(pad_rows(jnp.concatenate(blocks, axis=1), core_pack))
    at_row = jnp.arange(core_pack)[:, None] == 2 * ff_dev
    at_lane = at_row & (jnp.arange(E)[None, :] == C + 3)
    extra = jnp.where(at_lane, jnp.sum(g_spec * g_spec), 0.0)
    every, matrices, scalars = finish(lay, blocks, moments, extra, ff_dev, e_own, 6)
    grad_norm, clip_scale = scalars[0, 0], scalars[0, 1]
    d = lax.axis_index("dp")
    place = x * (ns_count // 2) + n // 2
    at_enc = 2 * ff_dev

    def own_block(values):
        return values[n % 2, place, z]

    def enc_block(values):
        both = by_device(values[:, :, :, at_enc : at_enc + e_own]).reshape(dp_count, lay.e_dev, E)
        return lax.dynamic_index_in_dim(both, d, keepdims=False)

    loss_sum = every[0, 0, 0, at_enc, C + 2]
    own_grad, own_step = own_block(every), own_block(matrices)
    enc_grad, enc_step = enc_block(every), enc_block(matrices)
    factors = [math.sqrt(max(1.0, FF / E))] * 2 + [math.sqrt(max(1.0, E / C))] * 2

    def muon(master, moment, gradient, matrix, factor):
        moment = MOMENTUM * moment + clip_scale * gradient.reshape(master.shape)
        step = RATE_MUON * (matrix.reshape(master.shape) * factor)
        return moment, master * (1.0 - RATE_MUON * DECAY) - step

    up, down_at = slice(0, ff_dev), slice(ff_dev, 2 * ff_dev)
    up_mom_new, up_new = muon(up_t, up_mom, own_grad[up], own_step[up], factors[0])
    down_mom_new, down_new = muon(
        down, down_mom, own_grad[down_at], own_step[down_at], factors[1]
    )
    enc_mom_new, enc_new = muon(enc_t, enc_mom, enc_grad[:, :C], enc_step[:, :C], factors[2])
    dec_at = slice(128, 128 + C)
    dec_mom_new, dec_new = muon(
        dec, dec_mom, enc_grad[:, dec_at], enc_step[:, dec_at], factors[3]
    )
    g_gain_own = enc_grad[:, C : C + 2][None]
    spec_m_new, spec_v_new, spec_new = adam_step(
        spec, spec_m, spec_v, clip_scale * g_spec, RATE_SPECTRAL
    )
    gain_m_new, gain_v_new, gain_new = adam_step(
        gains, gain_m, gain_v, clip_scale * g_gain_own, RATE_GAIN
    )
    return (
        loss_sum,
        loss_weight,
        grad_norm,
        enc_mom_new,
        enc_new,
        dec_mom_new,
        dec_new,
        up_mom_new,
        up_new,
        down_mom_new,
        down_new,
        spec_m_new,
        spec_v_new,
        spec_new,
        spec_new.astype(LOW),
        gain_m_new,
        gain_v_new,
        gain_new,
    )


def solution(mesh):
    rows = P(None, BOTH, None)
    shard = P("dp", None)
    whole = P(None, "dp", "ns", None, None)
    gain = P(None, "dp", None)
    placed = (
        P("ns", "dp", None, None),
        P(None, "ns", "dp", None, None),
        P("ns", "dp", None),
        P(),
        *[shard] * 4,
        *[whole] * 3,
        *[rows] * 4,
        *[gain] * 3,
    )
    return jax.shard_map(
        local,
        mesh=mesh,
        in_specs=placed,
        out_specs=(P(), P(), P(), *[shard] * 4, *[rows] * 4, *[whole] * 4, *[gain] * 3),
        check_vma=False,
    )
```

```python
import math
import types

import jax
import jax.numpy as jnp
import ml_dtypes
import numpy as np
from jax import lax
from jax.experimental import pallas as pl
from jax.experimental.layout import Layout as DeviceLayout
from jax.experimental.layout import with_layout_constraint
from jax.experimental.pallas import tpu as pltpu
from jax.sharding import PartitionSpec as P

E = 256
FF = 512
C = 73
LDEG = 96
MM = 96
NL = 1
NS_ITERS = 5
STEP = 10

EXACT = lax.Precision.HIGHEST
EPSILON = 1e-06
CLIP_NORM = 0.02
RATE_SPECTRAL = 0.05
RATE_GAIN = 0.1
RATE_MUON = 0.5
BETA_FIRST = 0.9
BETA_SECOND = 0.999
MOMENTUM = 0.95
DECAY = 0.01
NS_FIRST = 3.4445
NS_SECOND = -4.775
NS_THIRD = 2.0315
LOW = jnp.bfloat16
FULL = jnp.float32
MESH = pl.DeviceIdType.MESH
CHUNK = 16
BOTH = ("dp", "ns")


class Layout:
    def __init__(self, dp, ns, items, rows):
        self.dp, self.ns = dp, ns
        self.x, self.half, self.g = dp // ns, ns // 2, dp // 2
        self.block_rows, self.rows = rows, 2 * rows
        self.v = 2 if LDEG % (2 * dp) == 0 else 1
        self.owners = self.v * dp
        self.kper, self.lns = MM // self.g, LDEG // ns
        self.lper, self.lall = LDEG // self.owners, LDEG // dp
        self.kb = 8
        self.kd = self.kb * self.g // self.owners
        self.nkb = -(-self.kper // self.kb)
        self.blocks = [[i for i in range(self.lper) if i >= k * self.kd] for k in range(self.nkb)]
        self.counts = [len(b) for b in self.blocks]
        self.starts = np.cumsum([0] + self.counts).tolist()
        self.size = 2 * self.kb
        self.cols = self.rows * self.size
        self.ends = [min((k + 1) * self.kd, self.lper) for k in range(self.nkb)]
        self.ends[-1] = self.lper
        self.slots = -(-self.lns // dp)
        self.even = self.lns % dp == 0
        self.e_dev = E // dp
        self.e_plane = self.x * self.e_dev

    def here(self):
        d, n = lax.axis_index("dp"), lax.axis_index("ns")
        return d // self.x, d % self.x, n

    def row_blocks(self, n, x):
        return [(2 * (n % self.half) + s) * self.x + x for s in (0, 1)]

    def item_goes(self, at):
        z, x, n = self.here()
        plane = 2 * (n % self.half) + at
        to = n // self.half * self.half + z // 2
        return (plane * self.x + x, to), jnp.logical_and(plane == z, to == n)

    def item_comes(self, slot):
        z, x, n = self.here()
        return ((2 * (n % self.half) + slot) * self.x + x, n // self.half * self.half + z // 2)

    def stays(self):
        z, x, n = self.here()
        return z // 2 == n % self.half


def group_of(lay, kind):
    z, x, n = lay.here()
    if kind == "plane":
        return lay.dp, n * lay.x + x, lambda p: (z * lay.x + p % lay.x, p // lay.x)
    if kind == "owners":
        base = z // lay.v * lay.v
        return (
            lay.owners,
            (z - base) * lay.dp + n * lay.x + x,
            lambda p: ((base + p // lay.dp) * lay.x + p % lay.x, p % lay.dp // lay.x),
        )
    if kind == "half":
        first = n // lay.half * lay.half
        return (
            lay.g,
            n % lay.half * lay.x + x,
            lambda q: (z * lay.x + q % lay.x, first + q // lay.x),
        )
    return lay.ns, z, lambda q: (q * lay.x + x, n)


def exchange(lay, arrays, kinds, group, tag):
    count = {"plane": lay.dp, "line": lay.ns}[group]

    def kernel(*refs):
        total = len(arrays)
        ins, outs = refs[:total], refs[total : 2 * total]
        send, recv, own = refs[2 * total :]
        size, me, device = group_of(lay, group)
        barrier = pltpu.get_barrier_semaphore()

        @pl.loop(1, size)
        def _(step):
            pl.semaphore_signal(
                barrier, inc=1, device_id=device(lax.rem(me + step, size)), device_id_type=MESH
            )

        pl.semaphore_wait(barrier, size - 1)

        @pl.loop(1, size)
        def _(step):
            peer = lax.rem(me + step, size)
            for at in range(total):
                pltpu.make_async_remote_copy(
                    src_ref=ins[at].at[peer] if kinds[at] == "each" else ins[at],
                    dst_ref=outs[at].at[me],
                    send_sem=send.at[at],
                    recv_sem=recv.at[at],
                    device_id=device(peer),
                    device_id_type=MESH,
                ).start()

        for at in range(total):
            mine = ins[at].at[me] if kinds[at] == "each" else ins[at]
            copy = pltpu.make_async_copy(mine, outs[at].at[me], own)
            copy.start()
            copy.wait()
        for at in range(total):
            some = outs[at].at[pl.ds(0, size - 1)]
            pltpu.make_async_remote_copy(
                src_ref=some,
                dst_ref=some,
                send_sem=send.at[at],
                recv_sem=recv.at[at],
                device_id=device(lax.rem(me + 1, size)),
                device_id_type=MESH,
            ).wait()

    shapes = [
        jax.ShapeDtypeStruct(a.shape if k == "each" else (count,) + a.shape, a.dtype)
        for a, k in zip(arrays, kinds)
    ]
    spot = pl.BlockSpec(memory_space=pl.ANY)
    return pl.pallas_call(
        kernel,
        out_shape=shapes,
        in_specs=[spot] * len(arrays),
        out_specs=[spot] * len(arrays),
        scratch_shapes=[
            pltpu.SemaphoreType.DMA((len(arrays),)),
            pltpu.SemaphoreType.DMA((len(arrays),)),
            pltpu.SemaphoreType.DMA,
        ],
        compiler_params=pltpu.CompilerParams(collective_id=tag, has_side_effects=True),
        name=f"exchange_{group}_{tag}",
    )(*arrays)


def legendre(lat_count):
    colatitude = math.pi * (np.arange(lat_count) + 0.5) / lat_count
    cosine, log_sine = np.cos(colatitude)[None, :], np.log(np.sin(colatitude))[None, :]
    orders = np.arange(MM, dtype=np.float64)
    ladder = np.arange(1, MM, dtype=np.float64)
    sums = np.concatenate([[0.0], np.cumsum(np.log((2 * ladder - 1) / (2 * ladder)))])
    diagonal = np.exp(
        (0.5 * np.log((2 * orders + 1) / (4 * math.pi)) + 0.5 * sums)[:, None]
        + orders[:, None] * log_sine
    )
    table = np.zeros((LDEG, MM, lat_count))
    for degree in range(LDEG):
        for order in range(min(degree, MM - 1) + 1):
            if degree == order:
                table[degree, order] = diagonal[order]
                continue
            a = math.sqrt((4.0 * degree**2 - 1) / (degree**2 - order**2))
            value = cosine[0] * table[degree - 1, order]
            if degree >= 2:
                b = math.sqrt(
                    max((degree - 1.0) ** 2 - order**2, 0) / (4 * (degree - 1.0) ** 2 - 1)
                )
                value = value - b * table[degree - 2, order]
            table[degree, order] = a * value
    return table.astype(np.float32)


def low_table(values):
    return values.astype(np.float32).astype(ml_dtypes.bfloat16)


def dft_tables(lay, lon_count):
    turns = np.arange(lon_count)[:, None] * np.arange(MM)[None, :] % lon_count
    phases = 2 * math.pi / lon_count * turns
    paired = np.stack([np.cos(phases), -np.sin(phases)], axis=2)
    weight = np.where(np.arange(MM) == 0, 1.0, 2.0)
    forward = paired * (2 * math.pi / lon_count)
    inverse = paired * weight[None, :, None] / (2 * math.pi)

    def order(table):
        table = table.reshape(lon_count, lay.kper, lay.g, 2).transpose(0, 2, 1, 3)
        pad = lay.nkb * lay.kb - lay.kper
        table = np.pad(table, ((0, 0), (0, 0), (0, pad), (0, 0)))
        return low_table(table.reshape(lon_count, -1))

    return order(forward), order(inverse)


def legendre_tables(lay, lat_count):
    plain = legendre(lat_count)
    colatitude = math.pi * (np.arange(lat_count) + 0.5) / lat_count
    quadrature = 2 * math.pi * math.pi / lat_count * np.sin(colatitude)
    pad = lay.nkb * lay.kb - lay.kper

    def own(table):
        table = table.reshape(lay.lper, lay.owners, lay.kper, lay.g, lat_count)
        table = np.pad(table.transpose(3, 1, 0, 2, 4), ((0, 0), (0, 0), (0, 0), (0, pad), (0, 0)))
        table = low_table(table)
        blocks = []
        for k in range(lay.nkb):
            part = table[:, :, k * lay.kd :, k * lay.kb : (k + 1) * lay.kb]
            blocks.append(part.reshape(lay.g, -1, lay.kb * lat_count))
        across = [jnp.asarray(np.ascontiguousarray(b.swapaxes(1, 2))) for b in blocks]
        return jnp.asarray(np.concatenate(blocks, axis=1)), across

    col = np.arange(lay.g * lay.cols)
    col_part, col_k = col % 2, col // 2 % lay.kb
    member, row = col // lay.cols, col // lay.size % lay.rows
    block = (2 * (member // lay.x) + row // lay.block_rows) * lay.x + member % lay.x
    col_lat = block * lay.block_rows + row % lay.block_rows
    col_kind = col_part * lay.kb + col_k
    pick = col_k * lat_count + col_lat
    spread = np.arange(lay.kb * lat_count)[:, None] == pick[None, :]
    same = np.arange(lay.size)[:, None] == col_kind[None, :]
    wide_same = np.tile(same.T, (1, CHUNK))
    count = lay.owners * lay.lper
    repeat = np.arange(CHUNK * lay.size)[:, None] // lay.size == np.arange(CHUNK)[None, :]
    across = np.arange(count)[:, None] == np.arange(count * lay.size)[None, :] // lay.size
    ones = [
        jnp.asarray(v.astype(ml_dtypes.bfloat16))
        for v in (spread, spread.T, same, wide_same, repeat, across)
    ]
    return own(plain * quadrature.astype(np.float32)[None, None, :]), own(plain), ones


def normalize(values, gain_vec):
    return (
        values * lax.rsqrt(jnp.mean(values * values, axis=-1, keepdims=True) + EPSILON) * gain_vec
    )


def greet_senders(lay, greet):
    z, _, _ = lay.here()
    for slot in (0, 1):

        @pl.when(jnp.logical_not(jnp.logical_and(lay.stays(), z % 2 == slot)))
        def _():
            greet(lay.item_comes(slot))


class Swap:
    def __init__(self, lay, gone, come, sems):
        z, _, _ = lay.here()
        slot = z % 2
        self.here = [lay.item_goes(at)[1] for at in (0, 1)]
        self.far = [
            pltpu.make_async_remote_copy(
                src_ref=gone.at[at],
                dst_ref=come.at[slot],
                send_sem=sems[0],
                recv_sem=sems[1],
                device_id=lay.item_goes(at)[0],
                device_id_type=MESH,
            )
            for at in (0, 1)
        ]
        self.near = [
            pltpu.make_async_copy(gone.at[at], come.at[slot], sems[2]) for at in (0, 1)
        ]
        whole, one = come, come.at[0]
        self.stays = lay.stays()
        self.all_far, self.one_far = [
            pltpu.make_async_remote_copy(
                src_ref=ref,
                dst_ref=ref,
                send_sem=sems[0],
                recv_sem=sems[1],
                device_id=lay.item_goes(0)[0],
                device_id_type=MESH,
            )
            for ref in (whole, one)
        ]

    def start(self):
        for here, far, near in zip(self.here, self.far, self.near):

            @pl.when(here)
            def _():
                near.start()

            @pl.when(jnp.logical_not(here))
            def _():
                far.start()

    def wait(self):
        @pl.when(self.stays)
        def _():
            self.one_far.wait()
            self.near[0].wait()

        @pl.when(jnp.logical_not(self.stays))
        def _():
            self.all_far.wait()


class Total:
    def __init__(self, lay, put, every, scratch, sent, came):
        self.lay, self.put, self.every = lay, put, every
        self.pair_got, self.pair, self.line_got, self.line, self.plane_got = scratch
        self.sent, self.came = sent, came
        self.places, self.planes = lay.dp // 2, lay.ns
        self.z, self.x, n = lay.here()
        self.core, self.y, self.n, self.y_count = n % 2, n // 2, n, lay.ns // 2
        self.place = self.x * self.y_count + self.y

    @staticmethod
    def scratch(shape):
        whole = pltpu.VMEM(shape[1:], FULL)
        part = pltpu.VMEM(shape[2:], FULL)
        return [whole, whole, whole, part, part]

    def at_core(self):
        return (self.z * self.lay.x + self.x, self.n + 1 - 2 * self.core)

    def at_place(self, p):
        at = p % self.y_count * 2 + self.core
        return (self.z * self.lay.x + p // self.y_count, at)

    def at_plane(self, q):
        return (q * self.lay.x + self.x, self.n)

    def greet(self, greet):
        greet(self.at_core())

        @pl.loop(1, self.places)
        def _(step):
            greet(self.at_place(lax.rem(self.place + step, self.places)))

        @pl.loop(1, self.planes)
        def _(step):
            greet(self.at_plane(lax.rem(self.z + step, self.planes)))

        return self.places + self.planes - 1

    def remote(self, source, target, at, to):
        return pltpu.make_async_remote_copy(
            src_ref=source,
            dst_ref=target,
            send_sem=self.sent.at[at],
            recv_sem=self.came.at[at],
            device_id=to,
            device_id_type=MESH,
        )

    def settle(self, ref, at):
        self.remote(ref, ref, at, self.at_core()).wait()

    def pass_on(self, count, mine, stage, device, what):
        @pl.loop(1, count)
        def _(step):
            to = lax.rem(mine + step, count)
            source, target = what(to)
            self.remote(source, target, stage, device(to)).start()

    def step(self, stage, extra=None):
        core, place, z, places, planes = self.core, self.place, self.z, self.places, self.planes
        every, put = self.every, self.put
        if stage == 0:
            self.remote(put.at[1 - core], self.pair_got, 0, self.at_core()).start()
        if stage == 1:
            self.settle(self.pair_got, 0)
            for q in range(planes):
                self.pair[q] = put[core, q] + self.pair_got[q]
            there = self.line_got.at[z]
            self.pass_on(planes, z, 1, self.at_plane, lambda to: (self.pair.at[to], there))
        if stage == 2:
            self.line_got[z] = self.pair[z]
            self.settle(self.line_got.at[pl.ds(0, planes - 1)], 1)
            for p in range(places):
                total = self.line_got[0, p]
                for q in range(1, planes):
                    total = total + self.line_got[q, p]
                self.line[p] = total
            there = self.plane_got.at[place]
            self.pass_on(places, place, 2, self.at_place, lambda to: (self.line.at[to], there))
        if stage == 3:
            self.plane_got[place] = self.line[place]
            self.settle(self.plane_got.at[pl.ds(0, places - 1)], 2)
            total = self.plane_got[0]
            for p in range(1, places):
                total = total + self.plane_got[p]
            every[core, z, place] = total if extra is None else total + extra
            own = every.at[core, z, place]
            self.pass_on(planes, z, 3, self.at_plane, lambda to: (own, own))
        if stage == 4:
            self.settle(every.at[core, pl.ds(0, planes - 1), place], 3)
            own = every.at[core, pl.ds(0, planes), place]
            self.pass_on(places, place, 4, self.at_place, lambda to: (own, own))
        if stage == 5:
            self.settle(every.at[core, pl.ds(0, planes), pl.ds(0, places - 1)], 4)
            self.remote(every.at[core], every.at[core], 5, self.at_core()).start()
        if stage == 6:
            self.settle(every.at[core], 5)


def turned(real, imag):
    both = jnp.concatenate([real[:, None], imag[:, None]], axis=1)
    return both.reshape(-1, E).astype(LOW)


def parts_of(values):
    split = values.reshape(-1, 2, 8, E)
    return split[:, 0], split[:, 1]


def spectral(
    lay,
    values,
    first,
    second,
    ones,
    tag,
    spec_w,
    fetch=(),
    carry=(),
    saved=(),
    earlier=(),
    parts=(),
):
    back, last = bool(saved), bool(earlier)
    placed = spec_w.ndim == 5
    nkb, dp, ns, size, half = lay.nkb, lay.owners, lay.ns, lay.size, lay.g
    counts, ends, lper = lay.counts, lay.ends, lay.lper
    items, rows = values.shape[:2]
    laid = values.reshape(items, rows, half, nkb, size, E)
    laid = laid.transpose(2, 3, 0, 1, 4, 5).reshape(half, nkb, lay.cols, E)
    w_shape = (ns, lper, 2, lay.e_plane, E)
    dma = pltpu.SemaphoreType.DMA
    tiles = [(dp, c, size, E) for c in counts]
    spans = [(g * lay.kd, ends[g] - g * lay.kd) for g in range(nkb)]

    ins = dict(f=[laid], p1=[first], p2=list(second), ones=list(ones), w=[spec_w])
    ins |= dict(old=list(saved), earlier=list(earlier), carry=list(carry))
    outs = dict(y=[((half, nkb, lay.cols, E), LOW)])
    outs |= dict(keep=[] if back else [(t, LOW) for t in tiles])
    outs |= dict(whole=[(w_shape, LOW)] if fetch else [])
    outs |= dict(d=[(w_shape, LOW)] if back and not last else [])
    owned = (lay.lall, lay.x, 2, lay.e_dev, E)
    if lay.even:
        owned = (lay.dp, lay.slots, 2, lay.e_dev, E)
    outs |= dict(g=[(owned, LOW)] if last else [])
    outs |= dict(squares=[((8, 128), FULL)] if last else [])
    outs |= dict(carried=[(c.shape, c.dtype) for c in carry])
    ins |= dict(parts=list(parts))
    devices = lay.dp * ns
    part_rows = [v.shape[0] // devices for v in parts]
    every_shape = (2, ns, lay.dp // 2, sum(part_rows), E)
    outs |= dict(every=[(every_shape, FULL)] if parts else [])
    tall, broad = lay.size * dp * np.array(counts), half * lay.cols
    buffers = dict(
        f_got=[((nkb, half, lay.cols, E), LOW)],
        t1=[((int(h), broad), LOW) for h in tall],
        t2=[((broad, int(h)), LOW) for h in tall],
        p1_v=[(first.shape[1:], LOW)],
        p2_v=[(p.shape[1:], LOW) for p in second],
        ones_v=[(o.shape, LOW) for o in ones],
        w_v=[(w_shape, LOW)],
        s_put=[(t, LOW) for t in tiles],
        s_got=[(t, LOW) for t in tiles],
        m_put=[(t, LOW) for t in tiles],
        m_got=[(t, LOW) for t in tiles],
        y_put=[((half, nkb, lay.cols, E), LOW)],
        old_v=[(t, LOW) for t in tiles] if back else [],
        early_v=[(w_shape, LOW)] if last else [],
        d_put=[(w_shape, LOW)] if back else [],
        d_got=[(w_shape, LOW)] if last else [],
        g_put=[((lay.lall, lay.x, 2, lay.e_dev, E), LOW)] if last else [],
        part_v=[(v.shape, FULL) for v in parts],
        total=[(v.shape, FULL) for v in Total.scratch(every_shape)] if parts else [],
        square_v=[((8, 128), FULL)] if last else [],
        put_v=[(every_shape, FULL)] * 2 if parts else [],
    )
    sems = dict(f_sem=nkb, s_sem=nkb, m_sem=nkb, y_sem=1, send=4, own=nkb + 4)
    sems |= dict(load=2 + len(second) + len(ones) + len(saved) + 1)
    sems |= dict(part_sem=len(parts) + 1, total_sent=6, total_came=6)
    sems |= dict(line_send=1, line_got=nkb, own_w=1, carry_sem=4, g_sem=2)

    def kernel(*refs):
        refs = list(refs)
        r = types.SimpleNamespace()
        for group in (ins, outs, buffers):
            for name, entries in group.items():
                setattr(r, name, refs[: len(entries)])
                del refs[: len(entries)]
        for name in sems:
            setattr(r, name, refs.pop(0))
        (f_ref,), (y_ref,), (f_got,), (y_put,), (w,) = r.f, r.y, r.f_got, r.y_put, r.w_v
        t1, t2, s_put, s_got, m_put, m_got = r.t1, r.t2, r.s_put, r.s_got, r.m_put, r.m_got
        spread, spread_t, same, wide_same, repeat, across = r.ones_v
        send, own = r.send, r.own
        z, x, n = lay.here()
        _, me, device = group_of(lay, "owners")
        _, place_at, plane_device = group_of(lay, "plane")
        _, mine_at, half_device = group_of(lay, "half")
        _, _, line_device = group_of(lay, "line")
        line = bool(fetch) or last
        barrier = pltpu.get_barrier_semaphore()

        def greet(target):
            pl.semaphore_signal(barrier, inc=1, device_id=target, device_id_type=MESH)

        @pl.loop(1, dp)
        def _(step):
            greet(device(lax.rem(me + step, dp)))

        if line:

            @pl.loop(1, ns)
            def _(step):
                greet(line_device(lax.rem(z + step, ns)))

        if carry:
            greet_senders(lay, greet)
        waits = dp - 1 + (ns - 1 if line else 0)
        if parts:
            put, every = r.put_v
            summed = Total(lay, put, every, r.total, r.total_sent, r.total_came)
            waits = waits + summed.greet(greet)
            for at, ref in enumerate(r.part_v):
                pltpu.make_async_copy(r.parts[at], ref, r.part_sem.at[at]).start()
        pairs = [(r.p1[0].at[mine_at], r.p1_v[0])]
        pairs += [(a, b) for a, b in zip(r.ones, r.ones_v)]
        pairs += [(a.at[mine_at], b) for a, b in zip(r.p2, r.p2_v)]
        tables_at = len(pairs)
        if not fetch:
            pairs += [(r.w[0], w)]
        pairs += list(zip(r.old, r.old_v)) + list(zip(r.earlier, r.early_v))
        loads = []
        for at, (source, target) in enumerate(pairs):
            copy = pltpu.make_async_copy(source, target, r.load.at[at])
            copy.start()
            loads.append(copy)
        mine = []
        for k in range(nkb):
            copy = pltpu.make_async_copy(f_ref.at[mine_at, k], f_got.at[k, mine_at], own.at[k])
            copy.start()
            mine.append(copy)
        if carry:
            pl.semaphore_wait(barrier, waits + jnp.where(lay.stays(), 1, 2))
        else:
            pl.semaphore_wait(barrier, waits)

        def remote(source, target, sent, got, to):
            return pltpu.make_async_remote_copy(
                src_ref=source,
                dst_ref=target,
                send_sem=sent,
                recv_sem=got,
                device_id=to,
                device_id_type=MESH,
            )

        def push(source, target, sent, got, peer):
            remote(source, target, sent, got, device(peer)).start()

        def settle(ref, sent, got, sending):
            copy = remote(ref, ref, sent, got, device(lax.rem(me + 1, dp)))
            if sending:
                copy.wait_send()
            else:
                copy.wait_recv()

        for k in range(nkb):

            @pl.loop(1, half)
            def _(step):
                peer = lax.rem(mine_at + step, half)
                target = f_got.at[k, mine_at]
                sem = r.f_sem.at[k]
                remote(f_ref.at[peer, k], target, send.at[0], sem, half_device(peer)).start()

        if fetch:
            share = r.w[0].at[z] if placed else r.w[0]

            def share_of(to, degree):
                return share.at[degree * lay.v + lax.rem(to, lay.v)]

            for g in range(nkb):

                @pl.loop(*(spans[g][0], ends[g]))
                def _(degree):
                    pltpu.make_async_copy(
                        share_of(z, degree), w.at[z, degree], r.own_w.at[0]
                    ).start()
                    for step in range(1, ns):
                        to = lax.rem(z + step, ns)
                        remote(
                            share_of(to, degree),
                            w.at[z, degree],
                            r.line_send.at[0],
                            r.line_got.at[g],
                            line_device(to),
                        ).start()

        if carry:
            (gone,), (come,) = r.carry, r.carried
            swap = Swap(lay, gone, come, [r.carry_sem.at[at] for at in range(4)])
            swap.start()

        if parts:
            begin = 0
            for at, (ref, count) in enumerate(zip(r.part_v, part_rows)):
                pltpu.make_async_copy(r.parts[at], ref, r.part_sem.at[at]).wait()
                width = ref.shape[1]
                for index in range(devices):
                    d, n_at = divmod(index, ns)
                    place = d % lay.x * (ns // 2) + n_at // 2
                    block = put.at[n_at % 2, d // lay.x, place, pl.ds(begin, count)]
                    if width < E:
                        block[...] = jnp.zeros((count, E), FULL)
                    block[:, :width] = ref[pl.ds(index * count, count), :]
                begin += count
            summed.step(0)

        for at in range(tables_at):
            loads[at].wait()
        for k in range(nkb):

            @pl.loop(0, dp * counts[k] // CHUNK)
            def _(chunk):
                at = pl.multiple_of(dp * lay.starts[k] + chunk * CHUNK, CHUNK)
                part = r.p1_v[0][pl.ds(at, CHUNK), :]
                part = jnp.dot(repeat[...], part, preferred_element_type=FULL).astype(LOW)
                full = jnp.dot(part, spread[...], preferred_element_type=FULL)
                full = full.reshape(CHUNK, size, broad) * same[...].astype(FULL)[None]
                to = pl.multiple_of(chunk * CHUNK * size, CHUNK * size)
                t1[k][pl.ds(to, CHUNK * size), :] = full.reshape(CHUNK * size, broad).astype(LOW)

        if parts:
            summed.step(1)

        for k in range(nkb):
            mine[k].wait()
            settle(f_got.at[k, pl.ds(0, half - 1)], send.at[0], r.f_sem.at[k], False)
            high = counts[k] * size

            def modes_for(peer):
                part = t1[k][pl.ds(pl.multiple_of(peer * high, 16), high), :]
                got = f_got[k].reshape(half * lay.cols, E)
                out = jnp.dot(part, got, preferred_element_type=FULL).astype(LOW)
                return out.reshape(counts[k], size, E)

            @pl.loop(1, dp)
            def _(step):
                peer = lax.rem(me + step, dp)
                s_put[k][peer] = modes_for(peer)
                push(s_put[k].at[peer], s_got[k].at[me], send.at[1], r.s_sem.at[k], peer)

            s_got[k][me] = modes_for(me)

        if parts:
            summed.step(2)
        for k in range(nkb):
            width = CHUNK * size
            count = dp * counts[k]

            @pl.loop(0, count // CHUNK)
            def _(chunk):
                to = pl.ds(pl.multiple_of(chunk * width, width), width)
                part = jnp.dot(
                    r.p2_v[k][...], across[pl.ds(0, count), to], preferred_element_type=FULL
                )
                full = jnp.dot(spread_t[...], part.astype(LOW), preferred_element_type=FULL)
                t2[k][:, to] = (full * wide_same[...].astype(FULL)).astype(LOW)

        if parts:
            summed.step(3)

        for copy in loads[tables_at:]:
            copy.wait()
        def rows_at(group, degree, g):
            tiles = [group[k][:, degree - k * lay.kd] for k in range(g + 1)]
            return jnp.concatenate([t.reshape(dp * size, E) for t in tiles], axis=0)

        if fetch:
            pltpu.make_async_copy(w.at[z], w.at[z], r.own_w.at[0]).wait()
        for g, (begin, length) in enumerate(spans):
            settle(s_got[g].at[pl.ds(0, dp - 1)], send.at[1], r.s_sem.at[g], False)
            span = pl.ds(begin, length)
            if fetch:
                got = w.at[pl.ds(0, ns - 1), span]
                settle(got, r.line_send.at[0], r.line_got.at[g], False)

            @pl.loop(begin, ends[g])
            def _(degree):
                rows_in = rows_at(s_got, degree, g)
                dims = (((1,), (1 if back else 0,)), ((), ()))
                by_real, by_imag = (
                    lax.dot_general(
                        rows_in, w[:, degree, p].reshape(E, E), dims, preferred_element_type=FULL
                    )
                    for p in (0, 1)
                )
                (rr, ir), (ri, ii) = parts_of(by_real), parts_of(by_imag)
                mixed = turned(rr + ii, ir - ri) if back else turned(rr - ii, ri + ir)
                for k in range(g + 1):
                    part = mixed[k * dp * size : (k + 1) * dp * size]
                    m_put[k][:, degree - k * lay.kd] = part.reshape(dp, size, E)

            for k in range(g + 1):
                there = pl.ds(begin - k * lay.kd, length)

                @pl.loop(1, dp)
                def _(step):
                    peer = lax.rem(me + step, dp)
                    target = m_got[k].at[me, there]
                    push(m_put[k].at[peer, there], target, send.at[2], r.m_sem.at[k], peer)

        if back:
            (d_put,) = r.d_put
            for g, (begin, length) in enumerate(spans):
                span = pl.ds(begin, length)

                @pl.loop(begin, ends[g])
                def _(degree):
                    dims = (((0,), (0,)), ((), ()))
                    olds, grads = rows_at(r.old_v, degree, g), rows_at(s_got, degree, g)
                    real, imag = parts_of(grads.astype(FULL))
                    for p, right in ((0, grads), (1, turned(imag, -real))):
                        total = lax.dot_general(olds, right, dims, preferred_element_type=FULL)
                        total = total.reshape(ns, lay.e_plane, E)
                        if last:
                            total = total + r.early_v[0][:, degree, p].astype(FULL)
                        d_put[:, degree, p] = total.astype(LOW)

                if last:
                    (d_got,) = r.d_got

                    @pl.loop(1, ns)
                    def _(step):
                        to = lax.rem(z + step, ns)
                        remote(
                            d_put.at[to, span],
                            d_got.at[z, span],
                            r.line_send.at[0],
                            r.line_got.at[g],
                            line_device(to),
                        ).start()

                    d_got[z, span] = d_put[z, span]

        if parts:
            summed.step(4)
        for k in range(nkb):
            m_got[k][me] = m_put[k][me]
        keeps = []
        for at, (source, target) in enumerate(
            list(zip(s_got, r.keep)) + [(w, t) for t in r.whole] + list(zip(r.d_put, r.d))
        ):
            copy = pltpu.make_async_copy(source, target, own.at[at])
            copy.start()
            keeps.append(copy)

        for k in range(nkb):
            settle(m_got[k].at[pl.ds(0, dp - 1)], send.at[2], r.m_sem.at[k], False)

            def rows_for(peer):
                part = t2[k][pl.ds(pl.multiple_of(peer * lay.cols, 16), lay.cols), :]
                got = m_got[k][...].reshape(-1, E)
                return jnp.dot(part, got, preferred_element_type=FULL).astype(LOW)

            @pl.loop(1, half)
            def _(step):
                peer = lax.rem(mine_at + step, half)
                y_put[peer, k] = rows_for(peer)
                target, sem = y_ref.at[mine_at, k], r.y_sem.at[0]
                remote(y_put.at[peer, k], target, send.at[3], sem, half_device(peer)).start()

            y_put[mine_at, k] = rows_for(mine_at)
        ends_with = pltpu.make_async_copy(y_put.at[mine_at], y_ref.at[mine_at], own.at[nkb + 2])
        ends_with.start()

        if parts:
            summed.step(5)
        if last:
            (g_put,), (g_ref,), (square_v,) = r.g_put, r.g, r.square_v
            square_v[...] = jnp.zeros_like(square_v)
            for g, (begin, length) in enumerate(spans):
                if parts and g == nkb - 1:
                    summed.step(6)
                    pltpu.make_async_copy(every, r.every[0], r.part_sem.at[len(parts)]).start()
                got = d_got.at[pl.ds(0, ns - 1), pl.ds(begin, length)]
                settle(got, r.line_send.at[0], r.line_got.at[g], False)

                @pl.loop(begin * lay.v, ends[g] * lay.v)
                def _(at):
                    degree, s_at = at // lay.v, lax.rem(at, lay.v)
                    for p in (0, 1):
                        total = d_got[s_at, degree, p].astype(FULL)
                        for first_plane in range(lay.v, ns, lay.v):
                            total = total + d_got[first_plane + s_at, degree, p].astype(FULL)
                        folded = (total * total).reshape(-1, 8, E).sum(axis=0)
                        square_v[...] += folded[:, :128] + folded[:, 128:]
                        g_put[at, :, p] = total.astype(LOW).reshape(lay.x, lay.e_dev, E)
                    if lay.even:
                        slot = lax.rem(at, lay.slots)
                        for at_x in range(lay.x):
                            peer = at // lay.slots * lay.x + at_x

                            @pl.when(peer != place_at)
                            def _():
                                remote(
                                    g_put.at[at, at_x],
                                    g_ref.at[place_at, slot],
                                    r.g_sem.at[0],
                                    r.g_sem.at[1],
                                    plane_device(peer),
                                ).start()

            if lay.even:
                copy = pltpu.make_async_copy(
                    g_put.at[pl.ds(n * lay.slots, lay.slots), x], g_ref.at[place_at], own.at[nkb + 3]
                )
            else:
                copy = pltpu.make_async_copy(g_put, g_ref, own.at[nkb + 3])
            copy.start()
            copy.wait()
            copy = pltpu.make_async_copy(square_v, r.squares[0], own.at[nkb + 3])
            copy.start()
            copy.wait()
            if lay.even:
                some = g_ref.at[pl.ds(0, lay.dp - 1)]
                settle(some, r.g_sem.at[0], r.g_sem.at[1], True)
                settle(some, r.g_sem.at[0], r.g_sem.at[1], False)

        if parts:
            pltpu.make_async_copy(every, r.every[0], r.part_sem.at[len(parts)]).wait()
        ends_with.wait()
        for copy in keeps:
            copy.wait()
        settle(f_ref.at[pl.ds(0, half - 1)], send.at[0], r.f_sem.at[0], True)
        for k in range(nkb):
            settle(s_got[k].at[pl.ds(0, dp - 1)], send.at[1], r.s_sem.at[0], True)
            settle(m_got[k].at[pl.ds(0, dp - 1)], send.at[2], r.m_sem.at[0], True)
        if line:
            settle(w.at[pl.ds(0, ns - 1)], r.line_send.at[0], r.line_got.at[0], True)
        if carry:
            swap.wait()
        settle(y_put.at[pl.ds(0, half - 1)], send.at[3], r.y_sem.at[0], True)
        settle(y_put.at[pl.ds(0, half - 1)], send.at[3], r.y_sem.at[0], False)

    spot = pl.BlockSpec(memory_space=pl.ANY)
    operands = [v for group in ins.values() for v in group]
    results = [jax.ShapeDtypeStruct(*v) for group in outs.values() for v in group]
    scratch = [pltpu.VMEM(*v) for group in buffers.values() for v in group]
    need = sum(math.prod(shape[:-1]) * -(-shape[-1] // 128) * 128 * np.dtype(kind).itemsize
               for group in buffers.values() for shape, kind in group)
    scratch += [dma((count,)) for count in sems.values()]
    got = list(
        pl.pallas_call(
            kernel,
            out_shape=results,
            in_specs=[spot] * len(operands),
            out_specs=[spot] * len(results),
            scratch_shapes=scratch,
            compiler_params=pltpu.CompilerParams(
                collective_id=tag,
                has_side_effects=True,
                vmem_limit_bytes=min(58 << 20, need + (10 << 20)),
            ),
            cost_estimate=pl.CostEstimate(
                flops=40_000_000_000, bytes_accessed=100_000_000, transcendentals=0
            ),
            name="spectral_back" if back else "spectral",
        )(*operands)
    )
    given = types.SimpleNamespace()
    for name, entries in outs.items():
        setattr(given, name, got[: len(entries)])
        del got[: len(entries)]
    rows_out = given.y[0].reshape(half, nkb, items, rows, size, E)
    rows_out = rows_out.transpose(2, 3, 0, 1, 4, 5).reshape(items, rows, -1, E)
    return rows_out, given


def prologue(lay, spec_laid, small, swaps, tag):
    def kernel(*refs):
        spec_ref, small_ref = refs[:2]
        swap_refs = refs[2 : 2 + len(swaps)]
        spec_got, small_got = refs[2 + len(swaps) : 4 + len(swaps)]
        swap_got = refs[4 + len(swaps) : 4 + 2 * len(swaps)]
        sent, got, own, swap_sem = refs[4 + 2 * len(swaps) :]
        z, x, n = lay.here()
        _, me, device = group_of(lay, "plane")
        core, y_count, places = n % 2, lay.ns // 2, lay.dp // 2
        place = x * y_count + n // 2
        sibling = (z * lay.x + x, n + 1 - 2 * core)

        def at_plane(q):
            return q * lay.x + x, n

        def at_place(p):
            return z * lay.x + p // y_count, p % y_count * 2 + core

        barrier = pltpu.get_barrier_semaphore()

        def greet(target):
            pl.semaphore_signal(barrier, inc=1, device_id=target, device_id_type=MESH)

        @pl.loop(1, lay.dp)
        def _(step):
            greet(device(lax.rem(me + step, lay.dp)))

        @pl.loop(1, lay.ns)
        def _(step):
            greet(at_plane(lax.rem(z + step, lay.ns)))

        greet_senders(lay, greet)
        pl.semaphore_wait(barrier, lay.dp + lay.ns - 2 + jnp.where(lay.stays(), 1, 2))

        def remote(source, target, at, to):
            return pltpu.make_async_remote_copy(
                src_ref=source,
                dst_ref=target,
                send_sem=sent.at[at],
                recv_sem=got.at[at],
                device_id=to,
                device_id_type=MESH,
            )

        def spec_here():
            if lay.even:
                return spec_got.at[z, pl.ds(n * lay.slots, lay.slots), :, x]
            return spec_got.at[me]

        copy = pltpu.make_async_copy(small_ref, small_got.at[core, z, place], own.at[0])
        copy.start()

        @pl.loop(1, lay.ns)
        def _(step):
            to = at_plane(lax.rem(z + step, lay.ns))
            remote(small_ref, small_got.at[core, z, place], 1, to).start()

        moves = [
            Swap(lay, a, b, [swap_sem.at[at, k] for k in range(3)])
            for at, (a, b) in enumerate(zip(swap_refs, swap_got))
        ]
        for move in moves:
            move.start()
        @pl.loop(1, lay.dp)
        def _(step):
            peer = lax.rem(me + step, lay.dp)
            remote(spec_ref.at[peer], spec_here(), 0, device(peer)).start()

        pltpu.make_async_copy(spec_ref.at[me], spec_here(), got.at[0]).start()
        copy.wait()
        some = small_got.at[core, pl.ds(0, lay.ns - 1), place]
        remote(some, some, 1, sibling).wait()
        column = small_got.at[core, pl.ds(0, lay.ns), place]

        @pl.loop(1, places)
        def _(step):
            remote(column, column, 3, at_place(lax.rem(place + step, places))).start()

        some = small_got.at[core, pl.ds(0, lay.ns), pl.ds(0, places - 1)]
        remote(some, some, 3, sibling).wait()
        remote(small_got.at[core], small_got.at[core], 2, sibling).start()
        some = spec_ref.at[pl.ds(0, lay.dp - 1)]
        every = spec_got.at[z] if lay.even else spec_got
        remote(every, every, 0, sibling).wait_recv()
        remote(some, some, 0, sibling).wait_send()
        remote(small_got.at[core], small_got.at[core], 2, sibling).wait()
        for move in moves:
            move.wait()

    spot = pl.BlockSpec(memory_space=pl.ANY)
    w_shape = (lay.ns, lay.lall, 2, lay.x, lay.e_dev, E)
    spec_shape = jax.ShapeDtypeStruct(w_shape, LOW) if lay.even else spec_laid
    small_shape = (2, lay.ns, lay.dp // 2) + small.shape
    outs = [spec_shape, jax.ShapeDtypeStruct(small_shape, small.dtype), *swaps]
    count = 4
    got = pl.pallas_call(
        kernel,
        out_shape=[jax.ShapeDtypeStruct(o.shape, o.dtype) for o in outs],
        in_specs=[spot] * (2 + len(swaps)),
        out_specs=[spot] * len(outs),
        scratch_shapes=[
            pltpu.SemaphoreType.DMA((count,)),
            pltpu.SemaphoreType.DMA((count,)),
            pltpu.SemaphoreType.DMA((2,)),
            pltpu.SemaphoreType.DMA((len(swaps), 3)),
        ],
        compiler_params=pltpu.CompilerParams(collective_id=tag, has_side_effects=True),
        name="prologue",
    )(spec_laid, small, *swaps)
    every = jnp.moveaxis(got[1], 0, 2).reshape((lay.dp * lay.ns,) + small.shape)
    return got[0], every, list(got[2:])


def spec_out(lay, spec):
    z, x, n = lay.here()
    low = spec.astype(LOW).transpose(1, 2, 0, 3)
    tail = (2, lay.e_dev, E)
    if lay.even:
        laid = low.reshape((lay.slots, lay.dp) + tail).swapaxes(0, 1)
    else:
        at = (jnp.arange(lay.dp) - lay.lns * n) % lay.dp
        at = at[:, None] + lay.dp * jnp.arange(lay.slots)
        laid = jnp.take(low, jnp.minimum(at, lay.lns - 1), axis=0)
    return laid


def spec_in(lay, got):
    z, x, n = lay.here()
    if lay.even:
        return got.reshape(lay.ns, lay.lall, 2, lay.e_plane, E)
    member = n * lay.x + x
    got = got.reshape((lay.ns, lay.x, lay.slots, 2, lay.e_dev, E))
    got = got.transpose(0, 2, 3, 1, 4, 5).reshape(lay.ns, lay.slots, 2, lay.e_plane, E)
    degree = lay.dp * jnp.arange(lay.lall) + member
    return got[degree // lay.lns, degree % lay.lns // lay.dp]


def spec_home(lay, given, tag):
    z, x, n = lay.here()
    member = n * lay.x + x
    if lay.even:
        mine = given.swapaxes(0, 1).reshape(lay.lns, 2, lay.e_dev, E)
        return mine.transpose(2, 0, 1, 3)
    first = (member - lay.lns * jnp.arange(lay.ns)) % lay.dp + lay.lns * jnp.arange(lay.ns)
    at = (first[:, None] + lay.dp * jnp.arange(lay.slots) - member) // lay.dp
    slots = given[jnp.clip(at, 0, lay.lall - 1)]
    slots = slots.transpose(0, 2, 1, 3, 4, 5)
    (back,) = exchange(lay, [slots.reshape(lay.dp, -1, E)], ["each"], "plane", tag)
    back = back.reshape(lay.dp, lay.slots, 2, lay.e_dev, E)
    degree = lay.lns * n + jnp.arange(lay.lns)
    source = degree % lay.dp
    slot = (jnp.arange(lay.lns) - (source - lay.lns * n) % lay.dp) // lay.dp
    return back[source, slot].transpose(2, 0, 1, 3)


def pad_rows(values, rows):
    return jnp.pad(values, ((0, 0),) * (values.ndim - 2) + ((0, rows - values.shape[-2]), (0, 0)))


def wide(values):
    return jnp.pad(values, ((0, 0),) * (values.ndim - 1) + ((0, 128 - values.shape[-1]),))


def forward_block(lay, residual, weights, tables, tag, fetch, carry):
    spec_w, up_w, down_w, gain_low = weights
    gain_vec = gain_low.astype(FULL)
    dft_fwd, dft_inv, quad_tab, plain_tab, ones = tables
    normed_a = normalize(residual, gain_vec[:, 0]).astype(LOW)
    fourier = jnp.einsum("brke,kq->brqe", normed_a, dft_fwd, preferred_element_type=FULL)
    restored, given = spectral(
        lay, fourier.astype(LOW), quad_tab[0], plain_tab[1], ones, tag, spec_w, fetch, carry
    )
    middle = residual + jnp.einsum(
        "brqe,kq->brke", restored, dft_inv, preferred_element_type=FULL
    )
    normed_b = normalize(middle, gain_vec[:, 1]).astype(LOW)
    pre_act = jnp.einsum("brke,fe->brkf", normed_b, up_w, preferred_element_type=FULL)
    hidden = jax.nn.gelu(pre_act).astype(LOW)
    output = middle + jnp.einsum("brkf,fe->brke", hidden, down_w, preferred_element_type=FULL)
    return (output, (residual, given.keep, middle, normed_b, pre_act, hidden), given)


def backward_block(
    lay, output_gradient, saved, weights, tables, tag, earlier, carry, sums, closing, low_grad, aside
):
    residual, spectrum, middle, normed_b, pre_act, hidden = saved
    spec_w, up_w, down_w, gain_low = weights
    gain_vec = gain_low.astype(FULL)
    dft_fwd, dft_inv, quad_tab, plain_tab, ones = tables
    g_out = output_gradient.astype(LOW)
    d_hidden = jnp.einsum("brke,fe->brkf", g_out, down_w, preferred_element_type=FULL)
    d_pre = jax.vjp(jax.nn.gelu, pre_act)[1](d_hidden)[0].astype(LOW)
    d_normed_b = jnp.einsum("brkf,fe->brke", d_pre, up_w, preferred_element_type=FULL)
    d_mid_part, d_gain_b = jax.vjp(normalize, middle, gain_vec[:, 1])[1](d_normed_b)
    d_middle = output_gradient + d_mid_part
    d_restored = jnp.einsum(
        "brke,kq->brqe", d_middle.astype(LOW), dft_inv, preferred_element_type=FULL
    ).astype(LOW)
    products = [
        jnp.einsum("brkf,brke->fe", a, b, preferred_element_type=FULL)
        for a, b in ((d_pre, normed_b), (hidden, g_out), (closing, low_grad))
    ]
    sums = [a + b for a, b in zip(sums, products)] if sums else products
    d_restored, sums = lax.optimization_barrier((d_restored, sums))
    d_fourier, given = spectral(
        lay,
        d_restored,
        plain_tab[0],
        quad_tab[1],
        ones,
        tag,
        spec_w,
        carry=carry,
        saved=spectrum,
        earlier=earlier,
        parts=sums if aside and earlier else (),
    )
    d_normed_a = jnp.einsum("brqe,kq->brke", d_fourier, dft_fwd, preferred_element_type=FULL)
    d_res_part, d_gain_a = jax.vjp(normalize, residual, gain_vec[:, 0])[1](d_normed_a)
    d_gain = jnp.stack([d_gain_a, d_gain_b], axis=1)
    sums = given.every or sums
    return d_middle + d_res_part, given, sums, d_gain


def product(left, right, dims):
    parts = []
    for value in (left, right):
        high = value.astype(LOW)
        parts.append((high, (value - high.astype(FULL)).astype(LOW)))
    (a, a_rest), (b, b_rest) = parts

    def dot(p, q):
        return lax.dot_general(p, q, (dims, ((), ())), preferred_element_type=FULL)

    return dot(a, b) + (dot(a, b_rest) + dot(a_rest, b))


def finish(lay, blocks, given, moments, extra, own, ff_dev, e_own, tag):
    planes, places, pack = moments.shape[1:4]
    count = 2 * places * planes
    at_enc = 0 if given else 2 * ff_dev
    rows, lanes = blocks.shape[3:]

    def kernel(blocks_ref, moment_ref, extra_ref, *refs):
        given_ref = refs[0] if given else None
        refs = refs[len(given) :]
        own_refs, refs = refs[: len(own)], refs[len(own) :]
        every_ref, scalars_ref = refs[:2]
        new_refs, scratch = refs[2 : 2 + len(results)], refs[2 + len(results) :]
        mats, sent, came = scratch[5 : 5 + len(mat_shapes)], scratch[-2], scratch[-1]
        summed = Total(lay, blocks_ref, every_ref, scratch[:5], sent, came)
        barrier = pltpu.get_barrier_semaphore()

        def greet(target):
            pl.semaphore_signal(barrier, inc=1, device_id=target, device_id_type=MESH)

        pl.semaphore_wait(barrier, summed.greet(greet))
        for stage in range(7):
            summed.step(stage, extra_ref[...])

        every = every_ref[...].reshape(count, rows, lanes)
        row = lax.broadcasted_iota(jnp.int32, (rows, lanes), 0)
        lane = lax.broadcasted_iota(jnp.int32, (rows, lanes), 1)
        enc_rows = jnp.logical_and(row >= at_enc, row < at_enc + e_own)
        added = jnp.logical_and(enc_rows, jnp.logical_or(lane == C + 2, lane == C + 3))
        squares = jnp.sum(jnp.where(added[None], 0.0, every * every), axis=0)
        owned = jnp.logical_and(row == at_enc, lane == C + 3)
        squares = squares + jnp.where(owned, jnp.sum(every, axis=0), 0.0)
        squares = jnp.sum(squares, keepdims=True)
        if given:
            sums = given_ref[...].reshape(count, pack, E)
            squares = squares + jnp.sum(jnp.sum(sums * sums, axis=0), keepdims=True)
        norm = jnp.sqrt(squares)
        clip = CLIP_NORM / jnp.maximum(norm, CLIP_NORM)
        at_lane = lax.broadcasted_iota(jnp.int32, (8, 128), 1)
        loss = every[0, at_enc : at_enc + 1, C + 2 : C + 3]
        scalars_ref[...] = jnp.where(at_lane == 0, norm, jnp.where(at_lane == 1, clip, loss))

        old = moment_ref[...].reshape(count, pack, E)
        if given:

            def new(begin, size, grads, first=0, width=E):
                own = old[:, begin : begin + size, first : first + width].reshape(-1, width)
                return MOMENTUM * own + clip * grads.reshape(-1, width)

            near = lax.broadcasted_iota(jnp.int32, (e_own, 128), 1) < C
            enc_sums = jnp.where(near[None], every, 0.0)
            starts = [new(at, ff_dev, sums[:, at : at + ff_dev]) for at in (0, ff_dev)]
            starts.append(new(2 * ff_dev, e_own, enc_sums, 0, 128))
            starts.append(new(2 * ff_dev, e_own, sums[:, 2 * ff_dev :, :128], 128, 128))
        else:
            moment = MOMENTUM * old + clip[None] * every

            def rows_of(begin, size):
                inside = jnp.logical_and(row >= begin, row < begin + size)
                return jnp.where(inside[None], moment, 0.0).reshape(-1, E)

            both = rows_of(at_enc, e_own)
            near = lax.broadcasted_iota(jnp.int32, (both.shape[0], 128), 1) < C
            starts = [rows_of(0, ff_dev), rows_of(ff_dev, ff_dev)]
            starts += [jnp.where(near, both[:, :128], 0.0), both[:, 128:]]
        if given:
            first = summed.core == 0
            starts = [jnp.where(first, starts[k], starts[k + 1]) for k in (0, 2)]
        for start, out in zip(starts, mats):
            square = jnp.sum(start * start, keepdims=True)
            out[...] = start / (jnp.sqrt(square) + 1e-07)

        @pl.loop(0, NS_ITERS)
        def _(sweep):
            for out in mats[: len(starts)]:
                matrix = out[...]
                gram_mat = product(matrix, matrix, ((0,), (0,)))
                square = product(gram_mat, gram_mat, ((1,), (0,)))
                poly = NS_SECOND * gram_mat + NS_THIRD * square
                out[...] = NS_FIRST * matrix + product(matrix, poly, ((1,), (0,)))

        if not given:
            up, down, enc, dec = (m[...] for m in mats)
            both = jnp.concatenate([enc, dec], axis=1)
            new_refs[0][...] = (up + down + both).reshape((2, planes, places, pack, E))
            return
        tall, flat, give_tall, give_flat, got_tall, got_flat = mats
        core, z = summed.core, summed.z

        def block_at(c, p):
            return (c * planes + z) * places + p

        def rows_at(ref, block, size):
            return ref[pl.ds(pl.multiple_of(block * size, 8), size), :]

        give_tall[...] = rows_at(tall, block_at(1 - core, summed.place), ff_dev)
        enc_at = [(k % 2, summed.x * summed.y_count + k // 2) for k in range(planes)]
        for k, (c, p) in enumerate(enc_at):
            give_flat[pl.ds(k * e_own, e_own), :] = rows_at(flat, block_at(c, p), e_own)
        copies = [
            summed.remote(give_tall, got_tall, 6, summed.at_core()),
            summed.remote(give_flat, got_flat, 7, summed.at_core()),
        ]
        for copy in copies:
            copy.start()
        for copy in copies:
            copy.wait()
        mine = rows_at(tall, block_at(core, summed.place), ff_dev)
        steps = [(mine, got_tall[...]), (give_flat[...], got_flat[...])]
        own_sums = given_ref[core, z, summed.place]
        flat_sums = [
            jnp.concatenate([given_ref[c, z, p, 2 * ff_dev :, :128] for c, p in enc_at], axis=0),
            jnp.concatenate([every_ref[c, z, p] for c, p in enc_at], axis=0),
        ]
        grads = [own_sums[:ff_dev], own_sums[ff_dev : 2 * ff_dev]]
        grads += [flat_sums[1][:, :C], flat_sums[0][:, :C]]
        for at in range(4):
            here, there = steps[at // 2]
            step = jnp.where(first, here, there) if at % 2 == 0 else jnp.where(first, there, here)
            factor = RATE_MUON * math.sqrt(max(1.0, FF / E if at < 2 else E / C))
            master, moment = own_refs[2 * at][...], own_refs[2 * at + 1][...]
            moment = MOMENTUM * moment + clip * grads[at]
            new_refs[2 * at][...] = moment
            decayed = master * (1.0 - RATE_MUON * DECAY)
            new_refs[2 * at + 1][...] = decayed - factor * step[:, : master.shape[1]]
        gain, gain_m, gain_v = (ref[...] for ref in own_refs[8:])
        new = adam_step(gain, gain_m, gain_v, clip * flat_sums[1][:, C : C + 2], RATE_GAIN)
        for ref, value in zip(new_refs[8:], new):
            ref[...] = value

    if given:
        e_dev = lay.e_dev
        mat_shapes = [(FF, E), (E, 128)] + [(ff_dev, E), (e_dev, 128)] * 2
        results = [(v.shape, FULL) for v in own]
        results = [jax.ShapeDtypeStruct(*r) for r in results]
    else:
        mat_shapes = [(count * pack, E)] * 2 + [(count * pack, 128)] * 2
        results = [jax.ShapeDtypeStruct(moments.shape, FULL)]
    fast = pl.BlockSpec(memory_space=pltpu.VMEM)
    sums = [jax.ShapeDtypeStruct(blocks.shape, FULL), jax.ShapeDtypeStruct((8, 128), FULL)]
    got = pl.pallas_call(
        kernel,
        out_shape=sums + results,
        in_specs=[fast] * (3 + len(given) + len(own)),
        out_specs=[fast] * (2 + len(results)),
        scratch_shapes=[
            *Total.scratch(blocks.shape),
            *[pltpu.VMEM(m, FULL) for m in mat_shapes],
            pltpu.SemaphoreType.DMA((8,)),
            pltpu.SemaphoreType.DMA((8,)),
        ],
        compiler_params=pltpu.CompilerParams(
            collective_id=tag, has_side_effects=True, vmem_limit_bytes=56 << 20
        ),
        name="finish",
    )(blocks, moments, extra, *given, *own)
    return got[0], got[1], list(got[2:])


def natural(values):
    order = tuple(range(values.ndim))
    return with_layout_constraint(values, DeviceLayout(major_to_minor=order))


def adam_step(weight, moment_a, moment_b, gradient, step_rate):
    moment_a = BETA_FIRST * moment_a + (1.0 - BETA_FIRST) * gradient
    moment_b = BETA_SECOND * moment_b + (1.0 - BETA_SECOND) * gradient * gradient
    corrected_a = moment_a / (1.0 - BETA_FIRST**STEP)
    corrected_b = moment_b / (1.0 - BETA_SECOND**STEP)
    return (
        moment_a,
        moment_b,
        weight - step_rate * (corrected_a / (jnp.sqrt(corrected_b) + 1e-08) + DECAY * weight),
    )


def local(
    fields,
    targets,
    valid,
    var_class,
    enc_t,
    enc_mom,
    dec,
    dec_mom,
    spec,
    spec_m,
    spec_v,
    up_t,
    up_mom,
    down,
    down_mom,
    gains,
    gain_m,
    gain_v,
):
    dp_count, ns_count = lax.axis_size("dp"), lax.axis_size("ns")
    devices = dp_count * ns_count
    lay = Layout(dp_count, ns_count, fields.shape[0], fields.shape[1])
    z, x, n = lay.here()
    lat_count = lay.block_rows * dp_count

    ff_dev, e_own = up_t.shape[1], E // devices
    pack = -(-(2 * ff_dev + 2 * e_own) // 16) * 16

    def mine(values):
        return lax.dynamic_slice_in_dim(values, n * e_own, e_own, 0)

    def packed(up, down_, enc, dec_, extra):
        both = jnp.concatenate([wide(mine(enc)), wide(mine(dec_))], axis=1)
        return pad_rows(jnp.concatenate([up[0], down_[0], both, extra], axis=0), pack)

    def unpacked(every):
        up = every[:, :ff_dev].reshape(FF, E)
        down_ = every[:, ff_dev : 2 * ff_dev].reshape(FF, E)
        both = every[:, 2 * ff_dev : 2 * ff_dev + e_own].reshape(E, E)
        extra = every[:, 2 * ff_dev + e_own : 2 * ff_dev + 2 * e_own]
        return up, down_, both[:, :128], both[:, 128:], extra

    gain_rows = jnp.pad(mine(gains[0]), ((0, 0), (0, E - 2)))
    small = packed(up_t, down, enc_t, dec, gain_rows).astype(LOW)
    lon_count = fields.shape[2]

    def dense(values):
        fill = (-values.shape[-1] % 16, -lon_count % 128)
        values = values.transpose(0, 1, 3, 2)
        return jnp.pad(values, ((0, 0), (0, 0), (0, fill[0]), (0, fill[1])))

    def usual(values, count=C):
        values = values[:, :, :count, :lon_count].reshape((1, lay.rows, count, lon_count))
        return values.transpose(0, 1, 3, 2)

    swaps = [dense(fields), jnp.pad(valid, ((0, 0), (0, 0), (0, -lon_count % 128)))]
    spec_got, every_low, swaps = prologue(lay, spec_out(lay, spec[0]), small, swaps, 0)
    fields = usual(swaps[0])
    valid = swaps[1][..., :lon_count].reshape(1, lay.rows, lon_count)
    targets = [dense(targets[step]) for step in range(2)]
    up_w, down_w, enc_w, dec_w, extra = unpacked(every_low)
    enc_w, dec_w = enc_w[:, :C], dec_w[:, :C]
    gain_w = extra.reshape(E, E)[:, :2]
    spec_w = spec_in(lay, spec_got)

    colatitude = math.pi * (np.arange(lat_count) + 0.5) / lat_count
    sines = jnp.asarray(np.sin(colatitude).astype(np.float32).reshape(dp_count, lay.block_rows))
    local_sine = jnp.concatenate([sines[at] for at in lay.row_blocks(n, x)])
    var_weight = 1.0 + 0.5 * var_class.astype(FULL)
    pixel_map = valid.astype(FULL) * local_sine[None, :, None]
    weight_part = jnp.sum(pixel_map)
    weight_map = pixel_map[..., None] * var_weight
    weight_rows = jnp.broadcast_to(weight_part, (e_own, E))
    every_mom = lax.all_gather(packed(up_mom, down_mom, enc_mom, dec_mom, weight_rows), BOTH)
    loss_weight = jnp.sum(every_mom[:, 2 * ff_dev + e_own, 0]) * jnp.sum(var_weight)
    core_pack = -(-(2 * ff_dev + e_own) // 8) * 8

    def by_core(values):
        values = values.reshape((ns_count, dp_count // 2, 2) + values.shape[1:])
        return jnp.moveaxis(values, 2, 0)

    def by_device(values):
        return jnp.moveaxis(values, 0, 2).reshape((devices,) + values.shape[3:])

    moments = by_core(pad_rows(every_mom[:, : 2 * ff_dev + e_own], core_pack))

    tables = dft_tables(lay, fields.shape[2]) + legendre_tables(lay, lat_count)
    incoming = fields
    saved = []
    forecasts = []
    for step in range(2):
        weights = (spec_w, up_w, down_w, gain_w)
        hidden = jnp.einsum("brkc,ec->brke", incoming, enc_w, preferred_element_type=FULL)
        fetch, carry = ((True,), ()) if step == 0 else ((), (targets[1],))
        hidden, kept, given = forward_block(lay, hidden, weights, tables, 1 + step, fetch, carry)
        if step == 0:
            (spec_w,) = given.whole
        else:
            targets[1] = usual(given.carried[0])
        closing = hidden.astype(LOW)
        forecast = jnp.einsum("brke,ec->brkc", closing, dec_w, preferred_element_type=FULL)
        saved.append((incoming, kept, closing))
        forecasts.append(forecast)
        incoming = forecast.astype(LOW)

    def loss_of(step):
        error = forecasts[step] - targets[step].astype(FULL)
        return jnp.sum(weight_map * error * error), 2.0 * weight_map * error / loss_weight

    last_loss, gradient = loss_of(1)
    early, d_spec = (), ()
    aside = ff_dev % 8 == 0 and e_own % 8 == 0
    carry = (targets[0],)
    for step in (1, 0):
        incoming, kept, closing = saved[step]
        low_grad = gradient.astype(LOW)
        gradient = jnp.einsum("brkc,ec->brke", low_grad, dec_w, preferred_element_type=FULL)
        gradient, given, early, d_gain = backward_block(
            lay,
            gradient,
            kept,
            weights,
            tables,
            4 - step,
            d_spec,
            carry,
            early,
            closing,
            low_grad,
            aside,
        )
        d_spec, carry = given.d + given.g, ()
        squares = given.squares[0] if given.squares else None
        low_grad = gradient.astype(LOW)
        d_enc = jnp.einsum("brkc,brke->ec", incoming, low_grad, preferred_element_type=FULL)
        if step == 1:
            late = (d_gain, d_enc)
            targets[0] = usual(given.carried[0])
            first_loss, gradient = loss_of(0)
            gradient = gradient + jnp.einsum(
                "brke,ec->brkc", low_grad, enc_w, preferred_element_type=FULL
            )
            loss_local = first_loss + last_loss
    d_gain, d_enc = late[0] + d_gain, late[1] + d_enc
    g_spec = natural(spec_home(lay, d_spec[0], 5).astype(FULL)[None])
    near = jnp.concatenate([d_enc, d_gain, jnp.broadcast_to(loss_local, (E, 1))], axis=1)
    near = wide(near).reshape(devices, e_own, 128)
    if aside:
        blocks, given, at_enc = by_core(near), early, 0
    else:
        d_up, d_down, d_dec = early
        both = jnp.concatenate([near, wide(d_dec).reshape(near.shape)], axis=-1)
        blocks = [d_up.reshape(devices, ff_dev, E), d_down.reshape(devices, ff_dev, E), both]
        blocks = by_core(pad_rows(jnp.concatenate(blocks, axis=1), core_pack))
        given, at_enc = [], 2 * ff_dev
    at_row = jnp.arange(blocks.shape[3])[:, None] == at_enc
    at_lane = at_row & (jnp.arange(blocks.shape[4])[None, :] == C + 3)
    extra = jnp.where(at_lane, jnp.sum(squares), 0.0)
    masters = [up_t[0], up_mom[0], down[0], down_mom[0], enc_t, enc_mom, dec, dec_mom]
    own = masters + [gains[0], gain_m[0], gain_v[0]] if aside else []
    every, scalars, new = finish(lay, blocks, given, moments, extra, own, ff_dev, e_own, 6)
    grad_norm, clip_scale, loss_sum = scalars[0, 0], scalars[0, 1], scalars[0, 2]
    if not aside:
        (matrices,) = new
        d = lax.axis_index("dp")
        place = x * (ns_count // 2) + n // 2

        def enc_block(values):
            both = by_device(values[:, :, :, at_enc : at_enc + e_own])
            both = both.reshape(dp_count, lay.e_dev, E)
            return lax.dynamic_index_in_dim(both, d, keepdims=False)

        def muon(master, moment, gradient, matrix, factor):
            moment = MOMENTUM * moment + clip_scale * gradient
            return moment, master * (1.0 - RATE_MUON * DECAY) - RATE_MUON * (matrix * factor)

        grad, step = every[n % 2, z, place], matrices[n % 2, z, place]
        both_grad, both_step = enc_block(every), enc_block(matrices)
        new = []
        for at in range(4):
            begin = (0, ff_dev, 0, 128)[at]
            rows, columns = (FF, E) if at < 2 else (E, C)
            if at < 2:
                g, m = grad[begin : begin + ff_dev], step[begin : begin + ff_dev]
            else:
                g, m = both_grad[:, begin : begin + C], both_step[:, begin : begin + C]
            factor = math.sqrt(max(1.0, rows / columns))
            new += muon(masters[2 * at], masters[2 * at + 1], g, m, factor)
        g_gain = clip_scale * both_grad[:, C : C + 2]
        new += adam_step(gains[0], gain_m[0], gain_v[0], g_gain, RATE_GAIN)
    up_mom_new, up_new, down_mom_new, down_new = (v[None] for v in new[:4])
    enc_mom_new, enc_new, dec_mom_new, dec_new = new[4:8]
    gain_m_new, gain_v_new, gain_new = (v[None] for v in new[8:])
    spec_m_new, spec_v_new, spec_new = adam_step(
        spec, spec_m, spec_v, clip_scale * g_spec, RATE_SPECTRAL
    )
    return (
        loss_sum,
        loss_weight,
        grad_norm,
        enc_mom_new,
        enc_new,
        dec_mom_new,
        dec_new,
        up_mom_new,
        up_new,
        down_mom_new,
        down_new,
        spec_m_new,
        spec_v_new,
        spec_new,
        spec_new.astype(LOW),
        gain_m_new,
        gain_v_new,
        gain_new,
    )


def solution(mesh):
    rows = P(None, BOTH, None)
    shard = P("dp", None)
    whole = P(None, "dp", "ns", None, None)
    gain = P(None, "dp", None)
    placed = (
        P("ns", "dp", None, None),
        P(None, "ns", "dp", None, None),
        P("ns", "dp", None),
        P(),
        *[shard] * 4,
        *[whole] * 3,
        *[rows] * 4,
        *[gain] * 3,
    )
    return jax.shard_map(
        local,
        mesh=mesh,
        in_specs=placed,
        out_specs=(P(), P(), P(), *[shard] * 4, *[rows] * 4, *[whole] * 4, *[gain] * 3),
        check_vma=False,
    )
```

```python
import math
import types

import jax
import jax.numpy as jnp
import ml_dtypes
import numpy as np
from jax import lax
from jax.experimental import pallas as pl
from jax.experimental.layout import Layout as DeviceLayout
from jax.experimental.layout import with_layout_constraint
from jax.experimental.pallas import tpu as pltpu
from jax.sharding import PartitionSpec as P

E = 256
FF = 512
C = 73
LDEG = 96
MM = 96
NL = 1
NS_ITERS = 5
STEP = 10

EXACT = lax.Precision.HIGHEST
EPSILON = 1e-06
CLIP_NORM = 0.02
RATE_SPECTRAL = 0.05
RATE_GAIN = 0.1
RATE_MUON = 0.5
BETA_FIRST = 0.9
BETA_SECOND = 0.999
MOMENTUM = 0.95
DECAY = 0.01
NS_FIRST = 3.4445
NS_SECOND = -4.775
NS_THIRD = 2.0315
LOW = jnp.bfloat16
FULL = jnp.float32
MESH = pl.DeviceIdType.MESH
CHUNK = 16
BOTH = ("dp", "ns")


class Layout:
    def __init__(self, dp, ns, items, rows):
        self.dp, self.ns = dp, ns
        self.x, self.half, self.g = dp // ns, ns // 2, dp // 2
        self.block_rows, self.rows = rows, 2 * rows
        self.v = 2 if LDEG % (2 * dp) == 0 else 1
        self.owners = self.v * dp
        self.kper, self.lns = MM // self.g, LDEG // ns
        self.lper, self.lall = LDEG // self.owners, LDEG // dp
        self.kb = 8
        self.kd = self.kb * self.g // self.owners
        self.nkb = -(-self.kper // self.kb)
        self.blocks = [[i for i in range(self.lper) if i >= k * self.kd] for k in range(self.nkb)]
        self.counts = [len(b) for b in self.blocks]
        self.starts = np.cumsum([0] + self.counts).tolist()
        self.size = 2 * self.kb
        self.cols = self.rows * self.size
        self.ends = [min((k + 1) * self.kd, self.lper) for k in range(self.nkb)]
        self.ends[-1] = self.lper
        self.slots = -(-self.lns // dp)
        self.even = self.lns % dp == 0
        self.e_dev = E // dp
        self.e_plane = self.x * self.e_dev

    def here(self):
        d, n = lax.axis_index("dp"), lax.axis_index("ns")
        return d // self.x, d % self.x, n

    def row_blocks(self, n, x):
        return [(2 * (n % self.half) + s) * self.x + x for s in (0, 1)]

    def item_goes(self, at):
        z, x, n = self.here()
        plane = 2 * (n % self.half) + at
        to = n // self.half * self.half + z // 2
        return (plane * self.x + x, to), jnp.logical_and(plane == z, to == n)

    def item_comes(self, slot):
        z, x, n = self.here()
        return ((2 * (n % self.half) + slot) * self.x + x, n // self.half * self.half + z // 2)

    def stays(self):
        z, x, n = self.here()
        return z // 2 == n % self.half


def group_of(lay, kind):
    z, x, n = lay.here()
    if kind == "plane":
        return lay.dp, n * lay.x + x, lambda p: (z * lay.x + p % lay.x, p // lay.x)
    if kind == "owners":
        base = z // lay.v * lay.v
        return (
            lay.owners,
            (z - base) * lay.dp + n * lay.x + x,
            lambda p: ((base + p // lay.dp) * lay.x + p % lay.x, p % lay.dp // lay.x),
        )
    if kind == "half":
        first = n // lay.half * lay.half
        return (
            lay.g,
            n % lay.half * lay.x + x,
            lambda q: (z * lay.x + q % lay.x, first + q // lay.x),
        )
    return lay.ns, z, lambda q: (q * lay.x + x, n)


def exchange(lay, arrays, kinds, group, tag):
    count = {"plane": lay.dp, "line": lay.ns}[group]

    def kernel(*refs):
        total = len(arrays)
        ins, outs = refs[:total], refs[total : 2 * total]
        send, recv, own = refs[2 * total :]
        size, me, device = group_of(lay, group)
        barrier = pltpu.get_barrier_semaphore()

        @pl.loop(1, size)
        def _(step):
            pl.semaphore_signal(
                barrier, inc=1, device_id=device(lax.rem(me + step, size)), device_id_type=MESH
            )

        pl.semaphore_wait(barrier, size - 1)

        @pl.loop(1, size)
        def _(step):
            peer = lax.rem(me + step, size)
            for at in range(total):
                pltpu.make_async_remote_copy(
                    src_ref=ins[at].at[peer] if kinds[at] == "each" else ins[at],
                    dst_ref=outs[at].at[me],
                    send_sem=send.at[at],
                    recv_sem=recv.at[at],
                    device_id=device(peer),
                    device_id_type=MESH,
                ).start()

        for at in range(total):
            mine = ins[at].at[me] if kinds[at] == "each" else ins[at]
            copy = pltpu.make_async_copy(mine, outs[at].at[me], own)
            copy.start()
            copy.wait()
        for at in range(total):
            some = outs[at].at[pl.ds(0, size - 1)]
            pltpu.make_async_remote_copy(
                src_ref=some,
                dst_ref=some,
                send_sem=send.at[at],
                recv_sem=recv.at[at],
                device_id=device(lax.rem(me + 1, size)),
                device_id_type=MESH,
            ).wait()

    shapes = [
        jax.ShapeDtypeStruct(a.shape if k == "each" else (count,) + a.shape, a.dtype)
        for a, k in zip(arrays, kinds)
    ]
    spot = pl.BlockSpec(memory_space=pl.ANY)
    return pl.pallas_call(
        kernel,
        out_shape=shapes,
        in_specs=[spot] * len(arrays),
        out_specs=[spot] * len(arrays),
        scratch_shapes=[
            pltpu.SemaphoreType.DMA((len(arrays),)),
            pltpu.SemaphoreType.DMA((len(arrays),)),
            pltpu.SemaphoreType.DMA,
        ],
        compiler_params=pltpu.CompilerParams(collective_id=tag, has_side_effects=True),
        name=f"exchange_{group}_{tag}",
    )(*arrays)


def legendre(lat_count):
    colatitude = math.pi * (np.arange(lat_count) + 0.5) / lat_count
    cosine, log_sine = np.cos(colatitude)[None, :], np.log(np.sin(colatitude))[None, :]
    orders = np.arange(MM, dtype=np.float64)
    ladder = np.arange(1, MM, dtype=np.float64)
    sums = np.concatenate([[0.0], np.cumsum(np.log((2 * ladder - 1) / (2 * ladder)))])
    diagonal = np.exp(
        (0.5 * np.log((2 * orders + 1) / (4 * math.pi)) + 0.5 * sums)[:, None]
        + orders[:, None] * log_sine
    )
    table = np.zeros((LDEG, MM, lat_count))
    for degree in range(LDEG):
        for order in range(min(degree, MM - 1) + 1):
            if degree == order:
                table[degree, order] = diagonal[order]
                continue
            a = math.sqrt((4.0 * degree**2 - 1) / (degree**2 - order**2))
            value = cosine[0] * table[degree - 1, order]
            if degree >= 2:
                b = math.sqrt(
                    max((degree - 1.0) ** 2 - order**2, 0) / (4 * (degree - 1.0) ** 2 - 1)
                )
                value = value - b * table[degree - 2, order]
            table[degree, order] = a * value
    return table.astype(np.float32)


def low_table(values):
    return values.astype(np.float32).astype(ml_dtypes.bfloat16)


def dft_tables(lay, lon_count):
    turns = np.arange(lon_count)[:, None] * np.arange(MM)[None, :] % lon_count
    phases = 2 * math.pi / lon_count * turns
    paired = np.stack([np.cos(phases), -np.sin(phases)], axis=2)
    weight = np.where(np.arange(MM) == 0, 1.0, 2.0)
    forward = paired * (2 * math.pi / lon_count)
    inverse = paired * weight[None, :, None] / (2 * math.pi)

    def order(table):
        table = table.reshape(lon_count, lay.kper, lay.g, 2).transpose(0, 2, 1, 3)
        pad = lay.nkb * lay.kb - lay.kper
        table = np.pad(table, ((0, 0), (0, 0), (0, pad), (0, 0)))
        return low_table(table.reshape(lon_count, -1))

    return order(forward), order(inverse)


def legendre_tables(lay, lat_count):
    plain = legendre(lat_count)
    colatitude = math.pi * (np.arange(lat_count) + 0.5) / lat_count
    quadrature = 2 * math.pi * math.pi / lat_count * np.sin(colatitude)
    pad = lay.nkb * lay.kb - lay.kper

    def own(table):
        table = table.reshape(lay.lper, lay.owners, lay.kper, lay.g, lat_count)
        table = np.pad(table.transpose(3, 1, 0, 2, 4), ((0, 0), (0, 0), (0, 0), (0, pad), (0, 0)))
        table = low_table(table)
        blocks = []
        for k in range(lay.nkb):
            part = table[:, :, k * lay.kd :, k * lay.kb : (k + 1) * lay.kb]
            blocks.append(part.reshape(lay.g, -1, lay.kb * lat_count))
        across = [jnp.asarray(np.ascontiguousarray(b.swapaxes(1, 2))) for b in blocks]
        return jnp.asarray(np.concatenate(blocks, axis=1)), across

    col = np.arange(lay.g * lay.cols)
    col_part, col_k = col % 2, col // 2 % lay.kb
    member, row = col // lay.cols, col // lay.size % lay.rows
    block = (2 * (member // lay.x) + row // lay.block_rows) * lay.x + member % lay.x
    col_lat = block * lay.block_rows + row % lay.block_rows
    col_kind = col_part * lay.kb + col_k
    pick = col_k * lat_count + col_lat
    spread = np.arange(lay.kb * lat_count)[:, None] == pick[None, :]
    same = np.arange(lay.size)[:, None] == col_kind[None, :]
    wide_same = np.tile(same.T, (1, CHUNK))
    count = lay.owners * lay.lper
    repeat = np.arange(CHUNK * lay.size)[:, None] // lay.size == np.arange(CHUNK)[None, :]
    across = np.arange(count)[:, None] == np.arange(count * lay.size)[None, :] // lay.size
    ones = [
        jnp.asarray(v.astype(ml_dtypes.bfloat16))
        for v in (spread, spread.T, same, wide_same, repeat, across)
    ]
    return own(plain * quadrature.astype(np.float32)[None, None, :]), own(plain), ones


def normalize(values, gain_vec):
    return (
        values * lax.rsqrt(jnp.mean(values * values, axis=-1, keepdims=True) + EPSILON) * gain_vec
    )


def greet_senders(lay, greet):
    z, _, _ = lay.here()
    for slot in (0, 1):

        @pl.when(jnp.logical_not(jnp.logical_and(lay.stays(), z % 2 == slot)))
        def _():
            greet(lay.item_comes(slot))


class Swap:
    def __init__(self, lay, gone, come, sems):
        z, _, _ = lay.here()
        slot = z % 2
        self.here = [lay.item_goes(at)[1] for at in (0, 1)]
        self.far = [
            pltpu.make_async_remote_copy(
                src_ref=gone.at[at],
                dst_ref=come.at[slot],
                send_sem=sems[0],
                recv_sem=sems[1],
                device_id=lay.item_goes(at)[0],
                device_id_type=MESH,
            )
            for at in (0, 1)
        ]
        self.near = [
            pltpu.make_async_copy(gone.at[at], come.at[slot], sems[2]) for at in (0, 1)
        ]
        whole, one = come, come.at[0]
        self.stays = lay.stays()
        self.all_far, self.one_far = [
            pltpu.make_async_remote_copy(
                src_ref=ref,
                dst_ref=ref,
                send_sem=sems[0],
                recv_sem=sems[1],
                device_id=lay.item_goes(0)[0],
                device_id_type=MESH,
            )
            for ref in (whole, one)
        ]

    def start(self):
        for here, far, near in zip(self.here, self.far, self.near):

            @pl.when(here)
            def _():
                near.start()

            @pl.when(jnp.logical_not(here))
            def _():
                far.start()

    def wait(self):
        @pl.when(self.stays)
        def _():
            self.one_far.wait()
            self.near[0].wait()

        @pl.when(jnp.logical_not(self.stays))
        def _():
            self.all_far.wait()


class Total:
    def __init__(self, lay, put, every, scratch, sent, came):
        self.lay, self.put, self.every = lay, put, every
        self.pair_got, self.pair, self.line_got, self.line, self.plane_got = scratch
        self.sent, self.came = sent, came
        self.places, self.planes = lay.dp // 2, lay.ns
        self.z, self.x, n = lay.here()
        self.core, self.y, self.n, self.y_count = n % 2, n // 2, n, lay.ns // 2
        self.place = self.x * self.y_count + self.y

    @staticmethod
    def scratch(shape):
        whole = pltpu.VMEM(shape[1:], FULL)
        part = pltpu.VMEM(shape[2:], FULL)
        return [whole, whole, whole, part, part]

    def at_core(self):
        return (self.z * self.lay.x + self.x, self.n + 1 - 2 * self.core)

    def at_place(self, p):
        at = p % self.y_count * 2 + self.core
        return (self.z * self.lay.x + p // self.y_count, at)

    def at_plane(self, q):
        return (q * self.lay.x + self.x, self.n)

    def greet(self, greet):
        greet(self.at_core())

        @pl.loop(1, self.places)
        def _(step):
            greet(self.at_place(lax.rem(self.place + step, self.places)))

        @pl.loop(1, self.planes)
        def _(step):
            greet(self.at_plane(lax.rem(self.z + step, self.planes)))

        return self.places + self.planes - 1

    def remote(self, source, target, at, to):
        return pltpu.make_async_remote_copy(
            src_ref=source,
            dst_ref=target,
            send_sem=self.sent.at[at],
            recv_sem=self.came.at[at],
            device_id=to,
            device_id_type=MESH,
        )

    def settle(self, ref, at):
        self.remote(ref, ref, at, self.at_core()).wait()

    def at_chip(self, t):
        q, p = t // self.places, t % self.places
        at = p % self.y_count * 2 + self.core
        return (q * self.lay.x + p // self.y_count, at)

    def greet_chips(self, greet):
        count = self.places * self.planes
        greet(self.at_core())

        @pl.loop(1, count)
        def _(step):
            greet(self.at_chip(lax.rem(self.z * self.places + self.place + step, count)))

        return count

    def at_once(self, extra):
        core, z, place, count = self.core, self.z, self.place, self.places * self.planes
        every, mine = self.every, self.z * self.places + self.place

        def split(t):
            return t // self.places, t % self.places

        self.step(0)
        self.settle(self.pair_got, 0)
        self.pair[...] = self.put[core] + self.pair_got[...]

        @pl.loop(1, count)
        def _(step):
            to = lax.rem(mine + step, count)
            there = self.line_got.at[mine]
            self.remote(self.pair.at[split(to)], there, 1, self.at_chip(to)).start()

        self.line_got[mine] = self.pair[z, place]
        others = self.line_got.at[pl.ds(0, count - 1)]
        self.settle(others, 1)
        every[core, z, place] = jnp.sum(self.line_got[...], axis=0) + extra
        own = every.at[core, z, place]

        @pl.loop(1, count)
        def _(step):
            self.remote(own, own, 2, self.at_chip(lax.rem(mine + step, count))).start()

        self.settle(others, 2)
        self.remote(every.at[core], every.at[core], 5, self.at_core()).start()
        self.settle(every.at[core], 5)

    def pass_on(self, count, mine, stage, device, what):
        @pl.loop(1, count)
        def _(step):
            to = lax.rem(mine + step, count)
            source, target = what(to)
            self.remote(source, target, stage, device(to)).start()

    def step(self, stage, extra=None):
        core, place, z, places, planes = self.core, self.place, self.z, self.places, self.planes
        every, put = self.every, self.put
        if stage == 0:
            self.remote(put.at[1 - core], self.pair_got, 0, self.at_core()).start()
        if stage == 1:
            self.settle(self.pair_got, 0)
            for q in range(planes):
                self.pair[q] = put[core, q] + self.pair_got[q]
            there = self.line_got.at[z]
            self.pass_on(planes, z, 1, self.at_plane, lambda to: (self.pair.at[to], there))
        if stage == 2:
            self.line_got[z] = self.pair[z]
            self.settle(self.line_got.at[pl.ds(0, planes - 1)], 1)
            for p in range(places):
                total = self.line_got[0, p]
                for q in range(1, planes):
                    total = total + self.line_got[q, p]
                self.line[p] = total
            there = self.plane_got.at[place]
            self.pass_on(places, place, 2, self.at_place, lambda to: (self.line.at[to], there))
        if stage == 3:
            self.plane_got[place] = self.line[place]
            self.settle(self.plane_got.at[pl.ds(0, places - 1)], 2)
            total = self.plane_got[0]
            for p in range(1, places):
                total = total + self.plane_got[p]
            every[core, z, place] = total if extra is None else total + extra
            own = every.at[core, z, place]
            self.pass_on(planes, z, 3, self.at_plane, lambda to: (own, own))
        if stage == 4:
            self.settle(every.at[core, pl.ds(0, planes - 1), place], 3)
            own = every.at[core, pl.ds(0, planes), place]
            self.pass_on(places, place, 4, self.at_place, lambda to: (own, own))
        if stage == 5:
            self.settle(every.at[core, pl.ds(0, planes), pl.ds(0, places - 1)], 4)
            self.remote(every.at[core], every.at[core], 5, self.at_core()).start()
        if stage == 6:
            self.settle(every.at[core], 5)


def turned(real, imag):
    both = jnp.concatenate([real[:, None], imag[:, None]], axis=1)
    return both.reshape(-1, E).astype(LOW)


def parts_of(values):
    split = values.reshape(-1, 2, 8, E)
    return split[:, 0], split[:, 1]


def spectral(
    lay,
    values,
    first,
    second,
    ones,
    tag,
    spec_w,
    fetch=(),
    carry=(),
    saved=(),
    earlier=(),
    parts=(),
):
    back, last = bool(saved), bool(earlier)
    placed = spec_w.ndim == 5
    nkb, dp, ns, size, half = lay.nkb, lay.owners, lay.ns, lay.size, lay.g
    counts, ends, lper = lay.counts, lay.ends, lay.lper
    items, rows = values.shape[:2]
    laid = values.reshape(items, rows, half, nkb, size, E)
    laid = laid.transpose(2, 3, 0, 1, 4, 5).reshape(half, nkb, lay.cols, E)
    w_shape = (ns, lper, 2, lay.e_plane, E)
    dma = pltpu.SemaphoreType.DMA
    tiles = [(dp, c, size, E) for c in counts]
    spans = [(g * lay.kd, ends[g] - g * lay.kd) for g in range(nkb)]

    ins = dict(f=[laid], p1=[first], p2=list(second), ones=list(ones), w=[spec_w])
    ins |= dict(old=list(saved), earlier=list(earlier), carry=list(carry))
    outs = dict(y=[((half, nkb, lay.cols, E), LOW)])
    outs |= dict(keep=[] if back else [(t, LOW) for t in tiles])
    outs |= dict(whole=[(w_shape, LOW)] if fetch else [])
    outs |= dict(d=[(w_shape, LOW)] if back and not last else [])
    owned = (lay.lall, lay.x, 2, lay.e_dev, E)
    if lay.even:
        owned = (lay.dp, lay.slots, 2, lay.e_dev, E)
    outs |= dict(g=[(owned, LOW)] if last else [])
    outs |= dict(squares=[((8, 128), FULL)] if last else [])
    outs |= dict(carried=[(c.shape, c.dtype) for c in carry])
    ins |= dict(parts=list(parts))
    devices = lay.dp * ns
    part_rows = [v.shape[0] // devices for v in parts]
    every_shape = (2, ns, lay.dp // 2, sum(part_rows), E)
    outs |= dict(every=[(every_shape, FULL)] if parts else [])
    tall, broad = lay.size * dp * np.array(counts), half * lay.cols
    buffers = dict(
        f_got=[((nkb, half, lay.cols, E), LOW)],
        t1=[((int(h), broad), LOW) for h in tall],
        t2=[((broad, int(h)), LOW) for h in tall],
        p1_v=[(first.shape[1:], LOW)],
        p2_v=[(p.shape[1:], LOW) for p in second],
        ones_v=[(o.shape, LOW) for o in ones],
        w_v=[(w_shape, LOW)],
        s_put=[(t, LOW) for t in tiles],
        s_got=[(t, LOW) for t in tiles],
        m_put=[(t, LOW) for t in tiles],
        m_got=[(t, LOW) for t in tiles],
        y_put=[((half, nkb, lay.cols, E), LOW)],
        old_v=[(t, LOW) for t in tiles] if back else [],
        early_v=[(w_shape, LOW)] if last else [],
        d_put=[(w_shape, LOW)] if back else [],
        d_got=[(w_shape, LOW)] if last else [],
        g_put=[((lay.lall, lay.x, 2, lay.e_dev, E), LOW)] if last else [],
        part_v=[(v.shape, FULL) for v in parts],
        total=[(v.shape, FULL) for v in Total.scratch(every_shape)] if parts else [],
        square_v=[((8, 128), FULL)] if last else [],
        put_v=[(every_shape, FULL)] * 2 if parts else [],
    )
    sems = dict(f_sem=nkb, s_sem=nkb, m_sem=nkb, y_sem=1, send=4, own=nkb + 4)
    sems |= dict(load=2 + len(second) + len(ones) + len(saved) + 1)
    sems |= dict(part_sem=len(parts) + 1, total_sent=6, total_came=6)
    sems |= dict(line_send=1, line_got=nkb, own_w=1, carry_sem=4, g_sem=2)

    def kernel(*refs):
        refs = list(refs)
        r = types.SimpleNamespace()
        for group in (ins, outs, buffers):
            for name, entries in group.items():
                setattr(r, name, refs[: len(entries)])
                del refs[: len(entries)]
        for name in sems:
            setattr(r, name, refs.pop(0))
        (f_ref,), (y_ref,), (f_got,), (y_put,), (w,) = r.f, r.y, r.f_got, r.y_put, r.w_v
        t1, t2, s_put, s_got, m_put, m_got = r.t1, r.t2, r.s_put, r.s_got, r.m_put, r.m_got
        spread, spread_t, same, wide_same, repeat, across = r.ones_v
        send, own = r.send, r.own
        z, x, n = lay.here()
        _, me, device = group_of(lay, "owners")
        _, place_at, plane_device = group_of(lay, "plane")
        _, mine_at, half_device = group_of(lay, "half")
        _, _, line_device = group_of(lay, "line")
        line = bool(fetch) or last
        barrier = pltpu.get_barrier_semaphore()

        def greet(target):
            pl.semaphore_signal(barrier, inc=1, device_id=target, device_id_type=MESH)

        @pl.loop(1, dp)
        def _(step):
            greet(device(lax.rem(me + step, dp)))

        if line:

            @pl.loop(1, ns)
            def _(step):
                greet(line_device(lax.rem(z + step, ns)))

        if carry:
            greet_senders(lay, greet)
        waits = dp - 1 + (ns - 1 if line else 0)
        if parts:
            put, every = r.put_v
            summed = Total(lay, put, every, r.total, r.total_sent, r.total_came)
            waits = waits + summed.greet(greet)
            for at, ref in enumerate(r.part_v):
                pltpu.make_async_copy(r.parts[at], ref, r.part_sem.at[at]).start()
        pairs = [(r.p1[0].at[mine_at], r.p1_v[0])]
        pairs += [(a, b) for a, b in zip(r.ones, r.ones_v)]
        pairs += [(a.at[mine_at], b) for a, b in zip(r.p2, r.p2_v)]
        tables_at = len(pairs)
        if not fetch:
            pairs += [(r.w[0], w)]
        pairs += list(zip(r.old, r.old_v)) + list(zip(r.earlier, r.early_v))
        loads = []
        for at, (source, target) in enumerate(pairs):
            copy = pltpu.make_async_copy(source, target, r.load.at[at])
            copy.start()
            loads.append(copy)
        mine = []
        for k in range(nkb):
            copy = pltpu.make_async_copy(f_ref.at[mine_at, k], f_got.at[k, mine_at], own.at[k])
            copy.start()
            mine.append(copy)
        if carry:
            pl.semaphore_wait(barrier, waits + jnp.where(lay.stays(), 1, 2))
        else:
            pl.semaphore_wait(barrier, waits)

        def remote(source, target, sent, got, to):
            return pltpu.make_async_remote_copy(
                src_ref=source,
                dst_ref=target,
                send_sem=sent,
                recv_sem=got,
                device_id=to,
                device_id_type=MESH,
            )

        def push(source, target, sent, got, peer):
            remote(source, target, sent, got, device(peer)).start()

        def settle(ref, sent, got, sending):
            copy = remote(ref, ref, sent, got, device(lax.rem(me + 1, dp)))
            if sending:
                copy.wait_send()
            else:
                copy.wait_recv()

        for k in range(nkb):

            @pl.loop(1, half)
            def _(step):
                peer = lax.rem(mine_at + step, half)
                target = f_got.at[k, mine_at]
                sem = r.f_sem.at[k]
                remote(f_ref.at[peer, k], target, send.at[0], sem, half_device(peer)).start()

        if fetch:
            share = r.w[0].at[z] if placed else r.w[0]

            def share_of(to, degree):
                return share.at[degree * lay.v + lax.rem(to, lay.v)]

            for g in range(nkb):

                @pl.loop(*(spans[g][0], ends[g]))
                def _(degree):
                    pltpu.make_async_copy(
                        share_of(z, degree), w.at[z, degree], r.own_w.at[0]
                    ).start()
                    for step in range(1, ns):
                        to = lax.rem(z + step, ns)
                        remote(
                            share_of(to, degree),
                            w.at[z, degree],
                            r.line_send.at[0],
                            r.line_got.at[g],
                            line_device(to),
                        ).start()

        if carry:
            (gone,), (come,) = r.carry, r.carried
            swap = Swap(lay, gone, come, [r.carry_sem.at[at] for at in range(4)])
            swap.start()

        if parts:
            begin = 0
            for at, (ref, count) in enumerate(zip(r.part_v, part_rows)):
                pltpu.make_async_copy(r.parts[at], ref, r.part_sem.at[at]).wait()
                width = ref.shape[1]
                for index in range(devices):
                    d, n_at = divmod(index, ns)
                    place = d % lay.x * (ns // 2) + n_at // 2
                    block = put.at[n_at % 2, d // lay.x, place, pl.ds(begin, count)]
                    if width < E:
                        block[...] = jnp.zeros((count, E), FULL)
                    block[:, :width] = ref[pl.ds(index * count, count), :]
                begin += count
            summed.step(0)

        for at in range(tables_at):
            loads[at].wait()
        for k in range(nkb):

            @pl.loop(0, dp * counts[k] // CHUNK)
            def _(chunk):
                at = pl.multiple_of(dp * lay.starts[k] + chunk * CHUNK, CHUNK)
                part = r.p1_v[0][pl.ds(at, CHUNK), :]
                part = jnp.dot(repeat[...], part, preferred_element_type=FULL).astype(LOW)
                full = jnp.dot(part, spread[...], preferred_element_type=FULL)
                full = full.reshape(CHUNK, size, broad) * same[...].astype(FULL)[None]
                to = pl.multiple_of(chunk * CHUNK * size, CHUNK * size)
                t1[k][pl.ds(to, CHUNK * size), :] = full.reshape(CHUNK * size, broad).astype(LOW)

        if parts:
            summed.step(1)

        for k in range(nkb):
            mine[k].wait()
            settle(f_got.at[k, pl.ds(0, half - 1)], send.at[0], r.f_sem.at[k], False)
            high = counts[k] * size

            def modes_for(peer):
                part = t1[k][pl.ds(pl.multiple_of(peer * high, 16), high), :]
                got = f_got[k].reshape(half * lay.cols, E)
                out = jnp.dot(part, got, preferred_element_type=FULL).astype(LOW)
                return out.reshape(counts[k], size, E)

            @pl.loop(1, dp)
            def _(step):
                peer = lax.rem(me + step, dp)
                s_put[k][peer] = modes_for(peer)
                push(s_put[k].at[peer], s_got[k].at[me], send.at[1], r.s_sem.at[k], peer)

            s_got[k][me] = modes_for(me)

        if parts:
            summed.step(2)
        for k in range(nkb):
            width = CHUNK * size
            count = dp * counts[k]

            @pl.loop(0, count // CHUNK)
            def _(chunk):
                to = pl.ds(pl.multiple_of(chunk * width, width), width)
                part = jnp.dot(
                    r.p2_v[k][...], across[pl.ds(0, count), to], preferred_element_type=FULL
                )
                full = jnp.dot(spread_t[...], part.astype(LOW), preferred_element_type=FULL)
                t2[k][:, to] = (full * wide_same[...].astype(FULL)).astype(LOW)

        if parts:
            summed.step(3)

        for copy in loads[tables_at:]:
            copy.wait()
        def rows_at(group, degree, g):
            tiles = [group[k][:, degree - k * lay.kd] for k in range(g + 1)]
            return jnp.concatenate([t.reshape(dp * size, E) for t in tiles], axis=0)

        if fetch:
            pltpu.make_async_copy(w.at[z], w.at[z], r.own_w.at[0]).wait()
        for g, (begin, length) in enumerate(spans):
            settle(s_got[g].at[pl.ds(0, dp - 1)], send.at[1], r.s_sem.at[g], False)
            span = pl.ds(begin, length)
            if fetch:
                got = w.at[pl.ds(0, ns - 1), span]
                settle(got, r.line_send.at[0], r.line_got.at[g], False)

            @pl.loop(begin, ends[g])
            def _(degree):
                rows_in = rows_at(s_got, degree, g)
                dims = (((1,), (1 if back else 0,)), ((), ()))
                by_real, by_imag = (
                    lax.dot_general(
                        rows_in, w[:, degree, p].reshape(E, E), dims, preferred_element_type=FULL
                    )
                    for p in (0, 1)
                )
                (rr, ir), (ri, ii) = parts_of(by_real), parts_of(by_imag)
                mixed = turned(rr + ii, ir - ri) if back else turned(rr - ii, ri + ir)
                for k in range(g + 1):
                    part = mixed[k * dp * size : (k + 1) * dp * size]
                    m_put[k][:, degree - k * lay.kd] = part.reshape(dp, size, E)

            for k in range(g + 1):
                there = pl.ds(begin - k * lay.kd, length)

                @pl.loop(1, dp)
                def _(step):
                    peer = lax.rem(me + step, dp)
                    target = m_got[k].at[me, there]
                    push(m_put[k].at[peer, there], target, send.at[2], r.m_sem.at[k], peer)

        if back:
            (d_put,) = r.d_put
            for g, (begin, length) in enumerate(spans):
                span = pl.ds(begin, length)

                @pl.loop(begin, ends[g])
                def _(degree):
                    dims = (((0,), (0,)), ((), ()))
                    olds, grads = rows_at(r.old_v, degree, g), rows_at(s_got, degree, g)
                    real, imag = parts_of(grads.astype(FULL))
                    for p, right in ((0, grads), (1, turned(imag, -real))):
                        total = lax.dot_general(olds, right, dims, preferred_element_type=FULL)
                        total = total.reshape(ns, lay.e_plane, E)
                        if last:
                            total = total + r.early_v[0][:, degree, p].astype(FULL)
                        d_put[:, degree, p] = total.astype(LOW)

                if last:
                    (d_got,) = r.d_got

                    @pl.loop(1, ns)
                    def _(step):
                        to = lax.rem(z + step, ns)
                        remote(
                            d_put.at[to, span],
                            d_got.at[z, span],
                            r.line_send.at[0],
                            r.line_got.at[g],
                            line_device(to),
                        ).start()

                    d_got[z, span] = d_put[z, span]

        if parts:
            summed.step(4)
        for k in range(nkb):
            m_got[k][me] = m_put[k][me]
        keeps = []
        for at, (source, target) in enumerate(
            list(zip(s_got, r.keep)) + [(w, t) for t in r.whole] + list(zip(r.d_put, r.d))
        ):
            copy = pltpu.make_async_copy(source, target, own.at[at])
            copy.start()
            keeps.append(copy)

        for k in range(nkb):
            settle(m_got[k].at[pl.ds(0, dp - 1)], send.at[2], r.m_sem.at[k], False)

            def rows_for(peer):
                part = t2[k][pl.ds(pl.multiple_of(peer * lay.cols, 16), lay.cols), :]
                got = m_got[k][...].reshape(-1, E)
                return jnp.dot(part, got, preferred_element_type=FULL).astype(LOW)

            @pl.loop(1, half)
            def _(step):
                peer = lax.rem(mine_at + step, half)
                y_put[peer, k] = rows_for(peer)
                target, sem = y_ref.at[mine_at, k], r.y_sem.at[0]
                remote(y_put.at[peer, k], target, send.at[3], sem, half_device(peer)).start()

            y_put[mine_at, k] = rows_for(mine_at)
        ends_with = pltpu.make_async_copy(y_put.at[mine_at], y_ref.at[mine_at], own.at[nkb + 2])
        ends_with.start()

        if parts:
            summed.step(5)
        if last:
            (g_put,), (g_ref,), (square_v,) = r.g_put, r.g, r.square_v
            square_v[...] = jnp.zeros_like(square_v)
            for g, (begin, length) in enumerate(spans):
                if parts and g == nkb - 1:
                    summed.step(6)
                    pltpu.make_async_copy(every, r.every[0], r.part_sem.at[len(parts)]).start()
                got = d_got.at[pl.ds(0, ns - 1), pl.ds(begin, length)]
                settle(got, r.line_send.at[0], r.line_got.at[g], False)

                @pl.loop(begin * lay.v, ends[g] * lay.v)
                def _(at):
                    degree, s_at = at // lay.v, lax.rem(at, lay.v)
                    for p in (0, 1):
                        total = d_got[s_at, degree, p].astype(FULL)
                        for first_plane in range(lay.v, ns, lay.v):
                            total = total + d_got[first_plane + s_at, degree, p].astype(FULL)
                        folded = (total * total).reshape(-1, 8, E).sum(axis=0)
                        square_v[...] += folded[:, :128] + folded[:, 128:]
                        g_put[at, :, p] = total.astype(LOW).reshape(lay.x, lay.e_dev, E)
                    if lay.even:
                        slot = lax.rem(at, lay.slots)
                        for at_x in range(lay.x):
                            peer = at // lay.slots * lay.x + at_x

                            @pl.when(peer != place_at)
                            def _():
                                remote(
                                    g_put.at[at, at_x],
                                    g_ref.at[place_at, slot],
                                    r.g_sem.at[0],
                                    r.g_sem.at[1],
                                    plane_device(peer),
                                ).start()

            if lay.even:
                copy = pltpu.make_async_copy(
                    g_put.at[pl.ds(n * lay.slots, lay.slots), x], g_ref.at[place_at], own.at[nkb + 3]
                )
            else:
                copy = pltpu.make_async_copy(g_put, g_ref, own.at[nkb + 3])
            copy.start()
            copy.wait()
            copy = pltpu.make_async_copy(square_v, r.squares[0], own.at[nkb + 3])
            copy.start()
            copy.wait()
            if lay.even:
                some = g_ref.at[pl.ds(0, lay.dp - 1)]
                settle(some, r.g_sem.at[0], r.g_sem.at[1], True)
                settle(some, r.g_sem.at[0], r.g_sem.at[1], False)

        if parts:
            pltpu.make_async_copy(every, r.every[0], r.part_sem.at[len(parts)]).wait()
        ends_with.wait()
        for copy in keeps:
            copy.wait()
        settle(f_ref.at[pl.ds(0, half - 1)], send.at[0], r.f_sem.at[0], True)
        for k in range(nkb):
            settle(s_got[k].at[pl.ds(0, dp - 1)], send.at[1], r.s_sem.at[0], True)
            settle(m_got[k].at[pl.ds(0, dp - 1)], send.at[2], r.m_sem.at[0], True)
        if line:
            settle(w.at[pl.ds(0, ns - 1)], r.line_send.at[0], r.line_got.at[0], True)
        if carry:
            swap.wait()
        settle(y_put.at[pl.ds(0, half - 1)], send.at[3], r.y_sem.at[0], True)
        settle(y_put.at[pl.ds(0, half - 1)], send.at[3], r.y_sem.at[0], False)

    spot = pl.BlockSpec(memory_space=pl.ANY)
    operands = [v for group in ins.values() for v in group]
    steady = {id(v) for v in [first, *second, *ones]}
    places = [pl.BlockSpec(memory_space=pltpu.HBM) if id(v) in steady else spot for v in operands]
    results = [jax.ShapeDtypeStruct(*v) for group in outs.values() for v in group]
    scratch = [pltpu.VMEM(*v) for group in buffers.values() for v in group]
    need = sum(math.prod(shape[:-1]) * -(-shape[-1] // 128) * 128 * np.dtype(kind).itemsize
               for group in buffers.values() for shape, kind in group)
    scratch += [dma((count,)) for count in sems.values()]
    got = list(
        pl.pallas_call(
            kernel,
            out_shape=results,
            in_specs=places,
            out_specs=[spot] * len(results),
            scratch_shapes=scratch,
            compiler_params=pltpu.CompilerParams(
                collective_id=tag,
                has_side_effects=True,
                vmem_limit_bytes=min(58 << 20, need + (10 << 20)),
            ),
            cost_estimate=pl.CostEstimate(
                flops=40_000_000_000, bytes_accessed=100_000_000, transcendentals=0
            ),
            name="spectral_back" if back else "spectral",
        )(*operands)
    )
    given = types.SimpleNamespace()
    for name, entries in outs.items():
        setattr(given, name, got[: len(entries)])
        del got[: len(entries)]
    rows_out = given.y[0].reshape(half, nkb, items, rows, size, E)
    rows_out = rows_out.transpose(2, 3, 0, 1, 4, 5).reshape(items, rows, -1, E)
    return rows_out, given


def prologue(lay, spec_laid, small, swaps, tag):
    def kernel(*refs):
        spec_ref, small_ref = refs[:2]
        swap_refs = refs[2 : 2 + len(swaps)]
        spec_got, small_got = refs[2 + len(swaps) : 4 + len(swaps)]
        swap_got = refs[4 + len(swaps) : 4 + 2 * len(swaps)]
        sent, got, own, swap_sem = refs[4 + 2 * len(swaps) :]
        z, x, n = lay.here()
        _, me, device = group_of(lay, "plane")
        core, y_count, places = n % 2, lay.ns // 2, lay.dp // 2
        place = x * y_count + n // 2
        sibling = (z * lay.x + x, n + 1 - 2 * core)

        def at_plane(q):
            return q * lay.x + x, n

        def at_place(p):
            return z * lay.x + p // y_count, p % y_count * 2 + core

        barrier = pltpu.get_barrier_semaphore()

        def greet(target):
            pl.semaphore_signal(barrier, inc=1, device_id=target, device_id_type=MESH)

        @pl.loop(1, lay.dp)
        def _(step):
            greet(device(lax.rem(me + step, lay.dp)))

        @pl.loop(1, lay.ns)
        def _(step):
            greet(at_plane(lax.rem(z + step, lay.ns)))

        greet_senders(lay, greet)
        pl.semaphore_wait(barrier, lay.dp + lay.ns - 2 + jnp.where(lay.stays(), 1, 2))

        def remote(source, target, at, to):
            return pltpu.make_async_remote_copy(
                src_ref=source,
                dst_ref=target,
                send_sem=sent.at[at],
                recv_sem=got.at[at],
                device_id=to,
                device_id_type=MESH,
            )

        def spec_here():
            if lay.even:
                return spec_got.at[z, pl.ds(n * lay.slots, lay.slots), :, x]
            return spec_got.at[me]

        copy = pltpu.make_async_copy(small_ref, small_got.at[core, z, place], own.at[0])
        copy.start()

        @pl.loop(1, lay.ns)
        def _(step):
            to = at_plane(lax.rem(z + step, lay.ns))
            remote(small_ref, small_got.at[core, z, place], 1, to).start()

        moves = [
            Swap(lay, a, b, [swap_sem.at[at, k] for k in range(3)])
            for at, (a, b) in enumerate(zip(swap_refs, swap_got))
        ]
        for move in moves:
            move.start()
        @pl.loop(1, lay.dp)
        def _(step):
            peer = lax.rem(me + step, lay.dp)
            remote(spec_ref.at[peer], spec_here(), 0, device(peer)).start()

        pltpu.make_async_copy(spec_ref.at[me], spec_here(), got.at[0]).start()
        copy.wait()
        some = small_got.at[core, pl.ds(0, lay.ns - 1), place]
        remote(some, some, 1, sibling).wait()
        column = small_got.at[core, pl.ds(0, lay.ns), place]

        @pl.loop(1, places)
        def _(step):
            remote(column, column, 3, at_place(lax.rem(place + step, places))).start()

        some = small_got.at[core, pl.ds(0, lay.ns), pl.ds(0, places - 1)]
        remote(some, some, 3, sibling).wait()
        remote(small_got.at[core], small_got.at[core], 2, sibling).start()
        some = spec_ref.at[pl.ds(0, lay.dp - 1)]
        every = spec_got.at[z] if lay.even else spec_got
        remote(every, every, 0, sibling).wait_recv()
        remote(some, some, 0, sibling).wait_send()
        remote(small_got.at[core], small_got.at[core], 2, sibling).wait()
        for move in moves:
            move.wait()

    spot = pl.BlockSpec(memory_space=pl.ANY)
    w_shape = (lay.ns, lay.lall, 2, lay.x, lay.e_dev, E)
    spec_shape = jax.ShapeDtypeStruct(w_shape, LOW) if lay.even else spec_laid
    small_shape = (2, lay.ns, lay.dp // 2) + small.shape
    outs = [spec_shape, jax.ShapeDtypeStruct(small_shape, small.dtype), *swaps]
    count = 4
    got = pl.pallas_call(
        kernel,
        out_shape=[jax.ShapeDtypeStruct(o.shape, o.dtype) for o in outs],
        in_specs=[spot] * (2 + len(swaps)),
        out_specs=[spot] * len(outs),
        scratch_shapes=[
            pltpu.SemaphoreType.DMA((count,)),
            pltpu.SemaphoreType.DMA((count,)),
            pltpu.SemaphoreType.DMA((2,)),
            pltpu.SemaphoreType.DMA((len(swaps), 3)),
        ],
        compiler_params=pltpu.CompilerParams(collective_id=tag, has_side_effects=True),
        name="prologue",
    )(spec_laid, small, *swaps)
    every = jnp.moveaxis(got[1], 0, 2).reshape((lay.dp * lay.ns,) + small.shape)
    return got[0], every, list(got[2:])


def spec_out(lay, spec):
    z, x, n = lay.here()
    low = spec.astype(LOW).transpose(1, 2, 0, 3)
    tail = (2, lay.e_dev, E)
    if lay.even:
        laid = low.reshape((lay.slots, lay.dp) + tail).swapaxes(0, 1)
    else:
        at = (jnp.arange(lay.dp) - lay.lns * n) % lay.dp
        at = at[:, None] + lay.dp * jnp.arange(lay.slots)
        laid = jnp.take(low, jnp.minimum(at, lay.lns - 1), axis=0)
    return laid


def spec_in(lay, got):
    z, x, n = lay.here()
    if lay.even:
        return got.reshape(lay.ns, lay.lall, 2, lay.e_plane, E)
    member = n * lay.x + x
    got = got.reshape((lay.ns, lay.x, lay.slots, 2, lay.e_dev, E))
    got = got.transpose(0, 2, 3, 1, 4, 5).reshape(lay.ns, lay.slots, 2, lay.e_plane, E)
    degree = lay.dp * jnp.arange(lay.lall) + member
    return got[degree // lay.lns, degree % lay.lns // lay.dp]


def spec_home(lay, given, tag):
    z, x, n = lay.here()
    member = n * lay.x + x
    if lay.even:
        mine = given.swapaxes(0, 1).reshape(lay.lns, 2, lay.e_dev, E)
        return mine.transpose(2, 0, 1, 3)
    first = (member - lay.lns * jnp.arange(lay.ns)) % lay.dp + lay.lns * jnp.arange(lay.ns)
    at = (first[:, None] + lay.dp * jnp.arange(lay.slots) - member) // lay.dp
    slots = given[jnp.clip(at, 0, lay.lall - 1)]
    slots = slots.transpose(0, 2, 1, 3, 4, 5)
    (back,) = exchange(lay, [slots.reshape(lay.dp, -1, E)], ["each"], "plane", tag)
    back = back.reshape(lay.dp, lay.slots, 2, lay.e_dev, E)
    degree = lay.lns * n + jnp.arange(lay.lns)
    source = degree % lay.dp
    slot = (jnp.arange(lay.lns) - (source - lay.lns * n) % lay.dp) // lay.dp
    return back[source, slot].transpose(2, 0, 1, 3)


def pad_rows(values, rows):
    return jnp.pad(values, ((0, 0),) * (values.ndim - 2) + ((0, rows - values.shape[-2]), (0, 0)))


def wide(values):
    return jnp.pad(values, ((0, 0),) * (values.ndim - 1) + ((0, 128 - values.shape[-1]),))


def forward_block(lay, residual, weights, tables, tag, fetch, carry):
    spec_w, up_w, down_w, gain_low = weights
    gain_vec = gain_low.astype(FULL)
    dft_fwd, dft_inv, quad_tab, plain_tab, ones = tables
    normed_a = normalize(residual, gain_vec[:, 0]).astype(LOW)
    fourier = jnp.einsum("brke,kq->brqe", normed_a, dft_fwd, preferred_element_type=FULL)
    restored, given = spectral(
        lay, fourier.astype(LOW), quad_tab[0], plain_tab[1], ones, tag, spec_w, fetch, carry
    )
    middle = residual + jnp.einsum(
        "brqe,kq->brke", restored, dft_inv, preferred_element_type=FULL
    )
    normed_b = normalize(middle, gain_vec[:, 1]).astype(LOW)
    pre_act = jnp.einsum("brke,fe->brkf", normed_b, up_w, preferred_element_type=FULL)
    hidden = jax.nn.gelu(pre_act).astype(LOW)
    output = middle + jnp.einsum("brkf,fe->brke", hidden, down_w, preferred_element_type=FULL)
    return (output, (residual, given.keep, middle, normed_b, pre_act, hidden), given)


def backward_block(
    lay, output_gradient, saved, weights, tables, tag, earlier, carry, sums, closing, low_grad, aside
):
    residual, spectrum, middle, normed_b, pre_act, hidden = saved
    spec_w, up_w, down_w, gain_low = weights
    gain_vec = gain_low.astype(FULL)
    dft_fwd, dft_inv, quad_tab, plain_tab, ones = tables
    g_out = output_gradient.astype(LOW)
    d_hidden = jnp.einsum("brke,fe->brkf", g_out, down_w, preferred_element_type=FULL)
    d_pre = jax.vjp(jax.nn.gelu, pre_act)[1](d_hidden)[0].astype(LOW)
    d_normed_b = jnp.einsum("brkf,fe->brke", d_pre, up_w, preferred_element_type=FULL)
    d_mid_part, d_gain_b = jax.vjp(normalize, middle, gain_vec[:, 1])[1](d_normed_b)
    d_middle = output_gradient + d_mid_part
    d_restored = jnp.einsum(
        "brke,kq->brqe", d_middle.astype(LOW), dft_inv, preferred_element_type=FULL
    ).astype(LOW)
    products = [
        jnp.einsum("brkf,brke->fe", a, b, preferred_element_type=FULL)
        for a, b in ((d_pre, normed_b), (hidden, g_out), (closing, low_grad))
    ]
    sums = [a + b for a, b in zip(sums, products)] if sums else products
    d_restored, sums = lax.optimization_barrier((d_restored, sums))
    d_fourier, given = spectral(
        lay,
        d_restored,
        plain_tab[0],
        quad_tab[1],
        ones,
        tag,
        spec_w,
        carry=carry,
        saved=spectrum,
        earlier=earlier,
        parts=sums if aside and earlier else (),
    )
    d_normed_a = jnp.einsum("brqe,kq->brke", d_fourier, dft_fwd, preferred_element_type=FULL)
    d_res_part, d_gain_a = jax.vjp(normalize, residual, gain_vec[:, 0])[1](d_normed_a)
    d_gain = jnp.stack([d_gain_a, d_gain_b], axis=1)
    sums = given.every or sums
    return d_middle + d_res_part, given, sums, d_gain


def product(left, right, dims):
    parts = []
    for value in (left, right):
        high = value.astype(LOW)
        parts.append((high, (value - high.astype(FULL)).astype(LOW)))
    (a, a_rest), (b, b_rest) = parts

    def dot(p, q):
        return lax.dot_general(p, q, (dims, ((), ())), preferred_element_type=FULL)

    return dot(a, b) + (dot(a, b_rest) + dot(a_rest, b))


def finish(lay, blocks, given, moments, extra, ff_dev, e_own, tag):
    planes, places, pack = moments.shape[1:4]
    count = 2 * places * planes
    at_enc = 0 if given else 2 * ff_dev
    rows, lanes = blocks.shape[3:]

    def kernel(blocks_ref, moment_ref, extra_ref, *refs):
        given_ref = refs[0] if given else None
        refs = refs[len(given) :]
        every_ref, scalars_ref = refs[:2]
        new_refs, scratch = refs[2 : 2 + len(results)], refs[2 + len(results) :]
        mats, sent, came = scratch[5 : 5 + len(mat_shapes)], scratch[-2], scratch[-1]
        summed = Total(lay, blocks_ref, every_ref, scratch[:5], sent, came)
        barrier = pltpu.get_barrier_semaphore()

        def greet(target):
            pl.semaphore_signal(barrier, inc=1, device_id=target, device_id_type=MESH)

        pl.semaphore_wait(barrier, summed.greet_chips(greet))
        at_row = lax.broadcasted_iota(jnp.int32, (rows, lanes), 0) == at_enc
        at_lane = lax.broadcasted_iota(jnp.int32, (rows, lanes), 1) == C + 3
        squares = jnp.sum(extra_ref[...], keepdims=True)
        added = jnp.where(jnp.logical_and(at_row, at_lane), squares, 0.0)
        summed.at_once(added)

        every = every_ref[...].reshape(count, rows, lanes)
        row = lax.broadcasted_iota(jnp.int32, (rows, lanes), 0)
        lane = lax.broadcasted_iota(jnp.int32, (rows, lanes), 1)
        enc_rows = jnp.logical_and(row >= at_enc, row < at_enc + e_own)
        added = jnp.logical_and(enc_rows, jnp.logical_or(lane == C + 2, lane == C + 3))
        squares = jnp.sum(jnp.where(added[None], 0.0, every * every), axis=0)
        owned = jnp.logical_and(row == at_enc, lane == C + 3)
        squares = squares + jnp.where(owned, jnp.sum(every, axis=0), 0.0)
        squares = jnp.sum(squares, keepdims=True)
        if given:
            sums = given_ref[...].reshape(count, pack, E)
            squares = squares + jnp.sum(jnp.sum(sums * sums, axis=0), keepdims=True)
        norm = jnp.sqrt(squares)
        clip = CLIP_NORM / jnp.maximum(norm, CLIP_NORM)
        at_lane = lax.broadcasted_iota(jnp.int32, (8, 128), 1)
        loss = every[0, at_enc : at_enc + 1, C + 2 : C + 3]
        scalars_ref[...] = jnp.where(at_lane == 0, norm, jnp.where(at_lane == 1, clip, loss))

        old = moment_ref[...].reshape(count, pack, E)
        if given:

            def new(begin, size, grads, first=0, width=E):
                own = old[:, begin : begin + size, first : first + width].reshape(-1, width)
                return MOMENTUM * own + clip * grads.reshape(-1, width)

            near = lax.broadcasted_iota(jnp.int32, (e_own, 128), 1) < C
            enc_sums = jnp.where(near[None], every, 0.0)
            starts = [new(at, ff_dev, sums[:, at : at + ff_dev]) for at in (0, ff_dev)]
            starts.append(new(2 * ff_dev, e_own, enc_sums, 0, 128))
            starts.append(new(2 * ff_dev, e_own, sums[:, 2 * ff_dev :, :128], 128, 128))
        else:
            moment = MOMENTUM * old + clip[None] * every

            def rows_of(begin, size):
                inside = jnp.logical_and(row >= begin, row < begin + size)
                return jnp.where(inside[None], moment, 0.0).reshape(-1, E)

            both = rows_of(at_enc, e_own)
            near = lax.broadcasted_iota(jnp.int32, (both.shape[0], 128), 1) < C
            starts = [rows_of(0, ff_dev), rows_of(ff_dev, ff_dev)]
            starts += [jnp.where(near, both[:, :128], 0.0), both[:, 128:]]
        if given:
            first = summed.core == 0
            starts = [jnp.where(first, starts[k], starts[k + 1]) for k in (0, 2)]
        for start, out in zip(starts, mats):
            square = jnp.sum(start * start, keepdims=True)
            out[...] = start / (jnp.sqrt(square) + 1e-07)

        @pl.loop(0, NS_ITERS)
        def _(sweep):
            for out in mats[: len(starts)]:
                matrix = out[...]
                gram_mat = product(matrix, matrix, ((0,), (0,)))
                square = product(gram_mat, gram_mat, ((1,), (0,)))
                poly = NS_SECOND * gram_mat + NS_THIRD * square
                out[...] = NS_FIRST * matrix + product(matrix, poly, ((1,), (0,)))

        if not given:
            up, down, enc, dec = (m[...] for m in mats)
            both = jnp.concatenate([enc, dec], axis=1)
            new_refs[0][...] = (up + down + both).reshape((2, planes, places, pack, E))
            return
        tall, flat, give_tall, give_flat, got_tall, got_flat = mats
        core, z = summed.core, summed.z

        def block_at(c, p):
            return (c * planes + z) * places + p

        def rows_at(ref, block, size):
            return ref[pl.ds(pl.multiple_of(block * size, 8), size), :]

        give_tall[...] = rows_at(tall, block_at(1 - core, summed.place), ff_dev)
        enc_at = [(k % 2, summed.x * summed.y_count + k // 2) for k in range(planes)]
        for k, (c, p) in enumerate(enc_at):
            give_flat[pl.ds(k * e_own, e_own), :] = rows_at(flat, block_at(c, p), e_own)
        copies = [
            summed.remote(give_tall, got_tall, 6, summed.at_core()),
            summed.remote(give_flat, got_flat, 7, summed.at_core()),
        ]
        for copy in copies:
            copy.start()
        for copy in copies:
            copy.wait()
        mine = rows_at(tall, block_at(core, summed.place), ff_dev)
        steps = [(mine, got_tall[...]), (give_flat[...], got_flat[...])]
        own_sums = given_ref[core, z, summed.place]
        flat_sums = [
            jnp.concatenate([given_ref[c, z, p, 2 * ff_dev :, :128] for c, p in enc_at], axis=0),
            jnp.concatenate([every_ref[c, z, p] for c, p in enc_at], axis=0),
        ]
        grads = [own_sums[:ff_dev], own_sums[ff_dev : 2 * ff_dev], flat_sums[1], flat_sums[0]]
        for at in range(4):
            here, there = steps[at // 2]
            new_refs[2 * (at // 2)][at % 2] = grads[at]
            step = jnp.where(first, here, there) if at % 2 == 0 else jnp.where(first, there, here)
            new_refs[2 * (at // 2) + 1][at % 2] = step

    if given:
        e_dev = lay.e_dev
        mat_shapes = [(FF, E), (E, 128)] + [(ff_dev, E), (e_dev, 128)] * 2
        results = [jax.ShapeDtypeStruct((2, ff_dev, E), FULL)] * 2
        results += [jax.ShapeDtypeStruct((2, e_dev, 128), FULL)] * 2
    else:
        mat_shapes = [(count * pack, E)] * 2 + [(count * pack, 128)] * 2
        results = [jax.ShapeDtypeStruct(moments.shape, FULL)]
    fast = pl.BlockSpec(memory_space=pltpu.VMEM)
    sums = [jax.ShapeDtypeStruct(blocks.shape, FULL), jax.ShapeDtypeStruct((8, 128), FULL)]
    got = pl.pallas_call(
        kernel,
        out_shape=sums + results,
        in_specs=[fast] * (3 + len(given)),
        out_specs=[fast] * (2 + len(results)),
        scratch_shapes=[
            *Total.scratch(blocks.shape)[:2],
            pltpu.VMEM((planes * places,) + blocks.shape[3:], FULL),
            *Total.scratch(blocks.shape)[3:],
            *[pltpu.VMEM(m, FULL) for m in mat_shapes],
            pltpu.SemaphoreType.DMA((8,)),
            pltpu.SemaphoreType.DMA((8,)),
        ],
        compiler_params=pltpu.CompilerParams(
            collective_id=tag, has_side_effects=True, vmem_limit_bytes=56 << 20
        ),
        name="finish",
    )(blocks, moments, extra, *given)
    return got[0], got[1], list(got[2:])


def update(scalars, grads, own):
    def kernel(scalars_ref, tall_grad, tall_step, flat_grad, flat_step, *refs):
        own_refs, new_refs, last = refs[: len(own)], refs[len(own) : -3], refs[-3:]
        for at, ref in enumerate(last):
            ref[0, 0] = scalars_ref[0, at]
        clip = scalars_ref[0, 1]
        for at in range(4):
            grad, step = ((tall_grad, tall_step), (flat_grad, flat_step))[at // 2]
            factor = RATE_MUON * math.sqrt(max(1.0, FF / E if at < 2 else E / C))
            master, moment = own_refs[2 * at][...], own_refs[2 * at + 1][...]
            columns = master.shape[1]
            new_refs[2 * at][...] = MOMENTUM * moment + clip * grad[at % 2][:, :columns]
            decayed = master * (1.0 - RATE_MUON * DECAY)
            new_refs[2 * at + 1][...] = decayed - factor * step[at % 2][:, :columns]
        gain, gain_m, gain_v = (ref[...] for ref in own_refs[8:])
        gain_grad = jnp.transpose(flat_grad[0])[C : C + 2]
        new = adam_step(gain, gain_m, gain_v, clip * gain_grad, RATE_GAIN)
        for ref, value in zip(new_refs[8:], new):
            ref[...] = value

    fast = pl.BlockSpec(memory_space=pltpu.VMEM)
    slow = pl.BlockSpec(memory_space=pltpu.SMEM)
    got = pl.pallas_call(
        kernel,
        out_shape=[jax.ShapeDtypeStruct(v.shape, FULL) for v in own]
        + [jax.ShapeDtypeStruct((1, 1), FULL)] * 3,
        in_specs=[slow] + [fast] * (4 + len(own)),
        out_specs=[fast] * len(own) + [slow] * 3,
        name="update",
    )(scalars, *grads, *own)
    return list(got[:-3]), [v.reshape(()) for v in got[-3:]]


def natural(values):
    order = tuple(range(values.ndim))
    return with_layout_constraint(values, DeviceLayout(major_to_minor=order))


def adam_step(weight, moment_a, moment_b, gradient, step_rate):
    moment_a = BETA_FIRST * moment_a + (1.0 - BETA_FIRST) * gradient
    moment_b = BETA_SECOND * moment_b + (1.0 - BETA_SECOND) * gradient * gradient
    corrected_a = moment_a / (1.0 - BETA_FIRST**STEP)
    corrected_b = moment_b / (1.0 - BETA_SECOND**STEP)
    return (
        moment_a,
        moment_b,
        weight - step_rate * (corrected_a / (jnp.sqrt(corrected_b) + 1e-08) + DECAY * weight),
    )


def local(
    fields,
    targets,
    valid,
    var_class,
    enc_t,
    enc_mom,
    dec,
    dec_mom,
    spec,
    spec_m,
    spec_v,
    up_t,
    up_mom,
    down,
    down_mom,
    gains,
    gain_m,
    gain_v,
):
    dp_count, ns_count = lax.axis_size("dp"), lax.axis_size("ns")
    devices = dp_count * ns_count
    lay = Layout(dp_count, ns_count, fields.shape[0], fields.shape[1])
    z, x, n = lay.here()
    lat_count = lay.block_rows * dp_count

    ff_dev, e_own = up_t.shape[1], E // devices
    pack = -(-(2 * ff_dev + 2 * e_own) // 16) * 16

    def mine(values):
        return lax.dynamic_slice_in_dim(values, n * e_own, e_own, 0)

    def packed(up, down_, enc, dec_, extra):
        both = jnp.concatenate([wide(mine(enc)), wide(mine(dec_))], axis=1)
        return pad_rows(jnp.concatenate([up[0], down_[0], both, extra], axis=0), pack)

    def unpacked(every):
        up = every[:, :ff_dev].reshape(FF, E)
        down_ = every[:, ff_dev : 2 * ff_dev].reshape(FF, E)
        both = every[:, 2 * ff_dev : 2 * ff_dev + e_own].reshape(E, E)
        extra = every[:, 2 * ff_dev + e_own : 2 * ff_dev + 2 * e_own]
        return up, down_, both[:, :128], both[:, 128:], extra

    gain_rows = jnp.pad(mine(gains[0]), ((0, 0), (0, E - 2)))
    small = packed(up_t, down, enc_t, dec, gain_rows).astype(LOW)
    lon_count = fields.shape[2]

    def dense(values):
        fill = (-values.shape[-1] % 16, -lon_count % 128)
        values = values.transpose(0, 1, 3, 2)
        return jnp.pad(values, ((0, 0), (0, 0), (0, fill[0]), (0, fill[1])))

    def usual(values, count=C):
        values = values[:, :, :count, :lon_count].reshape((1, lay.rows, count, lon_count))
        return values.transpose(0, 1, 3, 2)

    swaps = [dense(fields), jnp.pad(valid, ((0, 0), (0, 0), (0, -lon_count % 128)))]
    spec_got, every_low, swaps = prologue(lay, spec_out(lay, spec[0]), small, swaps, 0)
    fields = usual(swaps[0])
    valid = swaps[1][..., :lon_count].reshape(1, lay.rows, lon_count)
    targets = [dense(targets[step]) for step in range(2)]
    up_w, down_w, enc_w, dec_w, extra = unpacked(every_low)
    enc_w, dec_w = enc_w[:, :C], dec_w[:, :C]
    gain_w = extra.reshape(E, E)[:, :2]
    spec_w = spec_in(lay, spec_got)

    colatitude = math.pi * (np.arange(lat_count) + 0.5) / lat_count
    sines = jnp.asarray(np.sin(colatitude).astype(np.float32).reshape(dp_count, lay.block_rows))
    local_sine = jnp.concatenate([sines[at] for at in lay.row_blocks(n, x)])
    var_weight = 1.0 + 0.5 * var_class.astype(FULL)
    pixel_map = valid.astype(FULL) * local_sine[None, :, None]
    weight_part = jnp.sum(pixel_map)
    weight_map = pixel_map[..., None] * var_weight
    weight_rows = jnp.broadcast_to(weight_part, (e_own, E))
    every_mom = lax.all_gather(packed(up_mom, down_mom, enc_mom, dec_mom, weight_rows), BOTH)
    loss_weight = jnp.sum(every_mom[:, 2 * ff_dev + e_own, 0]) * jnp.sum(var_weight)
    core_pack = -(-(2 * ff_dev + e_own) // 8) * 8

    def by_core(values):
        values = values.reshape((ns_count, dp_count // 2, 2) + values.shape[1:])
        return jnp.moveaxis(values, 2, 0)

    def by_device(values):
        return jnp.moveaxis(values, 0, 2).reshape((devices,) + values.shape[3:])

    moments = by_core(pad_rows(every_mom[:, : 2 * ff_dev + e_own], core_pack))

    tables = dft_tables(lay, fields.shape[2]) + legendre_tables(lay, lat_count)
    incoming = fields
    saved = []
    forecasts = []
    for step in range(2):
        weights = (spec_w, up_w, down_w, gain_w)
        hidden = jnp.einsum("brkc,ec->brke", incoming, enc_w, preferred_element_type=FULL)
        fetch, carry = ((True,), ()) if step == 0 else ((), (targets[1],))
        hidden, kept, given = forward_block(lay, hidden, weights, tables, 1 + step, fetch, carry)
        if step == 0:
            (spec_w,) = given.whole
        else:
            targets[1] = usual(given.carried[0])
        closing = hidden.astype(LOW)
        forecast = jnp.einsum("brke,ec->brkc", closing, dec_w, preferred_element_type=FULL)
        saved.append((incoming, kept, closing))
        forecasts.append(forecast)
        incoming = forecast.astype(LOW)

    def loss_of(step):
        error = forecasts[step] - targets[step].astype(FULL)
        return jnp.sum(weight_map * error * error), 2.0 * weight_map * error / loss_weight

    last_loss, gradient = loss_of(1)
    early, d_spec = (), ()
    aside = ff_dev % 8 == 0 and e_own % 8 == 0
    carry = (targets[0],)
    for step in (1, 0):
        incoming, kept, closing = saved[step]
        low_grad = gradient.astype(LOW)
        gradient = jnp.einsum("brkc,ec->brke", low_grad, dec_w, preferred_element_type=FULL)
        gradient, given, early, d_gain = backward_block(
            lay,
            gradient,
            kept,
            weights,
            tables,
            4 - step,
            d_spec,
            carry,
            early,
            closing,
            low_grad,
            aside,
        )
        d_spec, carry = given.d + given.g, ()
        squares = given.squares[0] if given.squares else None
        low_grad = gradient.astype(LOW)
        d_enc = jnp.einsum("brkc,brke->ec", incoming, low_grad, preferred_element_type=FULL)
        if step == 1:
            late = (d_gain, d_enc)
            targets[0] = usual(given.carried[0])
            first_loss, gradient = loss_of(0)
            gradient = gradient + jnp.einsum(
                "brke,ec->brkc", low_grad, enc_w, preferred_element_type=FULL
            )
            loss_local = first_loss + last_loss
    d_gain, d_enc = late[0] + d_gain, late[1] + d_enc
    g_spec = natural(spec_home(lay, d_spec[0], 5).astype(FULL)[None])
    near = jnp.concatenate([d_enc, d_gain, jnp.broadcast_to(loss_local, (E, 1))], axis=1)
    near = wide(near).reshape(devices, e_own, 128)
    if aside:
        blocks, given, at_enc = by_core(near), early, 0
    else:
        d_up, d_down, d_dec = early
        both = jnp.concatenate([near, wide(d_dec).reshape(near.shape)], axis=-1)
        blocks = [d_up.reshape(devices, ff_dev, E), d_down.reshape(devices, ff_dev, E), both]
        blocks = by_core(pad_rows(jnp.concatenate(blocks, axis=1), core_pack))
        given, at_enc = [], 2 * ff_dev
    masters = [up_t[0], up_mom[0], down[0], down_mom[0], enc_t, enc_mom, dec, dec_mom]
    every, scalars, new = finish(lay, blocks, given, moments, squares, ff_dev, e_own, 6)
    if aside:
        own = masters + [v[0].T for v in (gains, gain_m, gain_v)]
        new, (grad_norm, clip_scale, loss_sum) = update(scalars, new, own)
        new[8:] = [v.T for v in new[8:]]
    else:
        grad_norm, clip_scale, loss_sum = scalars[0, 0], scalars[0, 1], scalars[0, 2]
        (matrices,) = new
        d = lax.axis_index("dp")
        place = x * (ns_count // 2) + n // 2

        def enc_block(values):
            both = by_device(values[:, :, :, at_enc : at_enc + e_own])
            both = both.reshape(dp_count, lay.e_dev, E)
            return lax.dynamic_index_in_dim(both, d, keepdims=False)

        def muon(master, moment, gradient, matrix, factor):
            moment = MOMENTUM * moment + clip_scale * gradient
            return moment, master * (1.0 - RATE_MUON * DECAY) - RATE_MUON * (matrix * factor)

        grad, step = every[n % 2, z, place], matrices[n % 2, z, place]
        both_grad, both_step = enc_block(every), enc_block(matrices)
        new = []
        for at in range(4):
            begin = (0, ff_dev, 0, 128)[at]
            rows, columns = (FF, E) if at < 2 else (E, C)
            if at < 2:
                g, m = grad[begin : begin + ff_dev], step[begin : begin + ff_dev]
            else:
                g, m = both_grad[:, begin : begin + C], both_step[:, begin : begin + C]
            factor = math.sqrt(max(1.0, rows / columns))
            new += muon(masters[2 * at], masters[2 * at + 1], g, m, factor)
        g_gain = clip_scale * both_grad[:, C : C + 2]
        new += adam_step(gains[0], gain_m[0], gain_v[0], g_gain, RATE_GAIN)
    up_mom_new, up_new, down_mom_new, down_new = (v[None] for v in new[:4])
    enc_mom_new, enc_new, dec_mom_new, dec_new = new[4:8]
    gain_m_new, gain_v_new, gain_new = (v[None] for v in new[8:])
    spec_m_new, spec_v_new, spec_new = adam_step(
        spec, spec_m, spec_v, clip_scale * g_spec, RATE_SPECTRAL
    )
    return (
        loss_sum,
        loss_weight,
        grad_norm,
        enc_mom_new,
        enc_new,
        dec_mom_new,
        dec_new,
        up_mom_new,
        up_new,
        down_mom_new,
        down_new,
        spec_m_new,
        spec_v_new,
        spec_new,
        spec_new.astype(LOW),
        gain_m_new,
        gain_v_new,
        gain_new,
    )


def solution(mesh):
    rows = P(None, BOTH, None)
    shard = P("dp", None)
    whole = P(None, "dp", "ns", None, None)
    gain = P(None, "dp", None)
    placed = (
        P("ns", "dp", None, None),
        P(None, "ns", "dp", None, None),
        P("ns", "dp", None),
        P(),
        *[shard] * 4,
        *[whole] * 3,
        *[rows] * 4,
        *[gain] * 3,
    )
    return jax.shard_map(
        local,
        mesh=mesh,
        in_specs=placed,
        out_specs=(P(), P(), P(), *[shard] * 4, *[rows] * 4, *[whole] * 4, *[gain] * 3),
        check_vma=False,
    )
```

```python
import math
import types

import jax
import jax.numpy as jnp
import ml_dtypes
import numpy as np
from jax import lax
from jax.experimental import pallas as pl
from jax.experimental.layout import Layout as DeviceLayout
from jax.experimental.layout import with_layout_constraint
from jax.experimental.pallas import tpu as pltpu
from jax.sharding import PartitionSpec as P

E = 256
FF = 512
C = 73
LDEG = 96
MM = 96
NL = 1
NS_ITERS = 5
STEP = 10

EXACT = lax.Precision.HIGHEST
EPSILON = 1e-06
CLIP_NORM = 0.02
RATE_SPECTRAL = 0.05
RATE_GAIN = 0.1
RATE_MUON = 0.5
BETA_FIRST = 0.9
BETA_SECOND = 0.999
MOMENTUM = 0.95
DECAY = 0.01
NS_FIRST = 3.4445
NS_SECOND = -4.775
NS_THIRD = 2.0315
LOW = jnp.bfloat16
FULL = jnp.float32
MESH = pl.DeviceIdType.MESH
CHUNK = 16
BOTH = ("dp", "ns")


class Layout:
    def __init__(self, dp, ns, items, rows):
        self.dp, self.ns = dp, ns
        self.x, self.half, self.g = dp // ns, ns // 2, dp // 2
        self.block_rows, self.rows = rows, 2 * rows
        self.v = 2 if LDEG % (2 * dp) == 0 else 1
        self.owners = self.v * dp
        self.kper, self.lns = MM // self.g, LDEG // ns
        self.lper, self.lall = LDEG // self.owners, LDEG // dp
        self.kb = 8
        self.kd = self.kb * self.g // self.owners
        self.nkb = -(-self.kper // self.kb)
        self.blocks = [[i for i in range(self.lper) if i >= k * self.kd] for k in range(self.nkb)]
        self.counts = [len(b) for b in self.blocks]
        self.starts = np.cumsum([0] + self.counts).tolist()
        self.size = 2 * self.kb
        self.cols = self.rows * self.size
        self.ends = [min((k + 1) * self.kd, self.lper) for k in range(self.nkb)]
        self.ends[-1] = self.lper
        self.slots = -(-self.lns // dp)
        self.even = self.lns % dp == 0
        self.e_dev = E // dp
        self.e_plane = self.x * self.e_dev

    def here(self):
        d, n = lax.axis_index("dp"), lax.axis_index("ns")
        return d // self.x, d % self.x, n

    def row_blocks(self, n, x):
        return [(2 * (n % self.half) + s) * self.x + x for s in (0, 1)]

    def item_goes(self, at):
        z, x, n = self.here()
        plane = 2 * (n % self.half) + at
        to = n // self.half * self.half + z // 2
        return (plane * self.x + x, to), jnp.logical_and(plane == z, to == n)

    def item_comes(self, slot):
        z, x, n = self.here()
        return ((2 * (n % self.half) + slot) * self.x + x, n // self.half * self.half + z // 2)

    def stays(self):
        z, x, n = self.here()
        return z // 2 == n % self.half


def group_of(lay, kind):
    z, x, n = lay.here()
    if kind == "plane":
        return lay.dp, n * lay.x + x, lambda p: (z * lay.x + p % lay.x, p // lay.x)
    if kind == "owners":
        base = z // lay.v * lay.v
        return (
            lay.owners,
            (z - base) * lay.dp + n * lay.x + x,
            lambda p: ((base + p // lay.dp) * lay.x + p % lay.x, p % lay.dp // lay.x),
        )
    if kind == "half":
        first = n // lay.half * lay.half
        return (
            lay.g,
            n % lay.half * lay.x + x,
            lambda q: (z * lay.x + q % lay.x, first + q // lay.x),
        )
    return lay.ns, z, lambda q: (q * lay.x + x, n)


def exchange(lay, arrays, kinds, group, tag):
    count = {"plane": lay.dp, "line": lay.ns}[group]

    def kernel(*refs):
        total = len(arrays)
        ins, outs = refs[:total], refs[total : 2 * total]
        send, recv, own = refs[2 * total :]
        size, me, device = group_of(lay, group)
        barrier = pltpu.get_barrier_semaphore()

        @pl.loop(1, size)
        def _(step):
            pl.semaphore_signal(
                barrier, inc=1, device_id=device(lax.rem(me + step, size)), device_id_type=MESH
            )

        pl.semaphore_wait(barrier, size - 1)

        @pl.loop(1, size)
        def _(step):
            peer = lax.rem(me + step, size)
            for at in range(total):
                pltpu.make_async_remote_copy(
                    src_ref=ins[at].at[peer] if kinds[at] == "each" else ins[at],
                    dst_ref=outs[at].at[me],
                    send_sem=send.at[at],
                    recv_sem=recv.at[at],
                    device_id=device(peer),
                    device_id_type=MESH,
                ).start()

        for at in range(total):
            mine = ins[at].at[me] if kinds[at] == "each" else ins[at]
            copy = pltpu.make_async_copy(mine, outs[at].at[me], own)
            copy.start()
            copy.wait()
        for at in range(total):
            some = outs[at].at[pl.ds(0, size - 1)]
            pltpu.make_async_remote_copy(
                src_ref=some,
                dst_ref=some,
                send_sem=send.at[at],
                recv_sem=recv.at[at],
                device_id=device(lax.rem(me + 1, size)),
                device_id_type=MESH,
            ).wait()

    shapes = [
        jax.ShapeDtypeStruct(a.shape if k == "each" else (count,) + a.shape, a.dtype)
        for a, k in zip(arrays, kinds)
    ]
    spot = pl.BlockSpec(memory_space=pl.ANY)
    return pl.pallas_call(
        kernel,
        out_shape=shapes,
        in_specs=[spot] * len(arrays),
        out_specs=[spot] * len(arrays),
        scratch_shapes=[
            pltpu.SemaphoreType.DMA((len(arrays),)),
            pltpu.SemaphoreType.DMA((len(arrays),)),
            pltpu.SemaphoreType.DMA,
        ],
        compiler_params=pltpu.CompilerParams(collective_id=tag, has_side_effects=True),
        name=f"exchange_{group}_{tag}",
    )(*arrays)


def legendre(lat_count):
    colatitude = math.pi * (np.arange(lat_count) + 0.5) / lat_count
    cosine, log_sine = np.cos(colatitude)[None, :], np.log(np.sin(colatitude))[None, :]
    orders = np.arange(MM, dtype=np.float64)
    ladder = np.arange(1, MM, dtype=np.float64)
    sums = np.concatenate([[0.0], np.cumsum(np.log((2 * ladder - 1) / (2 * ladder)))])
    diagonal = np.exp(
        (0.5 * np.log((2 * orders + 1) / (4 * math.pi)) + 0.5 * sums)[:, None]
        + orders[:, None] * log_sine
    )
    table = np.zeros((LDEG, MM, lat_count))
    for degree in range(LDEG):
        for order in range(min(degree, MM - 1) + 1):
            if degree == order:
                table[degree, order] = diagonal[order]
                continue
            a = math.sqrt((4.0 * degree**2 - 1) / (degree**2 - order**2))
            value = cosine[0] * table[degree - 1, order]
            if degree >= 2:
                b = math.sqrt(
                    max((degree - 1.0) ** 2 - order**2, 0) / (4 * (degree - 1.0) ** 2 - 1)
                )
                value = value - b * table[degree - 2, order]
            table[degree, order] = a * value
    return table.astype(np.float32)


def low_table(values):
    return values.astype(np.float32).astype(ml_dtypes.bfloat16)


def dft_tables(lay, lon_count):
    turns = np.arange(lon_count)[:, None] * np.arange(MM)[None, :] % lon_count
    phases = 2 * math.pi / lon_count * turns
    paired = np.stack([np.cos(phases), -np.sin(phases)], axis=2)
    weight = np.where(np.arange(MM) == 0, 1.0, 2.0)
    forward = paired * (2 * math.pi / lon_count)
    inverse = paired * weight[None, :, None] / (2 * math.pi)

    def order(table):
        table = table.reshape(lon_count, lay.kper, lay.g, 2).transpose(0, 2, 1, 3)
        pad = lay.nkb * lay.kb - lay.kper
        table = np.pad(table, ((0, 0), (0, 0), (0, pad), (0, 0)))
        return low_table(table.reshape(lon_count, -1))

    return order(forward), order(inverse)


def legendre_tables(lay, lat_count):
    plain = legendre(lat_count)
    colatitude = math.pi * (np.arange(lat_count) + 0.5) / lat_count
    quadrature = 2 * math.pi * math.pi / lat_count * np.sin(colatitude)
    pad = lay.nkb * lay.kb - lay.kper

    def own(table):
        table = table.reshape(lay.lper, lay.owners, lay.kper, lay.g, lat_count)
        table = np.pad(table.transpose(3, 1, 0, 2, 4), ((0, 0), (0, 0), (0, 0), (0, pad), (0, 0)))
        table = low_table(table)
        blocks = []
        for k in range(lay.nkb):
            part = table[:, :, k * lay.kd :, k * lay.kb : (k + 1) * lay.kb]
            blocks.append(part.reshape(lay.g, -1, lay.kb * lat_count))
        across = [jnp.asarray(np.ascontiguousarray(b.swapaxes(1, 2))) for b in blocks]
        return jnp.asarray(np.concatenate(blocks, axis=1)), across

    col = np.arange(lay.g * lay.cols)
    col_part, col_k = col % 2, col // 2 % lay.kb
    member, row = col // lay.cols, col // lay.size % lay.rows
    block = (2 * (member // lay.x) + row // lay.block_rows) * lay.x + member % lay.x
    col_lat = block * lay.block_rows + row % lay.block_rows
    col_kind = col_part * lay.kb + col_k
    pick = col_k * lat_count + col_lat
    spread = np.arange(lay.kb * lat_count)[:, None] == pick[None, :]
    same = np.arange(lay.size)[:, None] == col_kind[None, :]
    wide_same = np.tile(same.T, (1, CHUNK))
    count = lay.owners * lay.lper
    repeat = np.arange(CHUNK * lay.size)[:, None] // lay.size == np.arange(CHUNK)[None, :]
    across = np.arange(count)[:, None] == np.arange(count * lay.size)[None, :] // lay.size
    ones = [
        jnp.asarray(v.astype(ml_dtypes.bfloat16))
        for v in (spread, spread.T, same, wide_same, repeat, across)
    ]
    return own(plain * quadrature.astype(np.float32)[None, None, :]), own(plain), ones


def normalize(values, gain_vec):
    return (
        values * lax.rsqrt(jnp.mean(values * values, axis=-1, keepdims=True) + EPSILON) * gain_vec
    )


def greet_senders(lay, greet):
    z, _, _ = lay.here()
    for slot in (0, 1):

        @pl.when(jnp.logical_not(jnp.logical_and(lay.stays(), z % 2 == slot)))
        def _():
            greet(lay.item_comes(slot))


class Swap:
    def __init__(self, lay, gone, come, sems):
        z, _, _ = lay.here()
        slot = z % 2
        self.here = [lay.item_goes(at)[1] for at in (0, 1)]
        self.far = [
            pltpu.make_async_remote_copy(
                src_ref=gone.at[at],
                dst_ref=come.at[slot],
                send_sem=sems[0],
                recv_sem=sems[1],
                device_id=lay.item_goes(at)[0],
                device_id_type=MESH,
            )
            for at in (0, 1)
        ]
        self.near = [
            pltpu.make_async_copy(gone.at[at], come.at[slot], sems[2]) for at in (0, 1)
        ]
        whole, one = come, come.at[0]
        self.stays = lay.stays()
        self.all_far, self.one_far = [
            pltpu.make_async_remote_copy(
                src_ref=ref,
                dst_ref=ref,
                send_sem=sems[0],
                recv_sem=sems[1],
                device_id=lay.item_goes(0)[0],
                device_id_type=MESH,
            )
            for ref in (whole, one)
        ]

    def start(self):
        for here, far, near in zip(self.here, self.far, self.near):

            @pl.when(here)
            def _():
                near.start()

            @pl.when(jnp.logical_not(here))
            def _():
                far.start()

    def wait(self):
        @pl.when(self.stays)
        def _():
            self.one_far.wait()
            self.near[0].wait()

        @pl.when(jnp.logical_not(self.stays))
        def _():
            self.all_far.wait()


class Total:
    def __init__(self, lay, put, every, scratch, sent, came):
        self.lay, self.put, self.every = lay, put, every
        self.pair_got, self.pair, self.line_got, self.line, self.plane_got = scratch
        self.sent, self.came = sent, came
        self.places, self.planes = lay.dp // 2, lay.ns
        self.z, self.x, n = lay.here()
        self.core, self.y, self.n, self.y_count = n % 2, n // 2, n, lay.ns // 2
        self.place = self.x * self.y_count + self.y

    @staticmethod
    def scratch(shape):
        whole = pltpu.VMEM(shape[1:], FULL)
        part = pltpu.VMEM(shape[2:], FULL)
        return [whole, whole, whole, part, part]

    def at_core(self):
        return (self.z * self.lay.x + self.x, self.n + 1 - 2 * self.core)

    def at_place(self, p):
        at = p % self.y_count * 2 + self.core
        return (self.z * self.lay.x + p // self.y_count, at)

    def at_plane(self, q):
        return (q * self.lay.x + self.x, self.n)

    def greet(self, greet):
        greet(self.at_core())

        @pl.loop(1, self.places)
        def _(step):
            greet(self.at_place(lax.rem(self.place + step, self.places)))

        @pl.loop(1, self.planes)
        def _(step):
            greet(self.at_plane(lax.rem(self.z + step, self.planes)))

        return self.places + self.planes - 1

    def remote(self, source, target, at, to):
        return pltpu.make_async_remote_copy(
            src_ref=source,
            dst_ref=target,
            send_sem=self.sent.at[at],
            recv_sem=self.came.at[at],
            device_id=to,
            device_id_type=MESH,
        )

    def settle(self, ref, at):
        self.remote(ref, ref, at, self.at_core()).wait()

    def at_chip(self, t):
        q, p = t // self.places, t % self.places
        at = p % self.y_count * 2 + self.core
        return (q * self.lay.x + p // self.y_count, at)

    def greet_chips(self, greet):
        count = self.places * self.planes
        greet(self.at_core())

        @pl.loop(1, count)
        def _(step):
            greet(self.at_chip(lax.rem(self.z * self.places + self.place + step, count)))

        return count

    def at_once(self, extra):
        core, z, place, count = self.core, self.z, self.place, self.places * self.planes
        every, mine = self.every, self.z * self.places + self.place

        def split(t):
            return t // self.places, t % self.places

        self.step(0)
        self.settle(self.pair_got, 0)
        self.pair[...] = self.put[core] + self.pair_got[...]

        @pl.loop(1, count)
        def _(step):
            to = lax.rem(mine + step, count)
            there = self.line_got.at[mine]
            self.remote(self.pair.at[split(to)], there, 1, self.at_chip(to)).start()

        self.line_got[mine] = self.pair[z, place]
        others = self.line_got.at[pl.ds(0, count - 1)]
        self.settle(others, 1)
        every[core, z, place] = jnp.sum(self.line_got[...], axis=0) + extra
        own = every.at[core, z, place]

        @pl.loop(1, count)
        def _(step):
            self.remote(own, own, 2, self.at_chip(lax.rem(mine + step, count))).start()

        self.settle(others, 2)
        self.remote(every.at[core], every.at[core], 5, self.at_core()).start()
        self.settle(every.at[core], 5)

    def pass_on(self, count, mine, stage, device, what):
        @pl.loop(1, count)
        def _(step):
            to = lax.rem(mine + step, count)
            source, target = what(to)
            self.remote(source, target, stage, device(to)).start()

    def step(self, stage, extra=None):
        core, place, z, places, planes = self.core, self.place, self.z, self.places, self.planes
        every, put = self.every, self.put
        if stage == 0:
            self.remote(put.at[1 - core], self.pair_got, 0, self.at_core()).start()
        if stage == 1:
            self.settle(self.pair_got, 0)
            for q in range(planes):
                self.pair[q] = put[core, q] + self.pair_got[q]
            there = self.line_got.at[z]
            self.pass_on(planes, z, 1, self.at_plane, lambda to: (self.pair.at[to], there))
        if stage == 2:
            self.line_got[z] = self.pair[z]
            self.settle(self.line_got.at[pl.ds(0, planes - 1)], 1)
            for p in range(places):
                total = self.line_got[0, p]
                for q in range(1, planes):
                    total = total + self.line_got[q, p]
                self.line[p] = total
            there = self.plane_got.at[place]
            self.pass_on(places, place, 2, self.at_place, lambda to: (self.line.at[to], there))
        if stage == 3:
            self.plane_got[place] = self.line[place]
            self.settle(self.plane_got.at[pl.ds(0, places - 1)], 2)
            total = self.plane_got[0]
            for p in range(1, places):
                total = total + self.plane_got[p]
            every[core, z, place] = total if extra is None else total + extra
            own = every.at[core, z, place]
            self.pass_on(planes, z, 3, self.at_plane, lambda to: (own, own))
        if stage == 4:
            self.settle(every.at[core, pl.ds(0, planes - 1), place], 3)
            own = every.at[core, pl.ds(0, planes), place]
            self.pass_on(places, place, 4, self.at_place, lambda to: (own, own))
        if stage == 5:
            self.settle(every.at[core, pl.ds(0, planes), pl.ds(0, places - 1)], 4)
            self.remote(every.at[core], every.at[core], 5, self.at_core()).start()
        if stage == 6:
            self.settle(every.at[core], 5)


def turned(real, imag):
    both = jnp.concatenate([real[:, None], imag[:, None]], axis=1)
    return both.reshape(-1, E).astype(LOW)


def parts_of(values):
    split = values.reshape(-1, 2, 8, E)
    return split[:, 0], split[:, 1]


def spectral(
    lay,
    values,
    first,
    second,
    ones,
    tag,
    spec_w,
    fetch=(),
    carry=(),
    saved=(),
    earlier=(),
    parts=(),
):
    back, last = bool(saved), bool(earlier)
    placed = spec_w.ndim == 5
    nkb, dp, ns, size, half = lay.nkb, lay.owners, lay.ns, lay.size, lay.g
    counts, ends, lper = lay.counts, lay.ends, lay.lper
    items, rows = values.shape[:2]
    laid = values.reshape(items, rows, half, nkb, size, E)
    laid = laid.transpose(2, 3, 0, 1, 4, 5).reshape(half, nkb, lay.cols, E)
    w_shape = (ns, lper, 2, lay.e_plane, E)
    dma = pltpu.SemaphoreType.DMA
    tiles = [(dp, c, size, E) for c in counts]
    spans = [(g * lay.kd, ends[g] - g * lay.kd) for g in range(nkb)]

    ins = dict(f=[laid], p1=[first], p2=list(second), ones=list(ones), w=[spec_w])
    ins |= dict(old=list(saved), earlier=list(earlier), carry=list(carry))
    outs = dict(y=[((half, nkb, lay.cols, E), LOW)])
    outs |= dict(keep=[] if back else [(t, LOW) for t in tiles])
    outs |= dict(whole=[(w_shape, LOW)] if fetch else [])
    outs |= dict(d=[(w_shape, LOW)] if back and not last else [])
    owned = (lay.lall, lay.x, 2, lay.e_dev, E)
    if lay.even:
        owned = (lay.dp, lay.slots, 2, lay.e_dev, E)
    outs |= dict(g=[(owned, LOW)] if last else [])
    outs |= dict(squares=[((8, 128), FULL)] if last else [])
    outs |= dict(carried=[(c.shape, c.dtype) for c in carry])
    ins |= dict(parts=list(parts))
    devices = lay.dp * ns
    part_rows = [v.shape[0] // devices for v in parts]
    every_shape = (2, ns, lay.dp // 2, sum(part_rows), E)
    outs |= dict(every=[(every_shape, FULL)] if parts else [])
    tall, broad = lay.size * dp * np.array(counts), half * lay.cols
    buffers = dict(
        f_got=[((nkb, half, lay.cols, E), LOW)],
        t1=[((int(h), broad), LOW) for h in tall],
        t2=[((broad, int(h)), LOW) for h in tall],
        p1_v=[(first.shape[1:], LOW)],
        p2_v=[(p.shape[1:], LOW) for p in second],
        ones_v=[(o.shape, LOW) for o in ones],
        w_v=[(w_shape, LOW)],
        s_put=[(t, LOW) for t in tiles],
        s_got=[(t, LOW) for t in tiles],
        m_put=[(t, LOW) for t in tiles],
        m_got=[(t, LOW) for t in tiles],
        y_put=[((half, nkb, lay.cols, E), LOW)],
        old_v=[(t, LOW) for t in tiles] if back else [],
        early_v=[(w_shape, LOW)] if last else [],
        d_put=[(w_shape, LOW)] if back else [],
        d_got=[(w_shape, LOW)] if last else [],
        g_put=[((lay.lall, lay.x, 2, lay.e_dev, E), LOW)] if last else [],
        part_v=[(v.shape, FULL) for v in parts],
        total=[(v.shape, FULL) for v in Total.scratch(every_shape)] if parts else [],
        square_v=[((8, 128), FULL)] if last else [],
        put_v=[(every_shape, FULL)] * 2 if parts else [],
    )
    sems = dict(f_sem=nkb, s_sem=nkb, m_sem=nkb, y_sem=1, send=4, own=nkb + 4)
    sems |= dict(load=2 + len(second) + len(ones) + len(saved) + 1)
    sems |= dict(part_sem=len(parts) + 1, total_sent=6, total_came=6)
    sems |= dict(line_send=1, line_got=nkb, own_w=1, carry_sem=4, g_sem=2)

    def kernel(*refs):
        refs = list(refs)
        r = types.SimpleNamespace()
        for group in (ins, outs, buffers):
            for name, entries in group.items():
                setattr(r, name, refs[: len(entries)])
                del refs[: len(entries)]
        for name in sems:
            setattr(r, name, refs.pop(0))
        (f_ref,), (y_ref,), (f_got,), (y_put,), (w,) = r.f, r.y, r.f_got, r.y_put, r.w_v
        t1, t2, s_put, s_got, m_put, m_got = r.t1, r.t2, r.s_put, r.s_got, r.m_put, r.m_got
        spread, spread_t, same, wide_same, repeat, across = r.ones_v
        send, own = r.send, r.own
        z, x, n = lay.here()
        _, me, device = group_of(lay, "owners")
        _, place_at, plane_device = group_of(lay, "plane")
        _, mine_at, half_device = group_of(lay, "half")
        _, _, line_device = group_of(lay, "line")
        line = bool(fetch) or last
        barrier = pltpu.get_barrier_semaphore()

        def greet(target):
            pl.semaphore_signal(barrier, inc=1, device_id=target, device_id_type=MESH)

        @pl.loop(1, dp)
        def _(step):
            greet(device(lax.rem(me + step, dp)))

        if line:

            @pl.loop(1, ns)
            def _(step):
                greet(line_device(lax.rem(z + step, ns)))

        if carry:
            greet_senders(lay, greet)
        waits = dp - 1 + (ns - 1 if line else 0)
        if parts:
            put, every = r.put_v
            summed = Total(lay, put, every, r.total, r.total_sent, r.total_came)
            waits = waits + summed.greet(greet)
            for at, ref in enumerate(r.part_v):
                pltpu.make_async_copy(r.parts[at], ref, r.part_sem.at[at]).start()
        pairs = [(r.p1[0].at[mine_at], r.p1_v[0])]
        pairs += [(a, b) for a, b in zip(r.ones, r.ones_v)]
        pairs += [(a.at[mine_at], b) for a, b in zip(r.p2, r.p2_v)]
        tables_at = len(pairs)
        if not fetch:
            pairs += [(r.w[0], w)]
        pairs += list(zip(r.old, r.old_v)) + list(zip(r.earlier, r.early_v))
        loads = []
        for at, (source, target) in enumerate(pairs):
            copy = pltpu.make_async_copy(source, target, r.load.at[at])
            copy.start()
            loads.append(copy)
        mine = []
        for k in range(nkb):
            copy = pltpu.make_async_copy(f_ref.at[mine_at, k], f_got.at[k, mine_at], own.at[k])
            copy.start()
            mine.append(copy)
        if carry:
            pl.semaphore_wait(barrier, waits + jnp.where(lay.stays(), 1, 2))
        else:
            pl.semaphore_wait(barrier, waits)

        def remote(source, target, sent, got, to):
            return pltpu.make_async_remote_copy(
                src_ref=source,
                dst_ref=target,
                send_sem=sent,
                recv_sem=got,
                device_id=to,
                device_id_type=MESH,
            )

        def push(source, target, sent, got, peer):
            remote(source, target, sent, got, device(peer)).start()

        def settle(ref, sent, got, sending):
            copy = remote(ref, ref, sent, got, device(lax.rem(me + 1, dp)))
            if sending:
                copy.wait_send()
            else:
                copy.wait_recv()

        for k in range(nkb):

            @pl.loop(1, half)
            def _(step):
                peer = lax.rem(mine_at + step, half)
                target = f_got.at[k, mine_at]
                sem = r.f_sem.at[k]
                remote(f_ref.at[peer, k], target, send.at[0], sem, half_device(peer)).start()

        if fetch:
            share = r.w[0].at[z] if placed else r.w[0]

            def share_of(to, degree):
                return share.at[degree * lay.v + lax.rem(to, lay.v)]

            for g in range(nkb):

                @pl.loop(*(spans[g][0], ends[g]))
                def _(degree):
                    pltpu.make_async_copy(
                        share_of(z, degree), w.at[z, degree], r.own_w.at[0]
                    ).start()
                    for step in range(1, ns):
                        to = lax.rem(z + step, ns)
                        remote(
                            share_of(to, degree),
                            w.at[z, degree],
                            r.line_send.at[0],
                            r.line_got.at[g],
                            line_device(to),
                        ).start()

        if carry:
            (gone,), (come,) = r.carry, r.carried
            swap = Swap(lay, gone, come, [r.carry_sem.at[at] for at in range(4)])
            swap.start()

        if parts:
            begin = 0
            for at, (ref, count) in enumerate(zip(r.part_v, part_rows)):
                pltpu.make_async_copy(r.parts[at], ref, r.part_sem.at[at]).wait()
                width = ref.shape[1]
                for index in range(devices):
                    d, n_at = divmod(index, ns)
                    place = d % lay.x * (ns // 2) + n_at // 2
                    block = put.at[n_at % 2, d // lay.x, place, pl.ds(begin, count)]
                    if width < E:
                        block[...] = jnp.zeros((count, E), FULL)
                    block[:, :width] = ref[pl.ds(index * count, count), :]
                begin += count
            summed.step(0)

        for at in range(tables_at):
            loads[at].wait()
        for k in range(nkb):

            @pl.loop(0, dp * counts[k] // CHUNK)
            def _(chunk):
                at = pl.multiple_of(dp * lay.starts[k] + chunk * CHUNK, CHUNK)
                part = r.p1_v[0][pl.ds(at, CHUNK), :]
                part = jnp.dot(repeat[...], part, preferred_element_type=FULL).astype(LOW)
                full = jnp.dot(part, spread[...], preferred_element_type=FULL)
                full = full.reshape(CHUNK, size, broad) * same[...].astype(FULL)[None]
                to = pl.multiple_of(chunk * CHUNK * size, CHUNK * size)
                t1[k][pl.ds(to, CHUNK * size), :] = full.reshape(CHUNK * size, broad).astype(LOW)

        if parts:
            summed.step(1)

        for k in range(nkb):
            mine[k].wait()
            settle(f_got.at[k, pl.ds(0, half - 1)], send.at[0], r.f_sem.at[k], False)
            high = counts[k] * size

            def modes_for(peer):
                part = t1[k][pl.ds(pl.multiple_of(peer * high, 16), high), :]
                got = f_got[k].reshape(half * lay.cols, E)
                out = jnp.dot(part, got, preferred_element_type=FULL).astype(LOW)
                return out.reshape(counts[k], size, E)

            @pl.loop(1, dp)
            def _(step):
                peer = lax.rem(me + step, dp)
                s_put[k][peer] = modes_for(peer)
                push(s_put[k].at[peer], s_got[k].at[me], send.at[1], r.s_sem.at[k], peer)

            s_got[k][me] = modes_for(me)

        if parts:
            summed.step(2)
        for k in range(nkb):
            width = CHUNK * size
            count = dp * counts[k]

            @pl.loop(0, count // CHUNK)
            def _(chunk):
                to = pl.ds(pl.multiple_of(chunk * width, width), width)
                part = jnp.dot(
                    r.p2_v[k][...], across[pl.ds(0, count), to], preferred_element_type=FULL
                )
                full = jnp.dot(spread_t[...], part.astype(LOW), preferred_element_type=FULL)
                t2[k][:, to] = (full * wide_same[...].astype(FULL)).astype(LOW)

        if parts:
            summed.step(3)

        for copy in loads[tables_at:]:
            copy.wait()
        def rows_at(group, degree, g):
            tiles = [group[k][:, degree - k * lay.kd] for k in range(g + 1)]
            return jnp.concatenate([t.reshape(dp * size, E) for t in tiles], axis=0)

        if fetch:
            pltpu.make_async_copy(w.at[z], w.at[z], r.own_w.at[0]).wait()
        for g, (begin, length) in enumerate(spans):
            settle(s_got[g].at[pl.ds(0, dp - 1)], send.at[1], r.s_sem.at[g], False)
            span = pl.ds(begin, length)
            if fetch:
                got = w.at[pl.ds(0, ns - 1), span]
                settle(got, r.line_send.at[0], r.line_got.at[g], False)

            @pl.loop(begin, ends[g])
            def _(degree):
                rows_in = rows_at(s_got, degree, g)
                dims = (((1,), (1 if back else 0,)), ((), ()))
                by_real, by_imag = (
                    lax.dot_general(
                        rows_in, w[:, degree, p].reshape(E, E), dims, preferred_element_type=FULL
                    )
                    for p in (0, 1)
                )
                (rr, ir), (ri, ii) = parts_of(by_real), parts_of(by_imag)
                mixed = turned(rr + ii, ir - ri) if back else turned(rr - ii, ri + ir)
                for k in range(g + 1):
                    part = mixed[k * dp * size : (k + 1) * dp * size]
                    m_put[k][:, degree - k * lay.kd] = part.reshape(dp, size, E)

            for k in range(g + 1):
                there = pl.ds(begin - k * lay.kd, length)

                @pl.loop(1, dp)
                def _(step):
                    peer = lax.rem(me + step, dp)
                    target = m_got[k].at[me, there]
                    push(m_put[k].at[peer, there], target, send.at[2], r.m_sem.at[k], peer)

        if back:
            (d_put,) = r.d_put
            for g, (begin, length) in enumerate(spans):
                span = pl.ds(begin, length)

                @pl.loop(begin, ends[g])
                def _(degree):
                    dims = (((0,), (0,)), ((), ()))
                    olds, grads = rows_at(r.old_v, degree, g), rows_at(s_got, degree, g)
                    real, imag = parts_of(grads.astype(FULL))
                    for p, right in ((0, grads), (1, turned(imag, -real))):
                        total = lax.dot_general(olds, right, dims, preferred_element_type=FULL)
                        total = total.reshape(ns, lay.e_plane, E)
                        if last:
                            total = total + r.early_v[0][:, degree, p].astype(FULL)
                        d_put[:, degree, p] = total.astype(LOW)

                if last:
                    (d_got,) = r.d_got

                    @pl.loop(1, ns)
                    def _(step):
                        to = lax.rem(z + step, ns)
                        remote(
                            d_put.at[to, span],
                            d_got.at[z, span],
                            r.line_send.at[0],
                            r.line_got.at[g],
                            line_device(to),
                        ).start()

                    d_got[z, span] = d_put[z, span]

        if parts:
            summed.step(4)
        for k in range(nkb):
            m_got[k][me] = m_put[k][me]
        keeps = []
        for at, (source, target) in enumerate(
            list(zip(s_got, r.keep)) + [(w, t) for t in r.whole] + list(zip(r.d_put, r.d))
        ):
            copy = pltpu.make_async_copy(source, target, own.at[at])
            copy.start()
            keeps.append(copy)

        for k in range(nkb):
            settle(m_got[k].at[pl.ds(0, dp - 1)], send.at[2], r.m_sem.at[k], False)

            def rows_for(peer):
                part = t2[k][pl.ds(pl.multiple_of(peer * lay.cols, 16), lay.cols), :]
                got = m_got[k][...].reshape(-1, E)
                return jnp.dot(part, got, preferred_element_type=FULL).astype(LOW)

            @pl.loop(1, half)
            def _(step):
                peer = lax.rem(mine_at + step, half)
                y_put[peer, k] = rows_for(peer)
                target, sem = y_ref.at[mine_at, k], r.y_sem.at[0]
                remote(y_put.at[peer, k], target, send.at[3], sem, half_device(peer)).start()

            y_put[mine_at, k] = rows_for(mine_at)
        ends_with = pltpu.make_async_copy(y_put.at[mine_at], y_ref.at[mine_at], own.at[nkb + 2])
        ends_with.start()

        if parts:
            summed.step(5)
        if last:
            (g_put,), (g_ref,), (square_v,) = r.g_put, r.g, r.square_v
            square_v[...] = jnp.zeros_like(square_v)
            for g, (begin, length) in enumerate(spans):
                if parts and g == nkb - 1:
                    summed.step(6)
                    pltpu.make_async_copy(every, r.every[0], r.part_sem.at[len(parts)]).start()
                got = d_got.at[pl.ds(0, ns - 1), pl.ds(begin, length)]
                settle(got, r.line_send.at[0], r.line_got.at[g], False)

                @pl.loop(begin * lay.v, ends[g] * lay.v)
                def _(at):
                    degree, s_at = at // lay.v, lax.rem(at, lay.v)
                    for p in (0, 1):
                        total = d_got[s_at, degree, p].astype(FULL)
                        for first_plane in range(lay.v, ns, lay.v):
                            total = total + d_got[first_plane + s_at, degree, p].astype(FULL)
                        folded = (total * total).reshape(-1, 8, E).sum(axis=0)
                        square_v[...] += folded[:, :128] + folded[:, 128:]
                        g_put[at, :, p] = total.astype(LOW).reshape(lay.x, lay.e_dev, E)
                    if lay.even:
                        slot = lax.rem(at, lay.slots)
                        for at_x in range(lay.x):
                            peer = at // lay.slots * lay.x + at_x

                            @pl.when(peer != place_at)
                            def _():
                                remote(
                                    g_put.at[at, at_x],
                                    g_ref.at[place_at, slot],
                                    r.g_sem.at[0],
                                    r.g_sem.at[1],
                                    plane_device(peer),
                                ).start()

            if lay.even:
                copy = pltpu.make_async_copy(
                    g_put.at[pl.ds(n * lay.slots, lay.slots), x], g_ref.at[place_at], own.at[nkb + 3]
                )
            else:
                copy = pltpu.make_async_copy(g_put, g_ref, own.at[nkb + 3])
            copy.start()
            copy.wait()
            copy = pltpu.make_async_copy(square_v, r.squares[0], own.at[nkb + 3])
            copy.start()
            copy.wait()
            if lay.even:
                some = g_ref.at[pl.ds(0, lay.dp - 1)]
                settle(some, r.g_sem.at[0], r.g_sem.at[1], True)
                settle(some, r.g_sem.at[0], r.g_sem.at[1], False)

        if parts:
            pltpu.make_async_copy(every, r.every[0], r.part_sem.at[len(parts)]).wait()
        ends_with.wait()
        for copy in keeps:
            copy.wait()
        settle(f_ref.at[pl.ds(0, half - 1)], send.at[0], r.f_sem.at[0], True)
        for k in range(nkb):
            settle(s_got[k].at[pl.ds(0, dp - 1)], send.at[1], r.s_sem.at[0], True)
            settle(m_got[k].at[pl.ds(0, dp - 1)], send.at[2], r.m_sem.at[0], True)
        if line:
            settle(w.at[pl.ds(0, ns - 1)], r.line_send.at[0], r.line_got.at[0], True)
        if carry:
            swap.wait()
        settle(y_put.at[pl.ds(0, half - 1)], send.at[3], r.y_sem.at[0], True)
        settle(y_put.at[pl.ds(0, half - 1)], send.at[3], r.y_sem.at[0], False)

    spot = pl.BlockSpec(memory_space=pl.ANY)
    operands = [v for group in ins.values() for v in group]
    steady = {id(v) for v in [first, *second, *ones]}
    places = [pl.BlockSpec(memory_space=pltpu.HBM) if id(v) in steady else spot for v in operands]
    results = [jax.ShapeDtypeStruct(*v) for group in outs.values() for v in group]
    scratch = [pltpu.VMEM(*v) for group in buffers.values() for v in group]
    need = sum(math.prod(shape[:-1]) * -(-shape[-1] // 128) * 128 * np.dtype(kind).itemsize
               for group in buffers.values() for shape, kind in group)
    scratch += [dma((count,)) for count in sems.values()]
    got = list(
        pl.pallas_call(
            kernel,
            out_shape=results,
            in_specs=places,
            out_specs=[spot] * len(results),
            scratch_shapes=scratch,
            compiler_params=pltpu.CompilerParams(
                collective_id=tag,
                has_side_effects=True,
                vmem_limit_bytes=min(58 << 20, need + (10 << 20)),
            ),
            cost_estimate=pl.CostEstimate(
                flops=40_000_000_000, bytes_accessed=100_000_000, transcendentals=0
            ),
            name="spectral_back" if back else "spectral",
        )(*operands)
    )
    given = types.SimpleNamespace()
    for name, entries in outs.items():
        setattr(given, name, got[: len(entries)])
        del got[: len(entries)]
    rows_out = given.y[0].reshape(half, nkb, items, rows, size, E)
    rows_out = rows_out.transpose(2, 3, 0, 1, 4, 5).reshape(items, rows, -1, E)
    return rows_out, given


def prologue(lay, spec_laid, small, swaps, tag):
    def kernel(*refs):
        spec_ref, small_ref = refs[:2]
        swap_refs = refs[2 : 2 + len(swaps)]
        spec_got, small_got = refs[2 + len(swaps) : 4 + len(swaps)]
        swap_got = refs[4 + len(swaps) : 4 + 2 * len(swaps)]
        sent, got, own, swap_sem = refs[4 + 2 * len(swaps) :]
        z, x, n = lay.here()
        _, me, device = group_of(lay, "plane")
        core, y_count, places = n % 2, lay.ns // 2, lay.dp // 2
        place = x * y_count + n // 2
        sibling = (z * lay.x + x, n + 1 - 2 * core)

        def at_plane(q):
            return q * lay.x + x, n

        def at_place(p):
            return z * lay.x + p // y_count, p % y_count * 2 + core

        barrier = pltpu.get_barrier_semaphore()

        def greet(target):
            pl.semaphore_signal(barrier, inc=1, device_id=target, device_id_type=MESH)

        @pl.loop(1, lay.dp)
        def _(step):
            greet(device(lax.rem(me + step, lay.dp)))

        @pl.loop(1, lay.ns)
        def _(step):
            greet(at_plane(lax.rem(z + step, lay.ns)))

        greet_senders(lay, greet)
        pl.semaphore_wait(barrier, lay.dp + lay.ns - 2 + jnp.where(lay.stays(), 1, 2))

        def remote(source, target, at, to):
            return pltpu.make_async_remote_copy(
                src_ref=source,
                dst_ref=target,
                send_sem=sent.at[at],
                recv_sem=got.at[at],
                device_id=to,
                device_id_type=MESH,
            )

        def spec_here():
            if lay.even:
                return spec_got.at[z, pl.ds(n * lay.slots, lay.slots), :, x]
            return spec_got.at[me]

        copy = pltpu.make_async_copy(small_ref, small_got.at[core, z, place], own.at[0])
        copy.start()

        @pl.loop(1, lay.ns)
        def _(step):
            to = at_plane(lax.rem(z + step, lay.ns))
            remote(small_ref, small_got.at[core, z, place], 1, to).start()

        moves = [
            Swap(lay, a, b, [swap_sem.at[at, k] for k in range(3)])
            for at, (a, b) in enumerate(zip(swap_refs, swap_got))
        ]
        for move in moves:
            move.start()
        @pl.loop(1, lay.dp)
        def _(step):
            peer = lax.rem(me + step, lay.dp)
            remote(spec_ref.at[peer], spec_here(), 0, device(peer)).start()

        pltpu.make_async_copy(spec_ref.at[me], spec_here(), got.at[0]).start()
        copy.wait()
        some = small_got.at[core, pl.ds(0, lay.ns - 1), place]
        remote(some, some, 1, sibling).wait()
        column = small_got.at[core, pl.ds(0, lay.ns), place]

        @pl.loop(1, places)
        def _(step):
            remote(column, column, 3, at_place(lax.rem(place + step, places))).start()

        some = small_got.at[core, pl.ds(0, lay.ns), pl.ds(0, places - 1)]
        remote(some, some, 3, sibling).wait()
        remote(small_got.at[core], small_got.at[core], 2, sibling).start()
        some = spec_ref.at[pl.ds(0, lay.dp - 1)]
        every = spec_got.at[z] if lay.even else spec_got
        remote(every, every, 0, sibling).wait_recv()
        remote(some, some, 0, sibling).wait_send()
        remote(small_got.at[core], small_got.at[core], 2, sibling).wait()
        for move in moves:
            move.wait()

    spot = pl.BlockSpec(memory_space=pl.ANY)
    w_shape = (lay.ns, lay.lall, 2, lay.x, lay.e_dev, E)
    spec_shape = jax.ShapeDtypeStruct(w_shape, LOW) if lay.even else spec_laid
    small_shape = (2, lay.ns, lay.dp // 2) + small.shape
    outs = [spec_shape, jax.ShapeDtypeStruct(small_shape, small.dtype), *swaps]
    count = 4
    got = pl.pallas_call(
        kernel,
        out_shape=[jax.ShapeDtypeStruct(o.shape, o.dtype) for o in outs],
        in_specs=[spot] * (2 + len(swaps)),
        out_specs=[spot] * len(outs),
        scratch_shapes=[
            pltpu.SemaphoreType.DMA((count,)),
            pltpu.SemaphoreType.DMA((count,)),
            pltpu.SemaphoreType.DMA((2,)),
            pltpu.SemaphoreType.DMA((len(swaps), 3)),
        ],
        compiler_params=pltpu.CompilerParams(collective_id=tag, has_side_effects=True),
        name="prologue",
    )(spec_laid, small, *swaps)
    every = jnp.moveaxis(got[1], 0, 2).reshape((lay.dp * lay.ns,) + small.shape)
    return got[0], every, list(got[2:])


def spec_out(lay, spec):
    z, x, n = lay.here()
    low = spec.astype(LOW).transpose(1, 2, 0, 3)
    tail = (2, lay.e_dev, E)
    if lay.even:
        laid = low.reshape((lay.slots, lay.dp) + tail).swapaxes(0, 1)
    else:
        at = (jnp.arange(lay.dp) - lay.lns * n) % lay.dp
        at = at[:, None] + lay.dp * jnp.arange(lay.slots)
        laid = jnp.take(low, jnp.minimum(at, lay.lns - 1), axis=0)
    return laid


def spec_in(lay, got):
    z, x, n = lay.here()
    if lay.even:
        return got.reshape(lay.ns, lay.lall, 2, lay.e_plane, E)
    member = n * lay.x + x
    got = got.reshape((lay.ns, lay.x, lay.slots, 2, lay.e_dev, E))
    got = got.transpose(0, 2, 3, 1, 4, 5).reshape(lay.ns, lay.slots, 2, lay.e_plane, E)
    degree = lay.dp * jnp.arange(lay.lall) + member
    return got[degree // lay.lns, degree % lay.lns // lay.dp]


def spec_home(lay, given, tag):
    z, x, n = lay.here()
    member = n * lay.x + x
    if lay.even:
        mine = given.swapaxes(0, 1).reshape(lay.lns, 2, lay.e_dev, E)
        return mine.transpose(2, 0, 1, 3)
    first = (member - lay.lns * jnp.arange(lay.ns)) % lay.dp + lay.lns * jnp.arange(lay.ns)
    at = (first[:, None] + lay.dp * jnp.arange(lay.slots) - member) // lay.dp
    slots = given[jnp.clip(at, 0, lay.lall - 1)]
    slots = slots.transpose(0, 2, 1, 3, 4, 5)
    (back,) = exchange(lay, [slots.reshape(lay.dp, -1, E)], ["each"], "plane", tag)
    back = back.reshape(lay.dp, lay.slots, 2, lay.e_dev, E)
    degree = lay.lns * n + jnp.arange(lay.lns)
    source = degree % lay.dp
    slot = (jnp.arange(lay.lns) - (source - lay.lns * n) % lay.dp) // lay.dp
    return back[source, slot].transpose(2, 0, 1, 3)


def pad_rows(values, rows):
    return jnp.pad(values, ((0, 0),) * (values.ndim - 2) + ((0, rows - values.shape[-2]), (0, 0)))


def wide(values):
    return jnp.pad(values, ((0, 0),) * (values.ndim - 1) + ((0, 128 - values.shape[-1]),))


def forward_block(lay, residual, weights, tables, tag, fetch, carry):
    spec_w, up_w, down_w, gain_low = weights
    gain_vec = gain_low.astype(FULL)
    dft_fwd, dft_inv, quad_tab, plain_tab, ones = tables
    normed_a = normalize(residual, gain_vec[:, 0]).astype(LOW)
    fourier = jnp.einsum("brke,kq->brqe", normed_a, dft_fwd, preferred_element_type=FULL)
    restored, given = spectral(
        lay, fourier.astype(LOW), quad_tab[0], plain_tab[1], ones, tag, spec_w, fetch, carry
    )
    middle = residual + jnp.einsum(
        "brqe,kq->brke", restored, dft_inv, preferred_element_type=FULL
    )
    normed_b = normalize(middle, gain_vec[:, 1]).astype(LOW)
    pre_act = jnp.einsum("brke,fe->brkf", normed_b, up_w, preferred_element_type=FULL)
    hidden = jax.nn.gelu(pre_act).astype(LOW)
    output = middle + jnp.einsum("brkf,fe->brke", hidden, down_w, preferred_element_type=FULL)
    return (output, (residual, given.keep, middle, normed_b, pre_act, hidden), given)


def backward_block(
    lay, output_gradient, saved, weights, tables, tag, earlier, carry, sums, closing, low_grad, aside
):
    residual, spectrum, middle, normed_b, pre_act, hidden = saved
    spec_w, up_w, down_w, gain_low = weights
    gain_vec = gain_low.astype(FULL)
    dft_fwd, dft_inv, quad_tab, plain_tab, ones = tables
    g_out = output_gradient.astype(LOW)
    d_hidden = jnp.einsum("brke,fe->brkf", g_out, down_w, preferred_element_type=FULL)
    d_pre = jax.vjp(jax.nn.gelu, pre_act)[1](d_hidden)[0].astype(LOW)
    d_normed_b = jnp.einsum("brkf,fe->brke", d_pre, up_w, preferred_element_type=FULL)
    d_mid_part, d_gain_b = jax.vjp(normalize, middle, gain_vec[:, 1])[1](d_normed_b)
    d_middle = output_gradient + d_mid_part
    d_restored = jnp.einsum(
        "brke,kq->brqe", d_middle.astype(LOW), dft_inv, preferred_element_type=FULL
    ).astype(LOW)
    products = [
        jnp.einsum("brkf,brke->fe", a, b, preferred_element_type=FULL)
        for a, b in ((d_pre, normed_b), (hidden, g_out), (closing, low_grad))
    ]
    sums = [a + b for a, b in zip(sums, products)] if sums else products
    d_restored, sums = lax.optimization_barrier((d_restored, sums))
    d_fourier, given = spectral(
        lay,
        d_restored,
        plain_tab[0],
        quad_tab[1],
        ones,
        tag,
        spec_w,
        carry=carry,
        saved=spectrum,
        earlier=earlier,
        parts=sums if aside and earlier else (),
    )
    d_normed_a = jnp.einsum("brqe,kq->brke", d_fourier, dft_fwd, preferred_element_type=FULL)
    d_res_part, d_gain_a = jax.vjp(normalize, residual, gain_vec[:, 0])[1](d_normed_a)
    d_gain = jnp.stack([d_gain_a, d_gain_b], axis=1)
    sums = given.every or sums
    return d_middle + d_res_part, given, sums, d_gain


def product(left, right, dims):
    parts = []
    for value in (left, right):
        high = value.astype(LOW)
        parts.append((high, (value - high.astype(FULL)).astype(LOW)))
    (a, a_rest), (b, b_rest) = parts

    def dot(p, q):
        return lax.dot_general(p, q, (dims, ((), ())), preferred_element_type=FULL)

    return dot(a, b) + (dot(a, b_rest) + dot(a_rest, b))


def finish(lay, blocks, given, moments, extra, ff_dev, e_own, tag):
    planes, places, pack = moments.shape[1:4]
    count = 2 * places * planes
    at_enc = 0 if given else 2 * ff_dev
    rows, lanes = blocks.shape[3:]

    def kernel(blocks_ref, moment_ref, extra_ref, *refs):
        given_ref = refs[0] if given else None
        refs = refs[len(given) :]
        every_ref, scalars_ref = refs[:2]
        new_refs, scratch = refs[2 : 2 + len(results)], refs[2 + len(results) :]
        mats, sent, came = scratch[5 : 5 + len(mat_shapes)], scratch[-2], scratch[-1]
        summed = Total(lay, blocks_ref, every_ref, scratch[:5], sent, came)
        barrier = pltpu.get_barrier_semaphore()

        def greet(target):
            pl.semaphore_signal(barrier, inc=1, device_id=target, device_id_type=MESH)

        pl.semaphore_wait(barrier, summed.greet_chips(greet))
        at_row = lax.broadcasted_iota(jnp.int32, (rows, lanes), 0) == at_enc
        at_lane = lax.broadcasted_iota(jnp.int32, (rows, lanes), 1) == C + 3
        squares = jnp.sum(extra_ref[...], keepdims=True)
        added = jnp.where(jnp.logical_and(at_row, at_lane), squares, 0.0)
        summed.at_once(added)

        every = every_ref[...].reshape(count, rows, lanes)
        row = lax.broadcasted_iota(jnp.int32, (rows, lanes), 0)
        lane = lax.broadcasted_iota(jnp.int32, (rows, lanes), 1)
        enc_rows = jnp.logical_and(row >= at_enc, row < at_enc + e_own)
        added = jnp.logical_and(enc_rows, jnp.logical_or(lane == C + 2, lane == C + 3))
        squares = jnp.sum(jnp.where(added[None], 0.0, every * every), axis=0)
        owned = jnp.logical_and(row == at_enc, lane == C + 3)
        squares = squares + jnp.where(owned, jnp.sum(every, axis=0), 0.0)
        squares = jnp.sum(squares, keepdims=True)
        if given:
            sums = given_ref[...].reshape(count, pack, E)
            squares = squares + jnp.sum(jnp.sum(sums * sums, axis=0), keepdims=True)
        norm = jnp.sqrt(squares)
        clip = CLIP_NORM / jnp.maximum(norm, CLIP_NORM)
        at_lane = lax.broadcasted_iota(jnp.int32, (8, 128), 1)
        loss = every[0, at_enc : at_enc + 1, C + 2 : C + 3]
        scalars_ref[...] = jnp.where(at_lane == 0, norm, jnp.where(at_lane == 1, clip, loss))

        old = moment_ref[...].reshape(count, pack, E)
        if given:

            def new(begin, size, grads, first=0, width=E):
                own = old[:, begin : begin + size, first : first + width].reshape(-1, width)
                return MOMENTUM * own + clip * grads.reshape(-1, width)

            near = lax.broadcasted_iota(jnp.int32, (e_own, 128), 1) < C
            enc_sums = jnp.where(near[None], every, 0.0)
            starts = [new(at, ff_dev, sums[:, at : at + ff_dev]) for at in (0, ff_dev)]
            starts.append(new(2 * ff_dev, e_own, enc_sums, 0, 128))
            starts.append(new(2 * ff_dev, e_own, sums[:, 2 * ff_dev :, :128], 128, 128))
        else:
            moment = MOMENTUM * old + clip[None] * every

            def rows_of(begin, size):
                inside = jnp.logical_and(row >= begin, row < begin + size)
                return jnp.where(inside[None], moment, 0.0).reshape(-1, E)

            both = rows_of(at_enc, e_own)
            near = lax.broadcasted_iota(jnp.int32, (both.shape[0], 128), 1) < C
            starts = [rows_of(0, ff_dev), rows_of(ff_dev, ff_dev)]
            starts += [jnp.where(near, both[:, :128], 0.0), both[:, 128:]]
        if given:
            first = summed.core == 0
            starts = [jnp.where(first, starts[k], starts[k + 1]) for k in (0, 2)]
        for start, out in zip(starts, mats):
            square = jnp.sum(start * start, keepdims=True)
            out[...] = start / (jnp.sqrt(square) + 1e-07)

        @pl.loop(0, NS_ITERS)
        def _(sweep):
            for out in mats[: len(starts)]:
                matrix = out[...]
                gram_mat = product(matrix, matrix, ((0,), (0,)))
                square = product(gram_mat, gram_mat, ((1,), (0,)))
                poly = NS_SECOND * gram_mat + NS_THIRD * square
                out[...] = NS_FIRST * matrix + product(matrix, poly, ((1,), (0,)))

        if not given:
            up, down, enc, dec = (m[...] for m in mats)
            both = jnp.concatenate([enc, dec], axis=1)
            new_refs[0][...] = (up + down + both).reshape((2, planes, places, pack, E))
            return
        tall, flat, give_tall, give_flat, got_tall, got_flat = mats
        core, z = summed.core, summed.z

        def block_at(c, p):
            return (c * planes + z) * places + p

        def rows_at(ref, block, size):
            return ref[pl.ds(pl.multiple_of(block * size, 8), size), :]

        give_tall[...] = rows_at(tall, block_at(1 - core, summed.place), ff_dev)
        enc_at = [(k % 2, summed.x * summed.y_count + k // 2) for k in range(planes)]
        for k, (c, p) in enumerate(enc_at):
            give_flat[pl.ds(k * e_own, e_own), :] = rows_at(flat, block_at(c, p), e_own)
        copies = [
            summed.remote(give_tall, got_tall, 6, summed.at_core()),
            summed.remote(give_flat, got_flat, 7, summed.at_core()),
        ]
        for copy in copies:
            copy.start()
        for copy in copies:
            copy.wait()
        mine = rows_at(tall, block_at(core, summed.place), ff_dev)
        steps = [(mine, got_tall[...]), (give_flat[...], got_flat[...])]
        own_sums = given_ref[core, z, summed.place]
        flat_sums = [
            jnp.concatenate([given_ref[c, z, p, 2 * ff_dev :, :128] for c, p in enc_at], axis=0),
            jnp.concatenate([every_ref[c, z, p] for c, p in enc_at], axis=0),
        ]
        grads = [own_sums[:ff_dev], own_sums[ff_dev : 2 * ff_dev], flat_sums[1], flat_sums[0]]
        for at in range(4):
            here, there = steps[at // 2]
            new_refs[2 * (at // 2)][at % 2] = grads[at]
            step = jnp.where(first, here, there) if at % 2 == 0 else jnp.where(first, there, here)
            new_refs[2 * (at // 2) + 1][at % 2] = step

    if given:
        e_dev = lay.e_dev
        mat_shapes = [(FF, E), (E, 128)] + [(ff_dev, E), (e_dev, 128)] * 2
        results = [jax.ShapeDtypeStruct((2, ff_dev, E), FULL)] * 2
        results += [jax.ShapeDtypeStruct((2, e_dev, 128), FULL)] * 2
    else:
        mat_shapes = [(count * pack, E)] * 2 + [(count * pack, 128)] * 2
        results = [jax.ShapeDtypeStruct(moments.shape, FULL)]
    fast = pl.BlockSpec(memory_space=pltpu.VMEM)
    sums = [jax.ShapeDtypeStruct(blocks.shape, FULL), jax.ShapeDtypeStruct((8, 128), FULL)]
    got = pl.pallas_call(
        kernel,
        out_shape=sums + results,
        in_specs=[fast] * (3 + len(given)),
        out_specs=[fast] * (2 + len(results)),
        scratch_shapes=[
            *Total.scratch(blocks.shape)[:2],
            pltpu.VMEM((planes * places,) + blocks.shape[3:], FULL),
            *Total.scratch(blocks.shape)[3:],
            *[pltpu.VMEM(m, FULL) for m in mat_shapes],
            pltpu.SemaphoreType.DMA((8,)),
            pltpu.SemaphoreType.DMA((8,)),
        ],
        compiler_params=pltpu.CompilerParams(
            collective_id=tag, has_side_effects=True, vmem_limit_bytes=56 << 20
        ),
        name="finish",
    )(blocks, moments, extra, *given)
    return got[0], got[1], list(got[2:])


def update(scalars, grads, own):
    def kernel(scalars_ref, tall_grad, tall_step, flat_grad, flat_step, *refs):
        own_refs, new_refs, last = refs[: len(own)], refs[len(own) : -3], refs[-3:]
        for at, ref in enumerate(last):
            ref[0, 0] = scalars_ref[0, at]
        clip = scalars_ref[0, 1]
        for at in range(4):
            grad, step = ((tall_grad, tall_step), (flat_grad, flat_step))[at // 2]
            factor = RATE_MUON * math.sqrt(max(1.0, FF / E if at < 2 else E / C))
            master, moment = own_refs[2 * at][...], own_refs[2 * at + 1][...]
            columns = master.shape[1]
            new_refs[2 * at][...] = MOMENTUM * moment + clip * grad[at % 2][:, :columns]
            decayed = master * (1.0 - RATE_MUON * DECAY)
            new_refs[2 * at + 1][...] = decayed - factor * step[at % 2][:, :columns]
        gain, gain_m, gain_v = (ref[...] for ref in own_refs[8:])
        gain_grad = jnp.transpose(flat_grad[0])[C : C + 2]
        new = adam_step(gain, gain_m, gain_v, clip * gain_grad, RATE_GAIN)
        for ref, value in zip(new_refs[8:], new):
            ref[...] = value

    fast = pl.BlockSpec(memory_space=pltpu.VMEM)
    slow = pl.BlockSpec(memory_space=pltpu.SMEM)
    got = pl.pallas_call(
        kernel,
        out_shape=[jax.ShapeDtypeStruct(v.shape, FULL) for v in own]
        + [jax.ShapeDtypeStruct((1, 1), FULL)] * 3,
        in_specs=[slow] + [fast] * (4 + len(own)),
        out_specs=[fast] * len(own) + [slow] * 3,
        name="update",
    )(scalars, *grads, *own)
    return list(got[:-3]), [v.reshape(()) for v in got[-3:]]


def natural(values):
    order = tuple(range(values.ndim))
    return with_layout_constraint(values, DeviceLayout(major_to_minor=order))


def adam_step(weight, moment_a, moment_b, gradient, step_rate):
    moment_a = BETA_FIRST * moment_a + (1.0 - BETA_FIRST) * gradient
    moment_b = BETA_SECOND * moment_b + (1.0 - BETA_SECOND) * gradient * gradient
    rate_a = step_rate / (1.0 - BETA_FIRST**STEP)
    corrected_b = moment_b * (1.0 / (1.0 - BETA_SECOND**STEP))
    step = rate_a * moment_a / (jnp.sqrt(corrected_b) + 1e-08)
    return moment_a, moment_b, weight - (step + step_rate * DECAY * weight)


def adam_rows(clip_scale, weight, moment_a, moment_b, gradient):
    def kernel(clip_ref, *refs):
        old, new = refs[:4], refs[4:]
        w, a, b, g = (ref[...] for ref in old)
        values = adam_step(w, a, b, clip_ref[0, 0] * g, RATE_SPECTRAL)
        for ref, value in zip(new, values):
            ref[...] = value
        new[3][...] = values[2].astype(LOW)

    rows = weight.shape[0]
    parts = 4
    block = pl.BlockSpec((rows // parts, 128), lambda at: (at, 0))
    full = jax.ShapeDtypeStruct(weight.shape, FULL)
    return pl.pallas_call(
        kernel,
        grid=(parts,),
        out_shape=[full] * 3 + [jax.ShapeDtypeStruct(weight.shape, LOW)],
        in_specs=[pl.BlockSpec(memory_space=pltpu.SMEM)] + [block] * 4,
        out_specs=[block] * 4,
        name="adam_rows",
    )(clip_scale.reshape(1, 1), weight, moment_a, moment_b, gradient)


def local(
    fields,
    targets,
    valid,
    var_class,
    enc_t,
    enc_mom,
    dec,
    dec_mom,
    spec,
    spec_m,
    spec_v,
    up_t,
    up_mom,
    down,
    down_mom,
    gains,
    gain_m,
    gain_v,
):
    dp_count, ns_count = lax.axis_size("dp"), lax.axis_size("ns")
    devices = dp_count * ns_count
    lay = Layout(dp_count, ns_count, fields.shape[0], fields.shape[1])
    z, x, n = lay.here()
    lat_count = lay.block_rows * dp_count

    ff_dev, e_own = up_t.shape[1], E // devices
    pack = -(-(2 * ff_dev + 2 * e_own) // 16) * 16

    def mine(values):
        return lax.dynamic_slice_in_dim(values, n * e_own, e_own, 0)

    def packed(up, down_, enc, dec_, extra):
        both = jnp.concatenate([wide(mine(enc)), wide(mine(dec_))], axis=1)
        return pad_rows(jnp.concatenate([up[0], down_[0], both, extra], axis=0), pack)

    def unpacked(every):
        up = every[:, :ff_dev].reshape(FF, E)
        down_ = every[:, ff_dev : 2 * ff_dev].reshape(FF, E)
        both = every[:, 2 * ff_dev : 2 * ff_dev + e_own].reshape(E, E)
        extra = every[:, 2 * ff_dev + e_own : 2 * ff_dev + 2 * e_own]
        return up, down_, both[:, :128], both[:, 128:], extra

    gain_rows = jnp.pad(mine(gains[0]), ((0, 0), (0, E - 2)))
    small = packed(up_t, down, enc_t, dec, gain_rows).astype(LOW)
    lon_count = fields.shape[2]

    def dense(values):
        fill = (-values.shape[-1] % 16, -lon_count % 128)
        values = values.transpose(0, 1, 3, 2)
        return jnp.pad(values, ((0, 0), (0, 0), (0, fill[0]), (0, fill[1])))

    def usual(values, count=C):
        values = values[:, :, :count, :lon_count].reshape((1, lay.rows, count, lon_count))
        return values.transpose(0, 1, 3, 2)

    swaps = [dense(fields), jnp.pad(valid, ((0, 0), (0, 0), (0, -lon_count % 128)))]
    spec_got, every_low, swaps = prologue(lay, spec_out(lay, spec[0]), small, swaps, 0)
    fields = usual(swaps[0])
    valid = swaps[1][..., :lon_count].reshape(1, lay.rows, lon_count)
    targets = [dense(targets[step]) for step in range(2)]
    up_w, down_w, enc_w, dec_w, extra = unpacked(every_low)
    enc_w, dec_w = enc_w[:, :C], dec_w[:, :C]
    gain_w = extra.reshape(E, E)[:, :2]
    spec_w = spec_in(lay, spec_got)

    rows_at = [lay.block_rows * at + np.arange(lay.block_rows) for at in lay.row_blocks(0, 0)]
    rows_at = np.concatenate(rows_at) + lay.block_rows * lay.row_blocks(n, x)[0]
    local_sine = jnp.sin(math.pi / lat_count * (rows_at.astype(FULL) + 0.5))
    var_weight = 1.0 + 0.5 * var_class.astype(FULL)
    pixel_map = valid.astype(FULL) * local_sine[None, :, None]
    weight_part = jnp.sum(pixel_map)
    weight_map = pixel_map[..., None] * var_weight
    weight_rows = jnp.broadcast_to(weight_part, (e_own, E))
    every_mom = lax.all_gather(packed(up_mom, down_mom, enc_mom, dec_mom, weight_rows), BOTH)
    loss_weight = jnp.sum(every_mom[:, 2 * ff_dev + e_own, 0]) * jnp.sum(var_weight)
    core_pack = -(-(2 * ff_dev + e_own) // 8) * 8

    def by_core(values):
        values = values.reshape((ns_count, dp_count // 2, 2) + values.shape[1:])
        return jnp.moveaxis(values, 2, 0)

    def by_device(values):
        return jnp.moveaxis(values, 0, 2).reshape((devices,) + values.shape[3:])

    moments = by_core(pad_rows(every_mom[:, : 2 * ff_dev + e_own], core_pack))

    tables = dft_tables(lay, fields.shape[2]) + legendre_tables(lay, lat_count)
    incoming = fields
    saved = []
    forecasts = []
    for step in range(2):
        weights = (spec_w, up_w, down_w, gain_w)
        hidden = jnp.einsum("brkc,ec->brke", incoming, enc_w, preferred_element_type=FULL)
        fetch, carry = ((True,), ()) if step == 0 else ((), (targets[1],))
        hidden, kept, given = forward_block(lay, hidden, weights, tables, 1 + step, fetch, carry)
        if step == 0:
            (spec_w,) = given.whole
        else:
            targets[1] = usual(given.carried[0])
        closing = hidden.astype(LOW)
        forecast = jnp.einsum("brke,ec->brkc", closing, dec_w, preferred_element_type=FULL)
        saved.append((incoming, kept, closing))
        forecasts.append(forecast)
        incoming = forecast.astype(LOW)

    def loss_of(step):
        error = forecasts[step] - targets[step].astype(FULL)
        return jnp.sum(weight_map * error * error), 2.0 * weight_map * error / loss_weight

    last_loss, gradient = loss_of(1)
    early, d_spec = (), ()
    aside = ff_dev % 8 == 0 and e_own % 8 == 0
    carry = (targets[0],)
    for step in (1, 0):
        incoming, kept, closing = saved[step]
        low_grad = gradient.astype(LOW)
        gradient = jnp.einsum("brkc,ec->brke", low_grad, dec_w, preferred_element_type=FULL)
        gradient, given, early, d_gain = backward_block(
            lay,
            gradient,
            kept,
            weights,
            tables,
            4 - step,
            d_spec,
            carry,
            early,
            closing,
            low_grad,
            aside,
        )
        d_spec, carry = given.d + given.g, ()
        squares = given.squares[0] if given.squares else None
        low_grad = gradient.astype(LOW)
        d_enc = jnp.einsum("brkc,brke->ec", incoming, low_grad, preferred_element_type=FULL)
        if step == 1:
            late = (d_gain, d_enc)
            targets[0] = usual(given.carried[0])
            first_loss, gradient = loss_of(0)
            gradient = gradient + jnp.einsum(
                "brke,ec->brkc", low_grad, enc_w, preferred_element_type=FULL
            )
            loss_local = first_loss + last_loss
    d_gain, d_enc = late[0] + d_gain, late[1] + d_enc
    g_spec = natural(spec_home(lay, d_spec[0], 5).astype(FULL)[None])
    near = jnp.concatenate([d_enc, d_gain, jnp.broadcast_to(loss_local, (E, 1))], axis=1)
    near = wide(near).reshape(devices, e_own, 128)
    if aside:
        blocks, given, at_enc = by_core(near), early, 0
    else:
        d_up, d_down, d_dec = early
        both = jnp.concatenate([near, wide(d_dec).reshape(near.shape)], axis=-1)
        blocks = [d_up.reshape(devices, ff_dev, E), d_down.reshape(devices, ff_dev, E), both]
        blocks = by_core(pad_rows(jnp.concatenate(blocks, axis=1), core_pack))
        given, at_enc = [], 2 * ff_dev
    masters = [up_t[0], up_mom[0], down[0], down_mom[0], enc_t, enc_mom, dec, dec_mom]
    every, scalars, new = finish(lay, blocks, given, moments, squares, ff_dev, e_own, 6)
    if aside:
        own = masters + [v[0].T for v in (gains, gain_m, gain_v)]
        new, (grad_norm, clip_scale, loss_sum) = update(scalars, new, own)
        new[8:] = [v.T for v in new[8:]]
    else:
        grad_norm, clip_scale, loss_sum = scalars[0, 0], scalars[0, 1], scalars[0, 2]
        (matrices,) = new
        d = lax.axis_index("dp")
        place = x * (ns_count // 2) + n // 2

        def enc_block(values):
            both = by_device(values[:, :, :, at_enc : at_enc + e_own])
            both = both.reshape(dp_count, lay.e_dev, E)
            return lax.dynamic_index_in_dim(both, d, keepdims=False)

        def muon(master, moment, gradient, matrix, factor):
            moment = MOMENTUM * moment + clip_scale * gradient
            return moment, master * (1.0 - RATE_MUON * DECAY) - RATE_MUON * (matrix * factor)

        grad, step = every[n % 2, z, place], matrices[n % 2, z, place]
        both_grad, both_step = enc_block(every), enc_block(matrices)
        new = []
        for at in range(4):
            begin = (0, ff_dev, 0, 128)[at]
            rows, columns = (FF, E) if at < 2 else (E, C)
            if at < 2:
                g, m = grad[begin : begin + ff_dev], step[begin : begin + ff_dev]
            else:
                g, m = both_grad[:, begin : begin + C], both_step[:, begin : begin + C]
            factor = math.sqrt(max(1.0, rows / columns))
            new += muon(masters[2 * at], masters[2 * at + 1], g, m, factor)
        g_gain = clip_scale * both_grad[:, C : C + 2]
        new += adam_step(gains[0], gain_m[0], gain_v[0], g_gain, RATE_GAIN)
    up_mom_new, up_new, down_mom_new, down_new = (v[None] for v in new[:4])
    enc_mom_new, enc_new, dec_mom_new, dec_new = new[4:8]
    gain_m_new, gain_v_new, gain_new = (v[None] for v in new[8:])
    def dense_rows(values):
        values = values.reshape(values.shape[1:4] + (2, 128)).transpose(0, 1, 3, 2, 4)
        return values.reshape(-1, 128)

    def as_before(values):
        values = values.reshape(spec.shape[1:3] + (2, 2, 128)).transpose(0, 1, 3, 2, 4)
        return values.reshape(spec.shape)

    spec_news = [
        as_before(v)
        for v in adam_rows(clip_scale, *(dense_rows(v) for v in (spec, spec_m, spec_v, g_spec)))
    ]
    spec_m_new, spec_v_new, spec_new, spec_copy = spec_news
    return (
        loss_sum,
        loss_weight,
        grad_norm,
        enc_mom_new,
        enc_new,
        dec_mom_new,
        dec_new,
        up_mom_new,
        up_new,
        down_mom_new,
        down_new,
        spec_m_new,
        spec_v_new,
        spec_new,
        spec_copy,
        gain_m_new,
        gain_v_new,
        gain_new,
    )


def solution(mesh):
    rows = P(None, BOTH, None)
    shard = P("dp", None)
    whole = P(None, "dp", "ns", None, None)
    gain = P(None, "dp", None)
    placed = (
        P("ns", "dp", None, None),
        P(None, "ns", "dp", None, None),
        P("ns", "dp", None),
        P(),
        *[shard] * 4,
        *[whole] * 3,
        *[rows] * 4,
        *[gain] * 3,
    )
    return jax.shard_map(
        local,
        mesh=mesh,
        in_specs=placed,
        out_specs=(P(), P(), P(), *[shard] * 4, *[rows] * 4, *[whole] * 4, *[gain] * 3),
        check_vma=False,
    )
```
